32 devices in a mesh: head: 4 (over y, x), ctx: 8 (over z, core).
Axes of the slice: x: 2, y: 2, z: 4, core: 2. Of those that a mesh axis runs over, the one named last changes fastest.
Arguments:
- queries: bfloat16 [16, 128, 2048], P('ctx', 'head'), may hold values from -8 to 8
- key_vectors: bfloat16 [16, 128, 256], P('ctx', 'head'), may hold values from -8 to 8
- value_vectors: bfloat16 [16, 128, 256], P('ctx', 'head'), may hold values from -4 to 4
- out_grad: bfloat16 [16, 128, 2048], P('ctx', 'head'), may hold values from -4 to 4
- block_order: int32 [16], replicated, may hold values from 0 to 15, each once
Outputs:
- attended: bfloat16 [16, 128, 2048], P('ctx', 'head')
- query_grad: bfloat16 [16, 128, 2048], P('ctx', 'head')
- key_grad: bfloat16 [16, 128, 256], P('ctx', 'head')
- value_grad: bfloat16 [16, 128, 256], P('ctx', 'head')
The draws below stay inside these ranges and needn't reach their ends.
All inputs are finite; a program needn't handle non-finite values.
Results may differ from the reference program's by a relative error of at most 0.025.
Values may be sent and summed in bfloat16 or wider, within the bound.
No kernel may reach another device: no remote copies, remote signals or barrier semaphores. Data moves between devices by JAX's collectives and lax.ppermute only.
A program may use at most 64 MiB of HBM per device.

```python
import math
import jax
import jax.numpy as jnp
from jax import lax

HD = 128
QH = 16
KVH = 2
BLOCK = 128
GROUP = 8
NBLOCK = 16


def draw_queries(key, part):
    normal_rows = jax.random.normal(jax.random.fold_in(key, 1), (NBLOCK, BLOCK, QH, HD), jnp.float32)
    entries = jnp.clip(normal_rows, -4.0, 4.0)
    return entries.reshape(NBLOCK, BLOCK, QH * HD).astype(jnp.bfloat16)


def draw_key_vectors(key, part):
    normal_rows = jax.random.normal(jax.random.fold_in(key, 3), (NBLOCK, BLOCK, KVH, HD), jnp.float32)
    entries = jnp.clip(normal_rows, -4.0, 4.0)
    return entries.reshape(NBLOCK, BLOCK, KVH * HD).astype(jnp.bfloat16)


def block_levels(key, shape, shards, low, top_value):
    gain, own = 1.0, jax.random.fold_in(key, 6)
    for position, blocks in shards:
        heights = jnp.exp(jax.random.uniform(jax.random.fold_in(own, position), (blocks,), jnp.float32, low / len(shards), top_value / len(shards)))
        gain = gain * jnp.repeat(heights, shape[position] // blocks).reshape([-1 if axis == position else 1 for axis in range(len(shape))])
    return gain


def noise(own_key, extent, deviation, limit, cuts=(), held_as=jnp.bfloat16):
    values = deviation * jax.random.normal(own_key, extent, jnp.float32)
    if cuts:
        values = values * block_levels(own_key, extent, cuts, -0.22, 0.18)
    return jnp.clip(values, -limit, limit).astype(held_as)


def setup_inputs(seed: int = 0) -> dict:
    splits = jax.random.split(jax.random.key(seed), 6)
    queries = draw_queries(jax.random.fold_in(splits[5], 71), 0)
    key_vectors = draw_key_vectors(jax.random.fold_in(splits[5], 71), 0)
    value_vectors = noise(splits[2], (NBLOCK, BLOCK, KVH * HD), 1.0, 4.0, ((0, 8), (1, 4)))
    out_grad = noise(splits[3], (NBLOCK, BLOCK, QH * HD), 1.0, 4.0, ((0, 8), (1, 4)))
    block_order = jax.random.permutation(splits[4], NBLOCK).astype(jnp.int32)
    return dict(queries=queries, key_vectors=key_vectors, value_vectors=value_vectors, out_grad=out_grad, block_order=block_order)


def head_pass(head_inputs, positions, scaling):
    query_rows, key_rows, value_rows, grad_rows = head_inputs
    tokens = query_rows.shape[0]
    tile_rows = 2 * BLOCK
    tile_count = tokens // tile_rows
    query_tiles = query_rows.reshape(tile_count, tile_rows, HD)
    grad_tiles = grad_rows.reshape(tile_count, tile_rows, HD)
    pos_tiles = positions.reshape(tile_count, tile_rows)

    def tile_step(totals, tile_inputs):
        key_total, value_total = totals
        query_tile, grad_tile, pos_tile = tile_inputs
        scores = jnp.dot(query_tile, key_rows.T, preferred_element_type=jnp.float32) * scaling
        allowed = positions[None, :] <= pos_tile[:, None]
        row_max = lax.optimization_barrier(jnp.max(jnp.where(allowed, scores, -jnp.inf), axis=1))
        row_sum = lax.optimization_barrier(jnp.sum(jnp.where(allowed, jnp.exp(scores - row_max[:, None]), 0.0), axis=1))
        log_total = row_max + jnp.log(row_sum)
        probs = jnp.where(allowed, jnp.exp(scores - log_total[:, None]), 0.0)
        weights = probs.astype(jnp.bfloat16)
        attended = jnp.dot(weights, value_rows, preferred_element_type=jnp.float32).astype(jnp.bfloat16)
        attended_wide = lax.optimization_barrier(attended).astype(jnp.float32)
        row_delta = lax.optimization_barrier(jnp.sum(grad_tile.astype(jnp.float32) * attended_wide, axis=1))
        grad_weights = jnp.dot(grad_tile, value_rows.T, preferred_element_type=jnp.float32)
        grad_scores = (probs * (grad_weights - row_delta[:, None])).astype(jnp.bfloat16)
        query_grad = (jnp.dot(grad_scores, key_rows, preferred_element_type=jnp.float32) * scaling).astype(jnp.bfloat16)
        key_total = key_total + jnp.dot(grad_scores.T, query_tile, preferred_element_type=jnp.float32)
        value_total = value_total + jnp.dot(weights.T, grad_tile, preferred_element_type=jnp.float32)
        return ((key_total, value_total), (attended, query_grad))
    empty_rows = jnp.zeros((tokens, HD), jnp.float32)
    totals, results = lax.scan(tile_step, (empty_rows, empty_rows), (query_tiles, grad_tiles, pos_tiles))
    attended = results[0].reshape(tokens, HD)
    query_grad = results[1].reshape(tokens, HD)
    return (attended, query_grad, totals[0], totals[1])

def reference(queries, key_vectors, value_vectors, out_grad, block_order):
    tokens = NBLOCK * BLOCK
    scaling = 1.0 / math.sqrt(HD)
    offsets = jnp.arange(BLOCK, dtype=jnp.int32)
    positions = (block_order.astype(jnp.int32)[:, None] * BLOCK + offsets[None, :]).reshape(tokens).astype(jnp.int32)
    query_heads = jnp.transpose(queries.reshape(tokens, QH, HD), (1, 0, 2))
    grad_heads = jnp.transpose(out_grad.reshape(tokens, QH, HD), (1, 0, 2))
    key_heads = jnp.repeat(jnp.transpose(key_vectors.reshape(tokens, KVH, HD), (1, 0, 2)), GROUP, axis=0)
    value_heads = jnp.repeat(jnp.transpose(value_vectors.reshape(tokens, KVH, HD), (1, 0, 2)), GROUP, axis=0)
    attended, query_grad, key_total, value_total = lax.map(lambda inputs: head_pass(inputs, positions, scaling), (query_heads, key_heads, value_heads, grad_heads))
    attended = jnp.transpose(attended, (1, 0, 2)).reshape(NBLOCK, BLOCK, QH * HD)
    query_grad = jnp.transpose(query_grad, (1, 0, 2)).reshape(NBLOCK, BLOCK, QH * HD)
    key_grad = (lax.optimization_barrier(jnp.sum(key_total.reshape(KVH, GROUP, tokens, HD), axis=1)) * scaling).astype(jnp.bfloat16)
    value_grad = lax.optimization_barrier(jnp.sum(value_total.reshape(KVH, GROUP, tokens, HD), axis=1)).astype(jnp.bfloat16)
    key_grad = jnp.transpose(key_grad, (1, 0, 2)).reshape(NBLOCK, BLOCK, KVH * HD)
    value_grad = jnp.transpose(value_grad, (1, 0, 2)).reshape(NBLOCK, BLOCK, KVH * HD)
    return (attended, query_grad, key_grad, value_grad)
```

```python
import functools
import math

import jax
import jax.numpy as jnp
from jax import lax
from jax.experimental import pallas as pl
from jax.experimental.pallas import tpu as pltpu
from jax.sharding import PartitionSpec as P

HD = 128
BF = jnp.bfloat16
F32 = jnp.float32
LOWEST = -1e30
LANES = 256


def params(*arrays_bytes):
    limit = int(sum(arrays_bytes)) + (12 << 20)
    return pltpu.CompilerParams(vmem_limit_bytes=min(limit, 60 << 20))


def nbytes(*shapes):
    return sum(math.prod(s.shape) * s.dtype.itemsize for s in shapes)


VMEM = pl.BlockSpec(memory_space=pltpu.VMEM)
SMEM = pl.BlockSpec(memory_space=pltpu.SMEM)


def swap(block, axis, mask):
    size = lax.axis_size(axis)
    return lax.ppermute(block, axis, [(i, i ^ mask) for i in range(size)])


def pack_kv_kernel(kv, key_ref, value_ref, out_ref):
    for dest in range(out_ref.shape[0]):
        cols = pl.ds((dest % kv) * HD, HD)
        out_ref[dest, :, :HD] = key_ref[:, cols]
        out_ref[dest, :, HD:] = value_ref[:, cols]


def pack_q_kernel(kv, core_ref, query_ref, grad_ref, keep_ref, send_ref):
    width = keep_ref.shape[2]
    for core in range(kv):

        @pl.when(core_ref[0] == core)
        def _():
            mine = pl.ds(core * width, width)
            keep_ref[0] = query_ref[:, mine]
            keep_ref[1] = grad_ref[:, mine]
            for step in range(1, kv):
                theirs = pl.ds((core ^ step) * width, width)
                send_ref[step - 1, 0] = query_ref[:, theirs]
                send_ref[step - 1, 1] = grad_ref[:, theirs]


def attend_kernel(
    kv,
    block_len,
    block_rows,
    tile_rows,
    heads,
    chunks,
    order_ref,
    place_ref,
    *refs,
):
    keep_ref, recv_ref = refs[0], refs[1]
    kv_refs = refs[2 : 2 + chunks]
    out_keep, out_send = refs[2 + chunks], refs[3 + chunks]
    dkv_refs = refs[4 + chunks : 4 + 2 * chunks]
    q_all, do_all, e_ref, p_ref, ds_ref = refs[4 + 2 * chunks :]
    rows = keep_ref.shape[1]
    ctx_size = kv_refs[0].shape[0]
    chunk_keys = ctx_size * rows
    blocks_here = rows // block_rows
    lanes = heads * tile_rows
    scaling = 1.0 / math.sqrt(HD)
    expo = scaling * math.log2(math.e)
    head_place = place_ref[0]
    pair_start = place_ref[1]
    core = place_ref[2]

    def part_q(step):
        return keep_ref if step == 0 else recv_ref.at[step - 1]

    def part_out(step):
        return out_keep if step == 0 else out_send.at[step - 1]

    lane_row = lax.broadcasted_iota(jnp.int32, (1, lanes), 1) % tile_rows
    key_iota = lax.broadcasted_iota(jnp.int32, (block_rows, lanes), 0)
    tiles = [(step, start) for step in range(kv) for start in range(0, rows, tile_rows)]
    for tile, (step, start) in enumerate(tiles):
        source = part_q(step)
        span = pl.ds(start, tile_rows)
        out_span = pl.ds(tile * lanes, lanes)
        for n in range(heads):
            at = pl.ds(tile * lanes + n * tile_rows, tile_rows)
            q_all[at, :] = source[0, span, pl.ds(n * HD, HD)]
            do_all[at, :] = source[1, span, pl.ds(n * HD, HD)]
        q = q_all[out_span, :]
        do = do_all[out_span, :]
        source_ctx = pair_start + (core ^ step)
        query_pos = jnp.zeros((1, lanes), jnp.int32)
        for b in range(start // block_rows, -(-(start + tile_rows) // block_rows)):
            block_pos = order_ref[source_ctx * blocks_here + b] * block_len + head_place * block_rows
            here = (lane_row + start) // block_rows == b
            query_pos = jnp.where(here, block_pos + (lane_row + start) % block_rows, query_pos)
        gap = query_pos - key_iota
        row_max = jnp.full((8, lanes), LOWEST, F32)
        for m in range(chunks):
            keys = kv_refs[m][:, :, :HD].reshape(chunk_keys, HD)
            scores = lax.dot_general(keys, q, (((1,), (1,)), ((), ())), preferred_element_type=F32)
            chunk_head = head_place ^ m
            for j in range(chunk_keys // block_rows):
                key_pos = order_ref[j] * block_len + chunk_head * block_rows
                part = scores[j * block_rows : (j + 1) * block_rows]
                part = jnp.where(gap >= key_pos, part, LOWEST)
                e_ref[pl.ds(m * chunk_keys + j * block_rows, block_rows), :] = part
                row_max = jnp.maximum(row_max, jnp.max(part.reshape(block_rows // 8, 8, lanes), axis=0))
        top = jnp.max(row_max, axis=0, keepdims=True) * expo
        row_sum = jnp.zeros((8, lanes), F32)
        for m in range(chunks):
            span_keys = pl.ds(m * chunk_keys, chunk_keys)
            part = jnp.exp2(e_ref[span_keys, :] * expo - top)
            e_ref[span_keys, :] = part
            row_sum = row_sum + jnp.sum(part.reshape(chunk_keys // 8, 8, lanes), axis=0)
        inverse = 1.0 / jnp.sum(row_sum, axis=0, keepdims=True)
        mixed = jnp.zeros((HD, lanes), F32)
        for m in range(chunks):
            span_keys = pl.ds(m * chunk_keys, chunk_keys)
            probs = (e_ref[span_keys, :] * inverse).astype(BF)
            p_ref[span_keys, out_span] = probs
            values = kv_refs[m][:, :, HD:].reshape(chunk_keys, HD)
            mixed = mixed + lax.dot_general(
                values, probs, (((0,), (0,)), ((), ())), preferred_element_type=F32
            )
        attended = mixed.T.astype(BF)
        for n in range(heads):
            part_out(step)[0, span, pl.ds(n * HD, HD)] = attended[n * tile_rows : (n + 1) * tile_rows]
        delta = jnp.sum(
            do.astype(F32).T * mixed.astype(BF).astype(F32), axis=0, keepdims=True
        )
        q_grad = jnp.zeros((HD, lanes), F32)
        for m in range(chunks):
            span_keys = pl.ds(m * chunk_keys, chunk_keys)
            values = kv_refs[m][:, :, HD:].reshape(chunk_keys, HD)
            keys = kv_refs[m][:, :, :HD].reshape(chunk_keys, HD)
            grad_w = lax.dot_general(values, do, (((1,), (1,)), ((), ())), preferred_element_type=F32)
            grad_s = ((e_ref[span_keys, :] * inverse) * (grad_w - delta)).astype(BF)
            ds_ref[span_keys, out_span] = grad_s
            q_grad = q_grad + lax.dot_general(
                keys, grad_s, (((0,), (0,)), ((), ())), preferred_element_type=F32
            )
        q_grad = (q_grad.T * scaling).astype(BF)
        for n in range(heads):
            part_out(step)[1, span, pl.ds(n * HD, HD)] = q_grad[n * tile_rows : (n + 1) * tile_rows]
    for m in range(chunks):
        span_keys = pl.ds(m * chunk_keys, chunk_keys)
        k_grad = jnp.dot(ds_ref[span_keys, :], q_all[...], preferred_element_type=F32)
        v_grad = jnp.dot(p_ref[span_keys, :], do_all[...], preferred_element_type=F32)
        dkv_refs[m][:, :, :HD] = k_grad.astype(BF).reshape(ctx_size, rows, HD)
        dkv_refs[m][:, :, HD:] = v_grad.astype(BF).reshape(ctx_size, rows, HD)


def sum_kernel(*refs):
    total = refs[0][...].astype(F32)
    for ref in refs[1:-1]:
        total = total + ref[...].astype(F32)
    refs[-1][...] = total.astype(BF)


def finish_kv_kernel(kv, scaling, parts_ref, key_ref, value_ref):
    for g in range(kv):
        total = parts_ref[g].astype(F32)
        for source in range(g + kv, parts_ref.shape[0], kv):
            total = total + parts_ref[source].astype(F32)
        cols = pl.ds(g * HD, HD)
        key_ref[:, cols] = (total[:, :HD] * scaling).astype(BF)
        value_ref[:, cols] = total[:, HD:].astype(BF)


def finish_q_kernel(kv, core_ref, keep_ref, recv_ref, att_ref, grad_ref):
    width = keep_ref.shape[2]
    for core in range(kv):

        @pl.when(core_ref[0] == core)
        def _():
            mine = pl.ds(core * width, width)
            att_ref[:, mine] = keep_ref[0]
            grad_ref[:, mine] = keep_ref[1]
            for step in range(1, kv):
                theirs = pl.ds((core ^ step) * width, width)
                att_ref[:, theirs] = recv_ref[step - 1, 0]
                grad_ref[:, theirs] = recv_ref[step - 1, 1]


def call(kernel, ins, specs, outs, scratch=(), scratch_bytes=0, cost=None, name=None):
    out_specs = [VMEM] * len(outs)
    single = len(outs) == 1
    return pl.pallas_call(
        kernel,
        out_shape=outs[0] if single else tuple(outs),
        in_specs=specs,
        out_specs=out_specs[0] if single else tuple(out_specs),
        scratch_shapes=list(scratch),
        compiler_params=params(nbytes(*ins), nbytes(*outs), scratch_bytes),
        cost_estimate=cost,
        name=name,
    )(*ins)


def shards(queries, key_vectors, value_vectors, out_grad, block_order):
    heads_devices = lax.axis_size("head")
    ctx_devices = lax.axis_size("ctx")
    halves, block_rows, query_width = queries.shape
    kv = key_vectors.shape[2] // HD
    rows = halves * block_rows
    width = query_width // kv
    group = width // HD
    block_len = block_rows * heads_devices
    ctx = lax.axis_index("ctx").astype(jnp.int32)
    core = (ctx % kv).reshape(1)
    place = jnp.stack([lax.axis_index("head").astype(jnp.int32), ctx - ctx % kv, ctx % kv])
    queries = queries.reshape(rows, query_width)
    out_grad = out_grad.reshape(rows, query_width)
    key_vectors = key_vectors.reshape(rows, kv * HD)
    value_vectors = value_vectors.reshape(rows, kv * HD)

    def shape(*dims):
        return jax.ShapeDtypeStruct(dims, BF)

    kv_send = call(
        functools.partial(pack_kv_kernel, kv),
        (key_vectors, value_vectors),
        [VMEM] * 2,
        [shape(ctx_devices, rows, 2 * HD)],
        name="pack_kv",
    )
    kv_own = lax.all_to_all(kv_send, "ctx", split_axis=0, concat_axis=0, tiled=True)
    keep, send = call(
        functools.partial(pack_q_kernel, kv),
        (core, queries, out_grad),
        [SMEM, VMEM, VMEM],
        [shape(2, rows, width), shape(kv - 1, 2, rows, width)],
        name="pack_q",
    )
    recv = jnp.stack([swap(send[step - 1], "ctx", step) for step in range(1, kv)])
    kv_parts = [kv_own] + [swap(kv_own, "head", m) for m in range(1, heads_devices)]

    tile_rows = block_rows if block_rows % 16 == 0 else rows
    lanes = group * tile_rows
    keys = heads_devices * ctx_devices * rows
    query_rows = kv * group * rows
    scratch = [
        pltpu.VMEM((query_rows, HD), BF),
        pltpu.VMEM((query_rows, HD), BF),
        pltpu.VMEM((keys, lanes), F32),
        pltpu.VMEM((keys, query_rows), BF),
        pltpu.VMEM((keys, query_rows), BF),
    ]
    outs = call(
        functools.partial(
            attend_kernel, kv, block_len, block_rows, tile_rows, group, heads_devices
        ),
        (block_order, place, keep, recv, *kv_parts),
        [SMEM, SMEM] + [VMEM] * (2 + heads_devices),
        [shape(2, rows, width), shape(kv - 1, 2, rows, width)]
        + [shape(ctx_devices, rows, 2 * HD)] * heads_devices,
        scratch,
        4 * query_rows * HD + keys * (4 * lanes + 4 * query_rows),
        name="attend",
    )
    out_keep, out_send = outs[0], outs[1]
    dkv = outs[2:]
    dkv_parts = [dkv[0]] + [swap(dkv[m], "head", m) for m in range(1, heads_devices)]
    out_recv = jnp.stack([swap(out_send[step - 1], "ctx", step) for step in range(1, kv)])
    dkv_sum = call(
        sum_kernel,
        tuple(dkv_parts),
        [VMEM] * heads_devices,
        [shape(ctx_devices, rows, 2 * HD)],
        name="sum_heads",
    )
    dkv_back = lax.all_to_all(dkv_sum, "ctx", split_axis=0, concat_axis=0, tiled=True)
    attended, query_grad = call(
        functools.partial(finish_q_kernel, kv),
        (core, out_keep, out_recv),
        [SMEM, VMEM, VMEM],
        [shape(rows, query_width)] * 2,
        name="finish_q",
    )
    key_grad, value_grad = call(
        functools.partial(finish_kv_kernel, kv, 1.0 / math.sqrt(HD)),
        (dkv_back,),
        [VMEM],
        [shape(rows, kv * HD)] * 2,
        name="finish_kv",
    )
    return (
        attended.reshape(halves, block_rows, query_width),
        query_grad.reshape(halves, block_rows, query_width),
        key_grad.reshape(halves, block_rows, kv * HD),
        value_grad.reshape(halves, block_rows, kv * HD),
    )


def solution(mesh):
    split = P("ctx", "head", None)
    return jax.shard_map(
        shards,
        mesh=mesh,
        in_specs=(split, split, split, split, P()),
        out_specs=(split, split, split, split),
        check_vma=False,
    )
```

```python
import functools
import math

import jax
import jax.numpy as jnp
from jax import lax
from jax.experimental import pallas as pl
from jax.experimental.pallas import tpu as pltpu
from jax.sharding import PartitionSpec as P

HD = 128
BF = jnp.bfloat16
F32 = jnp.float32
LOWEST = -1e30
LANES = 256


def params(*arrays_bytes):
    limit = int(sum(arrays_bytes)) + (12 << 20)
    return pltpu.CompilerParams(vmem_limit_bytes=min(limit, 60 << 20))


def nbytes(*shapes):
    return sum(math.prod(s.shape) * s.dtype.itemsize for s in shapes)


VMEM = pl.BlockSpec(memory_space=pltpu.VMEM)
SMEM = pl.BlockSpec(memory_space=pltpu.SMEM)


def swap(block, axis, mask):
    size = lax.axis_size(axis)
    return lax.ppermute(block, axis, [(i, i ^ mask) for i in range(size)])


def pack_kv_kernel(kv, core_ref, *refs):
    out_ref = refs[-1]
    for core in range(kv):

        @pl.when(core_ref[0] == core)
        def _():
            cols = pl.ds(core * HD, HD)
            for step in range(kv):
                out_ref[step, :, :HD] = refs[2 * step][:, cols]
                out_ref[step, :, HD:] = refs[2 * step + 1][:, cols]


def attend_kernel(
    kv,
    block_len,
    block_rows,
    tile_rows,
    heads,
    chunks,
    order_ref,
    place_ref,
    *refs,
):
    q_refs, do_refs = refs[:kv], refs[kv : 2 * kv]
    refs = refs[2 * kv :]
    kv_refs, refs = refs[:chunks], refs[chunks:]
    out_refs, refs = refs[:kv], refs[kv:]
    dkv_refs, refs = refs[:chunks], refs[chunks:]
    q_all, do_all, e_ref, p_ref, ds_ref = refs
    rows = q_refs[0].shape[0]
    z_size = kv_refs[0].shape[0]
    chunk_keys = z_size * kv * rows
    blocks_here = rows // block_rows
    lanes = heads * tile_rows
    scaling = 1.0 / math.sqrt(HD)
    expo = scaling * math.log2(math.e)
    head_place = place_ref[0]
    z_place = place_ref[1]
    core = place_ref[2]
    first_col = core * (heads * HD)
    lane_row = lax.broadcasted_iota(jnp.int32, (1, lanes), 1) % tile_rows
    key_iota = lax.broadcasted_iota(jnp.int32, (block_rows, lanes), 0)
    tiles = [(step, start) for step in range(kv) for start in range(0, rows, tile_rows)]
    for tile, (step, start) in enumerate(tiles):
        span = pl.ds(start, tile_rows)
        out_span = pl.ds(tile * lanes, lanes)
        for n in range(heads):
            at = pl.ds(tile * lanes + n * tile_rows, tile_rows)
            cols = pl.ds(pl.multiple_of(first_col + n * HD, HD), HD)
            q_all[at, :] = q_refs[step][span, cols]
            do_all[at, :] = do_refs[step][span, cols]
        q = q_all[out_span, :]
        do = do_all[out_span, :]
        source_ctx = z_place * kv + (core ^ step)
        query_pos = jnp.zeros((1, lanes), jnp.int32)
        for b in range(start // block_rows, -(-(start + tile_rows) // block_rows)):
            block_pos = order_ref[source_ctx * blocks_here + b] * block_len + head_place * block_rows
            here = (lane_row + start) // block_rows == b
            query_pos = jnp.where(here, block_pos + (lane_row + start) % block_rows, query_pos)
        gap = query_pos - key_iota
        row_max = jnp.full((8, lanes), LOWEST, F32)
        for m in range(chunks):
            keys = kv_refs[m][:, :, :, :HD].reshape(chunk_keys, HD)
            scores = lax.dot_general(keys, q, (((1,), (1,)), ((), ())), preferred_element_type=F32)
            chunk_head = head_place ^ m
            for j in range(chunk_keys // block_rows):
                m_z, s_b = divmod(j, kv * blocks_here)
                s, b = divmod(s_b, blocks_here)
                stored = ((z_place ^ m_z) * kv + (core ^ s)) * blocks_here + b
                key_pos = order_ref[stored] * block_len + chunk_head * block_rows
                part = scores[j * block_rows : (j + 1) * block_rows]
                part = jnp.where(gap >= key_pos, part, LOWEST)
                e_ref[pl.ds(m * chunk_keys + j * block_rows, block_rows), :] = part
                row_max = jnp.maximum(row_max, jnp.max(part.reshape(block_rows // 8, 8, lanes), axis=0))
        top = jnp.max(row_max, axis=0, keepdims=True) * expo
        row_sum = jnp.zeros((8, lanes), F32)
        for m in range(chunks):
            span_keys = pl.ds(m * chunk_keys, chunk_keys)
            part = jnp.exp2(e_ref[span_keys, :] * expo - top)
            e_ref[span_keys, :] = part
            row_sum = row_sum + jnp.sum(part.reshape(chunk_keys // 8, 8, lanes), axis=0)
        inverse = 1.0 / jnp.sum(row_sum, axis=0, keepdims=True)
        mixed = jnp.zeros((HD, lanes), F32)
        for m in range(chunks):
            span_keys = pl.ds(m * chunk_keys, chunk_keys)
            probs = (e_ref[span_keys, :] * inverse).astype(BF)
            p_ref[span_keys, out_span] = probs
            values = kv_refs[m][:, :, :, HD:].reshape(chunk_keys, HD)
            mixed = mixed + lax.dot_general(
                values, probs, (((0,), (0,)), ((), ())), preferred_element_type=F32
            )
        attended = mixed.T.astype(BF)
        for n in range(heads):
            out_refs[step][0, span, pl.ds(n * HD, HD)] = attended[n * tile_rows : (n + 1) * tile_rows]
        delta = jnp.sum(
            do.astype(F32).T * mixed.astype(BF).astype(F32), axis=0, keepdims=True
        )
        q_grad = jnp.zeros((HD, lanes), F32)
        for m in range(chunks):
            span_keys = pl.ds(m * chunk_keys, chunk_keys)
            values = kv_refs[m][:, :, :, HD:].reshape(chunk_keys, HD)
            keys = kv_refs[m][:, :, :, :HD].reshape(chunk_keys, HD)
            grad_w = lax.dot_general(values, do, (((1,), (1,)), ((), ())), preferred_element_type=F32)
            grad_s = ((e_ref[span_keys, :] * inverse) * (grad_w - delta)).astype(BF)
            ds_ref[span_keys, out_span] = grad_s
            q_grad = q_grad + lax.dot_general(
                keys, grad_s, (((0,), (0,)), ((), ())), preferred_element_type=F32
            )
        q_grad = (q_grad.T * scaling).astype(BF)
        for n in range(heads):
            out_refs[step][1, span, pl.ds(n * HD, HD)] = q_grad[n * tile_rows : (n + 1) * tile_rows]
    for m in range(chunks):
        span_keys = pl.ds(m * chunk_keys, chunk_keys)
        k_grad = jnp.dot(ds_ref[span_keys, :], q_all[...], preferred_element_type=F32)
        v_grad = jnp.dot(p_ref[span_keys, :], do_all[...], preferred_element_type=F32)
        dkv_refs[m][:, :, :, :HD] = k_grad.astype(BF).reshape(z_size, kv, rows, HD)
        dkv_refs[m][:, :, :, HD:] = v_grad.astype(BF).reshape(z_size, kv, rows, HD)


def sum_heads_kernel(parts, *refs):
    for m_z, out_ref in enumerate(refs[parts:]):
        total = refs[0][m_z].astype(F32)
        for ref in refs[1:parts]:
            total = total + ref[m_z].astype(F32)
        out_ref[...] = total.astype(BF)


def sum_z_kernel(kv, *refs):
    ins, outs = refs[:-kv], refs[-kv:]
    for s, out_ref in enumerate(outs):
        total = ins[0][s].astype(F32)
        for ref in ins[1:]:
            total = total + ref[s].astype(F32)
        out_ref[...] = total.astype(BF)


def finish_kv_kernel(kv, scaling, core_ref, *refs):
    key_ref, value_ref = refs[kv:]
    for core in range(kv):

        @pl.when(core_ref[0] == core)
        def _():
            for s in range(kv):
                cols = pl.ds((core ^ s) * HD, HD)
                key_ref[:, cols] = (refs[s][:, :HD].astype(F32) * scaling).astype(BF)
                value_ref[:, cols] = refs[s][:, HD:]


def finish_q_kernel(kv, core_ref, *refs):
    att_ref, grad_ref = refs[kv:]
    width = refs[0].shape[2]
    for core in range(kv):

        @pl.when(core_ref[0] == core)
        def _():
            for s in range(kv):
                cols = pl.ds((core ^ s) * width, width)
                att_ref[:, cols] = refs[s][0]
                grad_ref[:, cols] = refs[s][1]


def call(kernel, ins, specs, outs, scratch=(), scratch_bytes=0, cost=None, name=None):
    out_specs = [VMEM] * len(outs)
    single = len(outs) == 1
    return pl.pallas_call(
        kernel,
        out_shape=outs[0] if single else tuple(outs),
        in_specs=specs,
        out_specs=out_specs[0] if single else tuple(out_specs),
        scratch_shapes=list(scratch),
        compiler_params=params(nbytes(*ins), nbytes(*outs), scratch_bytes),
        cost_estimate=cost,
        name=name,
    )(*ins)


def shards(queries, key_vectors, value_vectors, out_grad, block_order):
    heads_devices = lax.axis_size("head")
    ctx_devices = lax.axis_size("ctx")
    halves, block_rows, query_width = queries.shape
    kv = key_vectors.shape[2] // HD
    rows = halves * block_rows
    width = query_width // kv
    group = width // HD
    block_len = block_rows * heads_devices
    ctx = lax.axis_index("ctx").astype(jnp.int32)
    core = (ctx % kv).reshape(1)
    z_devices = ctx_devices // kv
    place = jnp.stack([lax.axis_index("head").astype(jnp.int32), ctx // kv, ctx % kv])
    queries = queries.reshape(rows, query_width)
    out_grad = out_grad.reshape(rows, query_width)
    key_vectors = key_vectors.reshape(rows, kv * HD)
    value_vectors = value_vectors.reshape(rows, kv * HD)

    def shape(*dims):
        return jax.ShapeDtypeStruct(dims, BF)

    def from_cores(block):
        return [block] + [swap(block, "ctx", step) for step in range(1, kv)]

    def from_z(block):
        return [block] + [swap(block, "ctx", m * kv) for m in range(1, z_devices)]

    def from_heads(block):
        return [block] + [swap(block, "head", m) for m in range(1, heads_devices)]

    key_parts, value_parts = from_cores(key_vectors), from_cores(value_vectors)
    piece = call(
        functools.partial(pack_kv_kernel, kv),
        (core, *[part for pair in zip(key_parts, value_parts) for part in pair]),
        [SMEM] + [VMEM] * (2 * kv),
        [shape(kv, rows, 2 * HD)],
        name="pack_kv",
    )
    column = jnp.stack(from_z(piece))
    kv_parts = from_heads(column)
    query_parts, grad_parts = from_cores(queries), from_cores(out_grad)

    tile_rows = block_rows if block_rows % 16 == 0 else rows
    lanes = group * tile_rows
    keys = heads_devices * ctx_devices * rows
    query_rows = kv * group * rows
    scratch = [
        pltpu.VMEM((query_rows, HD), BF),
        pltpu.VMEM((query_rows, HD), BF),
        pltpu.VMEM((keys, lanes), F32),
        pltpu.VMEM((keys, query_rows), BF),
        pltpu.VMEM((keys, query_rows), BF),
    ]
    outs = call(
        functools.partial(
            attend_kernel, kv, block_len, block_rows, tile_rows, group, heads_devices
        ),
        (block_order, place, *query_parts, *grad_parts, *kv_parts),
        [SMEM, SMEM] + [VMEM] * (2 * kv + heads_devices),
        [shape(2, rows, width)] * kv + [shape(z_devices, kv, rows, 2 * HD)] * heads_devices,
        scratch,
        4 * query_rows * HD + keys * (4 * lanes + 4 * query_rows),
        name="attend",
    )
    out_parts, dkv = outs[:kv], outs[kv:]
    dkv_parts = [dkv[0]] + [swap(dkv[m], "head", m) for m in range(1, heads_devices)]
    out_parts = [out_parts[0]] + [swap(out_parts[s], "ctx", s) for s in range(1, kv)]
    z_parts = call(
        functools.partial(sum_heads_kernel, heads_devices),
        tuple(dkv_parts),
        [VMEM] * heads_devices,
        [shape(kv, rows, 2 * HD)] * z_devices,
        name="sum_heads",
    )
    z_parts = [z_parts[0]] + [swap(z_parts[m], "ctx", m * kv) for m in range(1, z_devices)]
    core_parts = call(
        functools.partial(sum_z_kernel, kv),
        tuple(z_parts),
        [VMEM] * z_devices,
        [shape(rows, 2 * HD)] * kv,
        name="sum_z",
    )
    core_parts = [core_parts[0]] + [swap(core_parts[s], "ctx", s) for s in range(1, kv)]
    attended, query_grad = call(
        functools.partial(finish_q_kernel, kv),
        (core, *out_parts),
        [SMEM] + [VMEM] * kv,
        [shape(rows, query_width)] * 2,
        name="finish_q",
    )
    key_grad, value_grad = call(
        functools.partial(finish_kv_kernel, kv, 1.0 / math.sqrt(HD)),
        (core, *core_parts),
        [SMEM] + [VMEM] * kv,
        [shape(rows, kv * HD)] * 2,
        name="finish_kv",
    )
    return (
        attended.reshape(halves, block_rows, query_width),
        query_grad.reshape(halves, block_rows, query_width),
        key_grad.reshape(halves, block_rows, kv * HD),
        value_grad.reshape(halves, block_rows, kv * HD),
    )


def solution(mesh):
    split = P("ctx", "head", None)
    return jax.shard_map(
        shards,
        mesh=mesh,
        in_specs=(split, split, split, split, P()),
        out_specs=(split, split, split, split),
        check_vma=False,
    )
```

```python
import functools
import math

import jax
import jax.numpy as jnp
from jax import lax
from jax.experimental import pallas as pl
from jax.experimental.pallas import tpu as pltpu
from jax.sharding import PartitionSpec as P

HD = 128
BF = jnp.bfloat16
F32 = jnp.float32
LOWEST = -1e30
CORES = 2


def params(*arrays_bytes):
    limit = int(sum(arrays_bytes)) + (12 << 20)
    return pltpu.CompilerParams(vmem_limit_bytes=min(limit, 60 << 20))


def nbytes(*shapes):
    return sum(math.prod(s.shape) * s.dtype.itemsize for s in shapes)


VMEM = pl.BlockSpec(memory_space=pltpu.VMEM)
SMEM = pl.BlockSpec(memory_space=pltpu.SMEM)


def swap(block, axis, mask):
    size = lax.axis_size(axis)
    return lax.ppermute(block, axis, [(i, i ^ mask) for i in range(size)])


def pack_own_kernel(kv, group_ref, key_ref, value_ref, out_ref):
    for g in range(kv):

        @pl.when(group_ref[0] == g)
        def _():
            cols = pl.ds(g * HD, HD)
            out_ref[:, :HD] = key_ref[:, cols]
            out_ref[:, HD:] = value_ref[:, cols]


def pack_kv_kernel(kv, group_ref, own_ref, *refs):
    out_ref = refs[-1]
    out_ref[0] = own_ref[...]
    for g in range(kv):

        @pl.when(group_ref[0] == g)
        def _():
            cols = pl.ds(g * HD, HD)
            for s in range(1, kv):
                out_ref[s, :, :HD] = refs[2 * s - 2][:, cols]
                out_ref[s, :, HD:] = refs[2 * s - 1][:, cols]


def pack_q_kernel(kv, group_ref, query_ref, grad_ref, *out_refs):
    width = out_refs[0].shape[2]
    for g in range(kv):

        @pl.when(group_ref[0] == g)
        def _():
            for s in range(1, kv):
                cols = pl.ds((g ^ s) * width, width)
                out_refs[s - 1][0] = query_ref[:, cols]
                out_refs[s - 1][1] = grad_ref[:, cols]


def attend_kernel(
    kv,
    block_len,
    block_rows,
    tile_rows,
    heads,
    cores,
    chunks,
    order_ref,
    place_ref,
    *refs,
):
    q_own, do_own, refs = refs[0], refs[1], refs[2:]
    q_parts, refs = refs[: kv - 1], refs[kv - 1 :]
    kv_refs, refs = refs[:chunks], refs[chunks:]
    out_refs, refs = refs[:kv], refs[kv:]
    dkv_refs, refs = refs[:chunks], refs[chunks:]
    q_all, do_all, e_ref, p_ref, ds_ref = refs
    rows = q_own.shape[0]
    z_size = kv_refs[0].shape[0]
    chunk_keys = z_size * kv * rows
    blocks_here = rows // block_rows
    lanes = heads * tile_rows
    scaling = 1.0 / math.sqrt(HD)
    expo = scaling * math.log2(math.e)
    head_place = place_ref[0]
    ctx_place = place_ref[1]
    first_col = (head_place % kv) * (heads * HD)
    lane_row = lax.broadcasted_iota(jnp.int32, (1, lanes), 1) % tile_rows
    key_iota = lax.broadcasted_iota(jnp.int32, (block_rows, lanes), 0)
    tiles = [(step, start) for step in range(kv) for start in range(0, rows, tile_rows)]
    for tile, (step, start) in enumerate(tiles):
        span = pl.ds(start, tile_rows)
        out_span = pl.ds(tile * lanes, lanes)
        for n in range(heads):
            at = pl.ds(tile * lanes + n * tile_rows, tile_rows)
            if step == 0:
                cols = pl.ds(pl.multiple_of(first_col + n * HD, HD), HD)
                q_all[at, :] = q_own[span, cols]
                do_all[at, :] = do_own[span, cols]
            else:
                q_all[at, :] = q_parts[step - 1][0, span, pl.ds(n * HD, HD)]
                do_all[at, :] = q_parts[step - 1][1, span, pl.ds(n * HD, HD)]
        q = q_all[out_span, :]
        do = do_all[out_span, :]
        part_row = (head_place ^ step) * block_rows
        query_pos = jnp.zeros((1, lanes), jnp.int32)
        for b in range(start // block_rows, -(-(start + tile_rows) // block_rows)):
            block_pos = order_ref[ctx_place * blocks_here + b] * block_len + part_row
            here = (lane_row + start) // block_rows == b
            query_pos = jnp.where(here, block_pos + (lane_row + start) % block_rows, query_pos)
        gap = query_pos - key_iota
        row_max = jnp.full((8, lanes), LOWEST, F32)
        for m in range(chunks):
            keys = kv_refs[m][:, :, :, :HD].reshape(chunk_keys, HD)
            scores = lax.dot_general(keys, q, (((1,), (1,)), ((), ())), preferred_element_type=F32)
            a, core = divmod(m, cores)
            for j in range(chunk_keys // block_rows):
                m_z, s_b = divmod(j, kv * blocks_here)
                s, b = divmod(s_b, blocks_here)
                stored = (ctx_place ^ (m_z * cores + core)) * blocks_here + b
                key_pos = order_ref[stored] * block_len + (head_place ^ (a * kv + s)) * block_rows
                part = scores[j * block_rows : (j + 1) * block_rows]
                part = jnp.where(gap >= key_pos, part, LOWEST)
                e_ref[pl.ds(m * chunk_keys + j * block_rows, block_rows), :] = part
                row_max = jnp.maximum(row_max, jnp.max(part.reshape(block_rows // 8, 8, lanes), axis=0))
        top = jnp.max(row_max, axis=0, keepdims=True) * expo
        row_sum = jnp.zeros((8, lanes), F32)
        for m in range(chunks):
            span_keys = pl.ds(m * chunk_keys, chunk_keys)
            part = jnp.exp2(e_ref[span_keys, :] * expo - top)
            e_ref[span_keys, :] = part
            row_sum = row_sum + jnp.sum(part.reshape(chunk_keys // 8, 8, lanes), axis=0)
        inverse = 1.0 / jnp.sum(row_sum, axis=0, keepdims=True)
        mixed = jnp.zeros((HD, lanes), F32)
        for m in range(chunks):
            span_keys = pl.ds(m * chunk_keys, chunk_keys)
            probs = (e_ref[span_keys, :] * inverse).astype(BF)
            p_ref[span_keys, out_span] = probs
            values = kv_refs[m][:, :, :, HD:].reshape(chunk_keys, HD)
            mixed = mixed + lax.dot_general(
                values, probs, (((0,), (0,)), ((), ())), preferred_element_type=F32
            )
        attended = mixed.T.astype(BF)
        for n in range(heads):
            out_refs[step][0, span, pl.ds(n * HD, HD)] = attended[n * tile_rows : (n + 1) * tile_rows]
        delta = jnp.sum(
            do.astype(F32).T * mixed.astype(BF).astype(F32), axis=0, keepdims=True
        )
        q_grad = jnp.zeros((HD, lanes), F32)
        for m in range(chunks):
            span_keys = pl.ds(m * chunk_keys, chunk_keys)
            values = kv_refs[m][:, :, :, HD:].reshape(chunk_keys, HD)
            keys = kv_refs[m][:, :, :, :HD].reshape(chunk_keys, HD)
            grad_w = lax.dot_general(values, do, (((1,), (1,)), ((), ())), preferred_element_type=F32)
            grad_s = ((e_ref[span_keys, :] * inverse) * (grad_w - delta)).astype(BF)
            ds_ref[span_keys, out_span] = grad_s
            q_grad = q_grad + lax.dot_general(
                keys, grad_s, (((0,), (0,)), ((), ())), preferred_element_type=F32
            )
        q_grad = (q_grad.T * scaling).astype(BF)
        for n in range(heads):
            out_refs[step][1, span, pl.ds(n * HD, HD)] = q_grad[n * tile_rows : (n + 1) * tile_rows]
    for m in range(chunks):
        span_keys = pl.ds(m * chunk_keys, chunk_keys)
        k_grad = jnp.dot(ds_ref[span_keys, :], q_all[...], preferred_element_type=F32)
        v_grad = jnp.dot(p_ref[span_keys, :], do_all[...], preferred_element_type=F32)
        dkv_refs[m][:, :, :, :HD] = k_grad.astype(BF).reshape(z_size, kv, rows, HD)
        dkv_refs[m][:, :, :, HD:] = v_grad.astype(BF).reshape(z_size, kv, rows, HD)


def sum_heads_kernel(parts, *refs):
    for m_z, out_ref in enumerate(refs[parts:]):
        total = refs[0][m_z].astype(F32)
        for ref in refs[1:parts]:
            total = total + ref[m_z].astype(F32)
        out_ref[...] = total.astype(BF)


def sum_cores_kernel(count, *refs):
    for a in range(count):
        total = refs[2 * a][...].astype(F32) + refs[2 * a + 1][...].astype(F32)
        refs[2 * count + a][...] = total.astype(BF)


def sum_z_kernel(kv, *refs):
    ins, outs = refs[:-kv], refs[-kv:]
    for s, out_ref in enumerate(outs):
        total = ins[0][s].astype(F32)
        for ref in ins[1:]:
            total = total + ref[s].astype(F32)
        out_ref[...] = total.astype(BF)


def finish_kv_kernel(kv, scaling, group_ref, *refs):
    key_ref, value_ref = refs[kv:]
    for g in range(kv):

        @pl.when(group_ref[0] == g)
        def _():
            for s in range(kv):
                cols = pl.ds((g ^ s) * HD, HD)
                key_ref[:, cols] = (refs[s][:, :HD].astype(F32) * scaling).astype(BF)
                value_ref[:, cols] = refs[s][:, HD:]


def finish_q_kernel(kv, group_ref, *refs):
    att_ref, grad_ref = refs[kv:]
    width = refs[0].shape[2]
    for g in range(kv):

        @pl.when(group_ref[0] == g)
        def _():
            for s in range(kv):
                cols = pl.ds((g ^ s) * width, width)
                att_ref[:, cols] = refs[s][0]
                grad_ref[:, cols] = refs[s][1]


def call(kernel, ins, specs, outs, scratch=(), scratch_bytes=0, cost=None, name=None):
    out_specs = [VMEM] * len(outs)
    single = len(outs) == 1
    return pl.pallas_call(
        kernel,
        out_shape=outs[0] if single else tuple(outs),
        in_specs=specs,
        out_specs=out_specs[0] if single else tuple(out_specs),
        scratch_shapes=list(scratch),
        compiler_params=params(nbytes(*ins), nbytes(*outs), scratch_bytes),
        cost_estimate=cost,
        name=name,
    )(*ins)


def shards(queries, key_vectors, value_vectors, out_grad, block_order):
    heads_devices = lax.axis_size("head")
    ctx_devices = lax.axis_size("ctx")
    halves, block_rows, query_width = queries.shape
    kv = key_vectors.shape[2] // HD
    rows = halves * block_rows
    width = query_width // kv
    group = width // HD
    block_len = block_rows * heads_devices
    head = lax.axis_index("head").astype(jnp.int32)
    place = jnp.stack([head, lax.axis_index("ctx").astype(jnp.int32)])
    own_group = (head % kv).reshape(1)
    cores = CORES if ctx_devices % CORES == 0 else 1
    z_devices = ctx_devices // cores
    spans = heads_devices // kv
    queries = queries.reshape(rows, query_width)
    out_grad = out_grad.reshape(rows, query_width)
    key_vectors = key_vectors.reshape(rows, kv * HD)
    value_vectors = value_vectors.reshape(rows, kv * HD)

    def shape(*dims):
        return jax.ShapeDtypeStruct(dims, BF)

    key_parts = [swap(key_vectors, "head", s) for s in range(1, kv)]
    value_parts = [swap(value_vectors, "head", s) for s in range(1, kv)]
    own = call(
        functools.partial(pack_own_kernel, kv),
        (own_group, key_vectors, value_vectors),
        [SMEM, VMEM, VMEM],
        [shape(rows, 2 * HD)],
        name="pack_own",
    )
    piece = call(
        functools.partial(pack_kv_kernel, kv),
        (own_group, own, *[part for pair in zip(key_parts, value_parts) for part in pair]),
        [SMEM] + [VMEM] * (2 * kv - 1),
        [shape(kv, rows, 2 * HD)],
        name="pack_kv",
    )
    column = jnp.stack([piece] + [swap(piece, "ctx", m * cores) for m in range(1, z_devices)])
    q_sends = pl.pallas_call(
        functools.partial(pack_q_kernel, kv),
        out_shape=[shape(2, rows, width)] * (kv - 1),
        in_specs=[SMEM, VMEM, VMEM],
        out_specs=[VMEM] * (kv - 1),
        name="pack_q",
    )(own_group, queries, out_grad)
    q_parts = [swap(q_sends[s - 1], "head", s) for s in range(1, kv)]
    kv_parts = []
    for a in range(spans):
        part = column if a == 0 else swap(column, "head", a * kv)
        kv_parts += [part] + [swap(part, "ctx", core) for core in range(1, cores)]
    chunks = spans * cores

    tile_rows = block_rows if block_rows % 16 == 0 else rows
    lanes = group * tile_rows
    keys = heads_devices * ctx_devices * rows
    query_rows = kv * group * rows
    scratch = [
        pltpu.VMEM((query_rows, HD), BF),
        pltpu.VMEM((query_rows, HD), BF),
        pltpu.VMEM((keys, lanes), F32),
        pltpu.VMEM((keys, query_rows), BF),
        pltpu.VMEM((keys, query_rows), BF),
    ]
    outs = call(
        functools.partial(
            attend_kernel, kv, block_len, block_rows, tile_rows, group, cores, chunks
        ),
        (block_order, place, queries, out_grad, *q_parts, *kv_parts),
        [SMEM, SMEM] + [VMEM] * (1 + kv + chunks),
        [shape(2, rows, width)] * kv + [shape(z_devices, kv, rows, 2 * HD)] * chunks,
        scratch,
        4 * query_rows * HD + keys * (4 * lanes + 4 * query_rows),
        name="attend",
    )
    out_parts, dkv = outs[:kv], outs[kv:]
    if cores > 1:
        both = [
            part
            for a in range(spans)
            for part in (dkv[a * cores], swap(dkv[a * cores + 1], "ctx", 1))
        ]
        dkv = call(
            functools.partial(sum_cores_kernel, spans),
            tuple(both),
            [VMEM] * (2 * spans),
            [shape(z_devices, kv, rows, 2 * HD)] * spans,
            name="sum_cores",
        )
    span_parts = [dkv[0]] + [swap(dkv[a], "head", a * kv) for a in range(1, spans)]
    out_parts = [out_parts[0]] + [swap(out_parts[s], "head", s) for s in range(1, kv)]
    z_parts = call(
        functools.partial(sum_heads_kernel, spans),
        tuple(span_parts),
        [VMEM] * spans,
        [shape(kv, rows, 2 * HD)] * z_devices,
        name="sum_heads",
    )
    z_parts = [z_parts[0]] + [swap(z_parts[m], "ctx", m * cores) for m in range(1, z_devices)]
    pair_parts = call(
        functools.partial(sum_z_kernel, kv),
        tuple(z_parts),
        [VMEM] * z_devices,
        [shape(rows, 2 * HD)] * kv,
        name="sum_z",
    )
    pair_parts = [pair_parts[0]] + [swap(pair_parts[s], "head", s) for s in range(1, kv)]
    attended, query_grad = call(
        functools.partial(finish_q_kernel, kv),
        (own_group, *out_parts),
        [SMEM] + [VMEM] * kv,
        [shape(rows, query_width)] * 2,
        name="finish_q",
    )
    key_grad, value_grad = call(
        functools.partial(finish_kv_kernel, kv, 1.0 / math.sqrt(HD)),
        (own_group, *pair_parts),
        [SMEM] + [VMEM] * kv,
        [shape(rows, kv * HD)] * 2,
        name="finish_kv",
    )
    return (
        attended.reshape(halves, block_rows, query_width),
        query_grad.reshape(halves, block_rows, query_width),
        key_grad.reshape(halves, block_rows, kv * HD),
        value_grad.reshape(halves, block_rows, kv * HD),
    )


def solution(mesh):
    split = P("ctx", "head", None)
    return jax.shard_map(
        shards,
        mesh=mesh,
        in_specs=(split, split, split, split, P()),
        out_specs=(split, split, split, split),
        check_vma=False,
    )
```

```python
import functools
import math

import jax
import jax.numpy as jnp
from jax import lax
from jax.experimental import pallas as pl
from jax.experimental.pallas import tpu as pltpu
from jax.sharding import PartitionSpec as P

HD = 128
CORES = 2
BF = jnp.bfloat16
F32 = jnp.float32
LOWEST = -1e30
FLOOR = -1e29
SCALING = 1.0 / math.sqrt(HD)
EXPO = SCALING * math.log2(math.e)

VMEM = pl.BlockSpec(memory_space=pltpu.VMEM)
SMEM = pl.BlockSpec(memory_space=pltpu.SMEM)
HBM = pl.BlockSpec(memory_space=pltpu.HBM)


def swap(block, axis, mask):
    size = lax.axis_size(axis)
    return lax.ppermute(block, axis, [(i, i ^ mask) for i in range(size)])


def nbytes(arrays):
    return sum(math.prod(a.shape) * a.dtype.itemsize for a in arrays)


def after(blocks, earlier):
    return lax.optimization_barrier((tuple(blocks), tuple(earlier)))[0]


def call(kernel, name, ins, outs, specs=None, scratch=(), extra=0, flops=0):
    limit = nbytes(ins) + nbytes(outs) + extra + (12 << 20)
    return pl.pallas_call(
        kernel,
        out_shape=list(outs),
        in_specs=specs or [VMEM] * len(ins),
        out_specs=[VMEM] * len(outs),
        scratch_shapes=list(scratch),
        compiler_params=pltpu.CompilerParams(vmem_limit_bytes=min(limit, 60 << 20)),
        cost_estimate=pl.CostEstimate(
            flops=flops, bytes_accessed=nbytes(ins) + nbytes(outs), transcendentals=0
        ),
        name=name,
    )(*ins)


def dot(left, right):
    return jnp.dot(left, right, preferred_element_type=F32)


def dot_rows(left, right):
    return lax.dot_general(left, right, (((1,), (1,)), ((), ())), preferred_element_type=F32)


def pack_own_kernel(kv, group_ref, key_ref, value_ref, query_ref, grad_ref, *refs):
    out_ref, q_outs, refs = refs[0], refs[1 : kv + 1], refs[kv + 1 :]
    key_buf, value_buf, query_buf, grad_buf, sems = refs
    pairs = ((key_ref, key_buf), (value_ref, value_buf), (query_ref, query_buf), (grad_ref, grad_buf))
    copies = [pltpu.make_async_copy(src, dst, sems.at[i]) for i, (src, dst) in enumerate(pairs)]
    for copy in copies:
        copy.start()
    for copy in copies:
        copy.wait()
    width = q_outs[0].shape[2]
    for g in range(kv):

        @pl.when(group_ref[0] == g)
        def _():
            cols = pl.ds(g * HD, HD)
            out_ref[:, :HD] = key_buf[:, cols]
            out_ref[:, HD:] = value_buf[:, cols]
            for s in range(kv):
                theirs = pl.ds((g ^ s) * width, width)
                q_outs[s][0] = query_buf[:, theirs]
                q_outs[s][1] = grad_buf[:, theirs]


def pack_kv_kernel(kv, group_ref, own_ref, *refs):
    out_ref = refs[-1]
    out_ref[0] = own_ref[...]
    for g in range(kv):

        @pl.when(group_ref[0] == g)
        def _():
            cols = pl.ds(g * HD, HD)
            for s in range(1, kv):
                out_ref[s, :, :HD] = refs[2 * s - 2][:, cols]
                out_ref[s, :, HD:] = refs[2 * s - 1][:, cols]


class Plan:
    def __init__(self, kv, block_len, block_rows, rows, group, cores, z_devices):
        self.kv, self.block_len, self.block_rows, self.rows = kv, block_len, block_rows, rows
        self.group, self.cores, self.z_devices = group, cores, z_devices
        self.blocks = rows // block_rows
        self.tile_rows = block_rows if block_rows % 16 == 0 else rows
        self.lanes = group * self.tile_rows
        self.query_rows = kv * group * rows
        self.chunk_keys = z_devices * kv * rows
        self.tiles = [(s, start) for s in range(kv) for start in range(0, rows, self.tile_rows)]

    def at(self, tile):
        return pl.ds(tile * self.lanes, self.lanes)

    def keys_at(self, i):
        return pl.ds(i * self.chunk_keys, self.chunk_keys)

    def gap(self, tile, info_ref):
        s, start = self.tiles[tile]
        head, ctx = info_ref[0], info_ref[1]
        row = lax.broadcasted_iota(jnp.int32, (1, self.lanes), 1) % self.tile_rows + start
        pos = jnp.zeros((1, self.lanes), jnp.int32)
        for b in range(start // self.block_rows, -(-(start + self.tile_rows) // self.block_rows)):
            first = info_ref[2 + ctx * self.blocks + b] * self.block_len + (head ^ s) * self.block_rows
            pos = jnp.where(row // self.block_rows == b, first + row % self.block_rows, pos)
        return pos - lax.broadcasted_iota(jnp.int32, (self.block_rows, self.lanes), 0)

    def masked(self, scores, gap, chunk, info_ref):
        head, ctx = info_ref[0], info_ref[1]
        a, core = divmod(chunk, self.cores)
        for j in range(self.chunk_keys // self.block_rows):
            m, rest = divmod(j, self.kv * self.blocks)
            s, b = divmod(rest, self.blocks)
            stored = (ctx ^ (m * self.cores + core)) * self.blocks + b
            first = info_ref[2 + stored] * self.block_len + (head ^ (a * self.kv + s)) * self.block_rows
            part = scores[j * self.block_rows : (j + 1) * self.block_rows]
            yield j * self.block_rows, jnp.where(gap >= first, part, LOWEST)

    def turn(self, kv_refs, turned_ref):
        for i, ref in enumerate(kv_refs):
            turned_ref[:, self.keys_at(i)] = ref[...].reshape(self.chunk_keys, 2 * HD).T

    def keys(self, ref):
        return ref[:, :, :, :HD].reshape(self.chunk_keys, HD)

    def values(self, ref):
        return ref[:, :, :, HD:].reshape(self.chunk_keys, HD)

    def fold(self, block):
        return block.reshape(block.shape[0] // 8, 8, self.lanes)

    def scores(self, tile, first_chunk, kv_refs, q, e_ref, cols, info_ref):
        gap = self.gap(tile, info_ref)
        top = jnp.full((8, self.lanes), FLOOR, F32)
        for i, ref in enumerate(kv_refs):
            scores = dot_rows(self.keys(ref), q)
            for row, part in self.masked(scores, gap, first_chunk + i, info_ref):
                e_ref[pl.ds(i * self.chunk_keys + row, part.shape[0]), cols] = part
                top = jnp.maximum(top, jnp.max(self.fold(part), axis=0))
        return jnp.max(top, axis=0, keepdims=True)

    def exponents(self, count, e_ref, cols, top):
        total = jnp.zeros((8, self.lanes), F32)
        for i in range(count):
            part = jnp.exp2(e_ref[self.keys_at(i), cols] * EXPO - top * EXPO)
            e_ref[self.keys_at(i), cols] = part
            total = total + jnp.sum(self.fold(part), axis=0)
        return jnp.sum(total, axis=0, keepdims=True)

    def store_heads(self, out_ref, tile, turned):
        s, start = self.tiles[tile]
        block = turned.T.astype(BF)
        for n in range(self.group):
            piece = block[n * self.tile_rows : (n + 1) * self.tile_rows]
            out_ref[pl.ds(start, self.tile_rows), pl.ds(n * HD, HD)] = piece

    def back(self, kv_refs, dkv_refs, p_ref, ds_ref, q_ref, do_ref):
        shape = (self.z_devices, self.kv, self.rows, HD)
        for i, out_ref in enumerate(dkv_refs):
            k_grad = dot(ds_ref[self.keys_at(i), :], q_ref[...])
            v_grad = dot(p_ref[self.keys_at(i), :], do_ref[...])
            out_ref[:, :, :, :HD] = k_grad.astype(BF).reshape(shape)
            out_ref[:, :, :, HD:] = v_grad.astype(BF).reshape(shape)


def near_kernel(plan, info_ref, *refs):
    kv, chunks = plan.kv, plan.cores
    q_parts, refs = refs[:kv], refs[kv:]
    kv_refs, refs = refs[:chunks], refs[chunks:]
    q_all, do_all, e_ref, top_ref, sum_ref, mix_ref, turned_ref = refs
    plan.turn(kv_refs, turned_ref)
    for tile, (s, start) in enumerate(plan.tiles):
        span = pl.ds(start, plan.tile_rows)
        for n in range(plan.group):
            at = pl.ds(tile * plan.lanes + n * plan.tile_rows, plan.tile_rows)
            q_all[at, :] = q_parts[s][0, span, pl.ds(n * HD, HD)]
            do_all[at, :] = q_parts[s][1, span, pl.ds(n * HD, HD)]
    for tile in range(len(plan.tiles)):
        at = plan.at(tile)
        top = plan.scores(tile, 0, kv_refs, q_all[at, :], e_ref, at, info_ref)
        top_ref[:, at] = top
        sum_ref[:, at] = plan.exponents(chunks, e_ref, at, top)
        mixed = jnp.zeros((HD, plan.lanes), F32)
        for i in range(chunks):
            weights = e_ref[plan.keys_at(i), at].astype(BF)
            mixed = mixed + dot(turned_ref[pl.ds(HD, HD), plan.keys_at(i)], weights)
        mix_ref[:, at] = mixed


def far_kernel(plan, chunks, info_ref, q_all, do_all, near_top, near_sum, near_mix, *refs):
    kv = plan.kv
    kv_refs, refs = refs[:chunks], refs[chunks:]
    att_refs, refs = refs[:kv], refs[kv:]
    near_scale, delta_ref, q_grad_ref = refs[:3]
    dkv_refs, refs = refs[3 : 3 + chunks], refs[3 + chunks :]
    turned_ref, e_ref, p_ref, ds_ref = refs
    here = pl.ds(0, plan.lanes)
    plan.turn(kv_refs, turned_ref)
    for tile, (s, _) in enumerate(plan.tiles):
        at = plan.at(tile)
        top = plan.scores(tile, plan.cores, kv_refs, q_all[at, :], e_ref, here, info_ref)
        top = jnp.maximum(top, near_top[:, at])
        total = plan.exponents(chunks, e_ref, here, top)
        factor = jnp.exp2((near_top[:, at] - top) * EXPO)
        inverse = 1.0 / (total + factor * near_sum[:, at])
        near_scale[:, at] = factor * inverse
        mixed = near_mix[:, at] * (factor * inverse)
        for i in range(chunks):
            probs = (e_ref[plan.keys_at(i), here] * inverse).astype(BF)
            p_ref[plan.keys_at(i), at] = probs
            mixed = mixed + dot(turned_ref[pl.ds(HD, HD), plan.keys_at(i)], probs)
        plan.store_heads(att_refs[s], tile, mixed)
        do = do_all[at, :]
        delta = jnp.sum(do.astype(F32).T * mixed.astype(BF).astype(F32), axis=0, keepdims=True)
        delta_ref[:, at] = delta
        q_grad = jnp.zeros((HD, plan.lanes), F32)
        for i, ref in enumerate(kv_refs):
            probs = e_ref[plan.keys_at(i), here] * inverse
            grad_s = (probs * (dot_rows(plan.values(ref), do) - delta)).astype(BF)
            ds_ref[plan.keys_at(i), at] = grad_s
            q_grad = q_grad + dot(turned_ref[pl.ds(0, HD), plan.keys_at(i)], grad_s)
        q_grad_ref[:, at] = q_grad
    plan.back(kv_refs, dkv_refs, p_ref, ds_ref, q_all, do_all)


def near_back_kernel(plan, chunk, q_all, do_all, e_ref, near_scale, delta_ref, q_grad_in, kv_ref, *refs):
    outs, (dkv_ref, turned_ref, p_ref, ds_ref) = refs[:-4], refs[-4:]
    plan.turn([kv_ref], turned_ref)
    for tile, (s, _) in enumerate(plan.tiles):
        at = plan.at(tile)
        do = do_all[at, :]
        probs = e_ref[plan.keys_at(chunk), at] * near_scale[:, at]
        p_ref[:, at] = probs.astype(BF)
        grad_s = (probs * (dot_rows(plan.values(kv_ref), do) - delta_ref[:, at])).astype(BF)
        ds_ref[:, at] = grad_s
        q_grad = q_grad_in[:, at] + dot(turned_ref[pl.ds(0, HD), :], grad_s)
        if chunk == 0:
            plan.store_heads(outs[s], tile, q_grad * SCALING)
        else:
            outs[0][:, at] = q_grad
    plan.back([kv_ref], [dkv_ref], p_ref, ds_ref, q_all, do_all)


def add_kernel(*refs):
    total = refs[0][...].astype(F32)
    for ref in refs[1:-1]:
        total = total + ref[...].astype(F32)
    refs[-1][...] = total.astype(BF)


def sum_heads_kernel(parts, *refs):
    for m_z, out_ref in enumerate(refs[parts:]):
        total = refs[0][m_z].astype(F32)
        for ref in refs[1:parts]:
            total = total + ref[m_z].astype(F32)
        out_ref[...] = total.astype(BF)


def sum_z_kernel(kv, *refs):
    ins, outs = refs[:-kv], refs[-kv:]
    for s, out_ref in enumerate(outs):
        total = ins[0][s].astype(F32)
        for ref in ins[1:]:
            total = total + ref[s].astype(F32)
        out_ref[...] = total.astype(BF)


def finish_kv_kernel(kv, group_ref, *refs):
    key_ref, value_ref = refs[kv:]
    for g in range(kv):

        @pl.when(group_ref[0] == g)
        def _():
            for s in range(kv):
                cols = pl.ds((g ^ s) * HD, HD)
                key_ref[:, cols] = (refs[s][:, :HD].astype(F32) * SCALING).astype(BF)
                value_ref[:, cols] = refs[s][:, HD:]


def finish_q_kernel(kv, group_ref, *refs):
    att_ref, grad_ref = refs[2 * kv :]
    width = refs[0].shape[1]
    for g in range(kv):

        @pl.when(group_ref[0] == g)
        def _():
            for s in range(kv):
                cols = pl.ds((g ^ s) * width, width)
                att_ref[:, cols] = refs[s][...]
                grad_ref[:, cols] = refs[kv + s][...]


def shards(queries, key_vectors, value_vectors, out_grad, block_order):
    heads_devices = lax.axis_size("head")
    ctx_devices = lax.axis_size("ctx")
    halves, block_rows, query_width = queries.shape
    kv = key_vectors.shape[2] // HD
    rows = halves * block_rows
    width = query_width // kv
    cores = CORES if ctx_devices % CORES == 0 else 1
    z_devices = ctx_devices // cores
    spans = heads_devices // kv
    plan = Plan(kv, block_rows * heads_devices, block_rows, rows, width // HD, cores, z_devices)
    head = lax.axis_index("head").astype(jnp.int32)
    place = jnp.stack([head, lax.axis_index("ctx").astype(jnp.int32)])
    info = jnp.concatenate([place, block_order])
    own_group = (head % kv).reshape(1)
    queries = queries.reshape(rows, query_width)
    out_grad = out_grad.reshape(rows, query_width)
    key_vectors = key_vectors.reshape(rows, kv * HD)
    value_vectors = value_vectors.reshape(rows, kv * HD)

    def bf(*dims):
        return jax.ShapeDtypeStruct(dims, BF)

    def f32(*dims):
        return jax.ShapeDtypeStruct(dims, F32)

    def with_swaps(blocks):
        return [blocks[0]] + [swap(blocks[s], "head", s) for s in range(1, kv)]

    key_parts = [swap(key_vectors, "head", s) for s in range(1, kv)]
    value_parts = [swap(value_vectors, "head", s) for s in range(1, kv)]
    own, *q_parts = pl.pallas_call(
        functools.partial(pack_own_kernel, kv),
        out_shape=[bf(rows, 2 * HD)] + [bf(2, rows, width)] * kv,
        in_specs=[SMEM] + [HBM] * 4,
        out_specs=[VMEM] * (kv + 1),
        scratch_shapes=[pltpu.VMEM((rows, kv * HD), BF)] * 2
        + [pltpu.VMEM((rows, query_width), BF)] * 2
        + [pltpu.SemaphoreType.DMA((4,))],
        name="pack_own",
    )(own_group, key_vectors, value_vectors, queries, out_grad)
    q_parts = with_swaps(q_parts)
    piece = call(
        functools.partial(pack_kv_kernel, kv),
        "pack_kv",
        (own_group, own, *[part for pair in zip(key_parts, value_parts) for part in pair]),
        [bf(kv, rows, 2 * HD)],
        [SMEM] + [VMEM] * (2 * kv - 1),
    )[0]
    column = jnp.stack([piece] + [swap(piece, "ctx", m * cores) for m in range(1, z_devices)])
    columns = [swap(column, "head", a * kv) for a in range(1, spans)]
    near_kv = [column] + [swap(column, "ctx", core) for core in range(1, cores)]
    far_chunks = len(columns) * cores

    near_keys = len(near_kv) * plan.chunk_keys
    far_keys = far_chunks * plan.chunk_keys
    query_rows = plan.query_rows
    row = f32(1, query_rows)
    q_all, do_all, near_e, near_top, near_sum, near_mix = call(
        functools.partial(near_kernel, plan),
        "attend_near",
        (info, *q_parts, *near_kv),
        [bf(query_rows, HD)] * 2 + [f32(near_keys, query_rows), row, row, f32(HD, query_rows)],
        [SMEM] + [VMEM] * (kv + len(near_kv)),
        [pltpu.VMEM((2 * HD, near_keys), BF)],
        near_keys * 4 * HD,
        8 * near_keys * query_rows * HD,
    )
    columns = after(columns, [near_top])
    far_kv = []
    for part in columns:
        far_kv += [part] + [swap(part, "ctx", core) for core in range(1, cores)]
    outs = call(
        functools.partial(far_kernel, plan, len(far_kv)),
        "attend_far",
        (info, q_all, do_all, near_top, near_sum, near_mix, *far_kv),
        [bf(rows, width)] * kv
        + [row, row, f32(HD, query_rows)]
        + [bf(z_devices, kv, rows, 2 * HD)] * len(far_kv),
        [SMEM] + [VMEM] * (5 + len(far_kv)),
        [
            pltpu.VMEM((2 * HD, far_keys), BF),
            pltpu.VMEM((far_keys, plan.lanes), F32),
            pltpu.VMEM((far_keys, query_rows), BF),
            pltpu.VMEM((far_keys, query_rows), BF),
        ],
        far_keys * (4 * HD + 4 * plan.lanes + 4 * query_rows),
        16 * far_keys * query_rows * HD,
    )
    att_parts, outs = outs[:kv], outs[kv:]
    (near_scale, delta, far_q_grad), far_dkv = outs[:3], outs[3:]
    sums = []
    for a in range(spans - 1):
        parts = far_dkv[a * cores : (a + 1) * cores]
        swapped = [swap(parts[core], "ctx", core) for core in range(1, cores)]
        sums += call(add_kernel, "sum_cores", (parts[0], *swapped), [bf(*parts[0].shape)])
    near_dkv, q_grad = [], far_q_grad
    for chunk in reversed(range(cores)):
        q_outs = [f32(HD, query_rows)] if chunk else [bf(rows, width)] * kv
        outs = call(
            functools.partial(near_back_kernel, plan, chunk),
            "attend_near_back",
            (q_all, do_all, near_e, near_scale, delta, q_grad, near_kv[chunk]),
            q_outs + [bf(z_devices, kv, rows, 2 * HD)],
            None,
            [
                pltpu.VMEM((2 * HD, plan.chunk_keys), BF),
                pltpu.VMEM((plan.chunk_keys, query_rows), BF),
                pltpu.VMEM((plan.chunk_keys, query_rows), BF),
            ],
            plan.chunk_keys * (4 * HD + 4 * query_rows),
            12 * plan.chunk_keys * query_rows * HD,
        )
        q_grad = outs[0]
        near_dkv = [swap(outs[-1], "ctx", chunk) if chunk else outs[-1]] + near_dkv
    q_grad_parts = outs[:-1]
    sums = [swap(part, "head", (a + 1) * kv) for a, part in enumerate(sums)]
    sums = near_dkv + sums
    z_parts = call(
        functools.partial(sum_heads_kernel, len(sums)),
        "sum_heads",
        sums,
        [bf(kv, rows, 2 * HD)] * z_devices,
    )
    z_parts = [z_parts[0]] + [swap(z_parts[m], "ctx", m * cores) for m in range(1, z_devices)]
    pair_parts = call(
        functools.partial(sum_z_kernel, kv), "sum_z", z_parts, [bf(rows, 2 * HD)] * kv
    )
    pair_parts = with_swaps(pair_parts)
    attended, query_grad = call(
        functools.partial(finish_q_kernel, kv),
        "finish_q",
        (own_group, *with_swaps(att_parts), *with_swaps(q_grad_parts)),
        [bf(rows, query_width)] * 2,
        [SMEM] + [VMEM] * (2 * kv),
    )
    key_grad, value_grad = call(
        functools.partial(finish_kv_kernel, kv),
        "finish_kv",
        (own_group, *pair_parts),
        [bf(rows, kv * HD)] * 2,
        [SMEM] + [VMEM] * kv,
    )
    return (
        attended.reshape(halves, block_rows, query_width),
        query_grad.reshape(halves, block_rows, query_width),
        key_grad.reshape(halves, block_rows, kv * HD),
        value_grad.reshape(halves, block_rows, kv * HD),
    )


def solution(mesh):
    split = P("ctx", "head", None)
    return jax.shard_map(
        shards,
        mesh=mesh,
        in_specs=(split, split, split, split, P()),
        out_specs=(split, split, split, split),
        check_vma=False,
    )
```

```python
import functools
import math

import jax
import jax.numpy as jnp
from jax import lax
from jax.experimental import pallas as pl
from jax.experimental.pallas import tpu as pltpu
from jax.sharding import PartitionSpec as P

HD = 128
CORES = 2
BF = jnp.bfloat16
F32 = jnp.float32
LOWEST = -1e30
FLOOR = -1e29
SCALING = 1.0 / math.sqrt(HD)
EXPO = SCALING * math.log2(math.e)

VMEM = pl.BlockSpec(memory_space=pltpu.VMEM)
SMEM = pl.BlockSpec(memory_space=pltpu.SMEM)


def swap(block, axis, mask):
    size = lax.axis_size(axis)
    return lax.ppermute(block, axis, [(i, i ^ mask) for i in range(size)])


def nbytes(arrays):
    return sum(math.prod(a.shape) * a.dtype.itemsize for a in arrays)


def after(blocks, earlier):
    if not earlier:
        return tuple(blocks)
    return lax.optimization_barrier((tuple(blocks), tuple(earlier)))[0]


def call(kernel, name, ins, outs, specs=None, scratch=(), extra=0, flops=0):
    limit = nbytes(ins) + nbytes(outs) + extra + (12 << 20)
    return pl.pallas_call(
        kernel,
        out_shape=list(outs),
        in_specs=specs or [VMEM] * len(ins),
        out_specs=[VMEM] * len(outs),
        scratch_shapes=list(scratch),
        compiler_params=pltpu.CompilerParams(vmem_limit_bytes=min(limit, 60 << 20)),
        cost_estimate=pl.CostEstimate(
            flops=flops, bytes_accessed=nbytes(ins) + nbytes(outs), transcendentals=0
        ),
        name=name,
    )(*ins)


def dot(left, right):
    return jnp.dot(left, right, preferred_element_type=F32)


def dot_rows(left, right):
    return lax.dot_general(left, right, (((1,), (1,)), ((), ())), preferred_element_type=F32)


def pack_kv_kernel(kv, group_ref, *refs):
    out_ref = refs[-1]
    out_ref[0] = refs[0][...]
    for g in range(kv):

        @pl.when(group_ref[0] == g)
        def _():
            cols = pl.ds(g * HD, HD)
            for s in range(1, kv):
                out_ref[s, :, :HD] = refs[2 * s - 1][:, cols]
                out_ref[s, :, HD:] = refs[2 * s][:, cols]


def pack_q_kernel(kv, group_ref, query_ref, grad_ref, *out_refs):
    width = out_refs[0].shape[2]
    for g in range(kv):

        @pl.when(group_ref[0] == g)
        def _():
            for s in range(kv):
                cols = pl.ds((g ^ s) * width, width)
                out_refs[s][0] = query_ref[:, cols]
                out_refs[s][1] = grad_ref[:, cols]


class Plan:
    def __init__(self, kv, block_len, block_rows, rows, group, cores, z_devices, parts):
        self.kv, self.block_len, self.block_rows, self.rows = kv, block_len, block_rows, rows
        self.group, self.cores, self.parts, self.z_part = group, cores, parts, z_devices // parts
        self.blocks = rows // block_rows
        self.tile_rows = block_rows if block_rows % 16 == 0 else rows
        self.lanes = group * self.tile_rows
        self.query_rows = kv * group * rows
        self.part_keys = self.z_part * kv * rows
        self.chunk_keys = parts * self.part_keys
        self.tiles = [(s, start) for s in range(kv) for start in range(0, rows, self.tile_rows)]

    def zone(self, part):
        first = (self.parts - 1 - part) * self.z_part
        return range(first, first + self.z_part)

    def at(self, tile):
        return pl.ds(tile * self.lanes, self.lanes)

    def keys_at(self, i):
        return pl.ds(i * self.chunk_keys, self.chunk_keys)

    def gap(self, tile, info_ref):
        s, start = self.tiles[tile]
        head, ctx = info_ref[0], info_ref[1]
        row = lax.broadcasted_iota(jnp.int32, (1, self.lanes), 1) % self.tile_rows + start
        pos = jnp.zeros((1, self.lanes), jnp.int32)
        for b in range(start // self.block_rows, -(-(start + self.tile_rows) // self.block_rows)):
            first = info_ref[2 + ctx * self.blocks + b] * self.block_len + (head ^ s) * self.block_rows
            pos = jnp.where(row // self.block_rows == b, first + row % self.block_rows, pos)
        return pos - lax.broadcasted_iota(jnp.int32, (self.block_rows, self.lanes), 0)

    def masked(self, scores, gap, chunk, info_ref):
        head, ctx = info_ref[0], info_ref[1]
        a, core = chunk
        for j in range(self.chunk_keys // self.block_rows):
            m, rest = divmod(j, self.kv * self.blocks)
            s, b = divmod(rest, self.blocks)
            stored = (ctx ^ (m * self.cores + core)) * self.blocks + b
            first = info_ref[2 + stored] * self.block_len + (head ^ (a * self.kv + s)) * self.block_rows
            block = scores[j * self.block_rows : (j + 1) * self.block_rows]
            yield j * self.block_rows, jnp.where(gap >= first, block, LOWEST)

    def turn(self, kv_refs, turned_ref):
        for i, ref in enumerate(kv_refs):
            turned_ref[:, self.keys_at(i)] = ref[...].reshape(self.chunk_keys, 2 * HD).T

    def keys(self, ref):
        return ref[:, :, :, :HD].reshape(self.chunk_keys, HD)

    def values(self, ref):
        return ref[:, :, :, HD:].reshape(self.chunk_keys, HD)

    def fold(self, block):
        return block.reshape(block.shape[0] // 8, 8, self.lanes)

    def scores(self, tile, chunks, kv_refs, q, e_ref, cols, info_ref):
        gap = self.gap(tile, info_ref)
        top = jnp.full((8, self.lanes), FLOOR, F32)
        for i, ref in enumerate(kv_refs):
            scores = dot_rows(self.keys(ref), q)
            for row, part in self.masked(scores, gap, chunks[i], info_ref):
                e_ref[pl.ds(i * self.chunk_keys + row, part.shape[0]), cols] = part
                top = jnp.maximum(top, jnp.max(self.fold(part), axis=0))
        return jnp.max(top, axis=0, keepdims=True)

    def exponents(self, count, e_ref, cols, top):
        total = jnp.zeros((8, self.lanes), F32)
        for i in range(count):
            part = jnp.exp2(e_ref[self.keys_at(i), cols] * EXPO - top * EXPO)
            e_ref[self.keys_at(i), cols] = part
            total = total + jnp.sum(self.fold(part), axis=0)
        return jnp.sum(total, axis=0, keepdims=True)

    def store_heads(self, out_ref, tile, turned):
        s, start = self.tiles[tile]
        block = turned.T.astype(BF)
        for n in range(self.group):
            piece = block[n * self.tile_rows : (n + 1) * self.tile_rows]
            out_ref[pl.ds(start, self.tile_rows), pl.ds(n * HD, HD)] = piece

    def back(self, kv_refs, dkv_refs, p_ref, ds_ref, q_ref, do_ref):
        shape = (self.z_part, self.kv, self.rows, HD)
        for i in range(len(kv_refs)):
            for part in range(self.parts):
                at = pl.ds(i * self.chunk_keys + self.zone(part)[0] * self.kv * self.rows, self.part_keys)
                out_ref = dkv_refs[i * self.parts + part]
                out_ref[:, :, :, :HD] = dot(ds_ref[at, :], q_ref[...]).astype(BF).reshape(shape)
                out_ref[:, :, :, HD:] = dot(p_ref[at, :], do_ref[...]).astype(BF).reshape(shape)


def near_kernel(plan, chunks, info_ref, *refs):
    kv, count = plan.kv, len(chunks)
    q_parts, refs = refs[:kv], refs[kv:]
    kv_refs, refs = refs[:count], refs[count:]
    q_all, do_all, e_ref, top_ref, sum_ref, mix_ref, turned_ref = refs
    plan.turn(kv_refs, turned_ref)
    for tile, (s, start) in enumerate(plan.tiles):
        span = pl.ds(start, plan.tile_rows)
        for n in range(plan.group):
            at = pl.ds(tile * plan.lanes + n * plan.tile_rows, plan.tile_rows)
            q_all[at, :] = q_parts[s][0, span, pl.ds(n * HD, HD)]
            do_all[at, :] = q_parts[s][1, span, pl.ds(n * HD, HD)]
    for tile in range(len(plan.tiles)):
        at = plan.at(tile)
        top = plan.scores(tile, chunks, kv_refs, q_all[at, :], e_ref, at, info_ref)
        top_ref[:, at] = top
        sum_ref[:, at] = plan.exponents(count, e_ref, at, top)
        mixed = jnp.zeros((HD, plan.lanes), F32)
        for i in range(count):
            weights = e_ref[plan.keys_at(i), at].astype(BF)
            mixed = mixed + dot(turned_ref[pl.ds(HD, HD), plan.keys_at(i)], weights)
        mix_ref[:, at] = mixed


def far_kernel(plan, chunks, info_ref, q_all, do_all, near_top, near_sum, near_mix, *refs):
    kv, count = plan.kv, len(chunks)
    kv_refs, refs = refs[:count], refs[count:]
    att_refs, refs = refs[:kv], refs[kv:]
    near_scale, delta_ref, q_grad_ref = refs[:3]
    dkv_refs, refs = refs[3 : 3 + count * plan.parts], refs[3 + count * plan.parts :]
    turned_ref, e_ref, p_ref, ds_ref = refs
    here = pl.ds(0, plan.lanes)
    plan.turn(kv_refs, turned_ref)
    for tile, (s, _) in enumerate(plan.tiles):
        at = plan.at(tile)
        top = plan.scores(tile, chunks, kv_refs, q_all[at, :], e_ref, here, info_ref)
        top = jnp.maximum(top, near_top[:, at])
        total = plan.exponents(count, e_ref, here, top)
        factor = jnp.exp2((near_top[:, at] - top) * EXPO)
        inverse = 1.0 / (total + factor * near_sum[:, at])
        near_scale[:, at] = factor * inverse
        mixed = near_mix[:, at] * (factor * inverse)
        for i in range(count):
            probs = (e_ref[plan.keys_at(i), here] * inverse).astype(BF)
            p_ref[plan.keys_at(i), at] = probs
            mixed = mixed + dot(turned_ref[pl.ds(HD, HD), plan.keys_at(i)], probs)
        plan.store_heads(att_refs[s], tile, mixed)
        do = do_all[at, :]
        delta = jnp.sum(do.astype(F32).T * mixed.astype(BF).astype(F32), axis=0, keepdims=True)
        delta_ref[:, at] = delta
        q_grad = jnp.zeros((HD, plan.lanes), F32)
        for i, ref in enumerate(kv_refs):
            probs = e_ref[plan.keys_at(i), here] * inverse
            grad_s = (probs * (dot_rows(plan.values(ref), do) - delta)).astype(BF)
            ds_ref[plan.keys_at(i), at] = grad_s
            q_grad = q_grad + dot(turned_ref[pl.ds(0, HD), plan.keys_at(i)], grad_s)
        q_grad_ref[:, at] = q_grad
    plan.back(kv_refs, dkv_refs, p_ref, ds_ref, q_all, do_all)


def near_back_kernel(plan, chunk, q_all, do_all, e_ref, near_scale, delta_ref, q_grad_in, kv_ref, *refs):
    refs, (turned_ref, p_ref, ds_ref) = refs[:-3], refs[-3:]
    outs, dkv_refs = refs[: -plan.parts], refs[-plan.parts :]
    plan.turn([kv_ref], turned_ref)
    for tile, (s, _) in enumerate(plan.tiles):
        at = plan.at(tile)
        do = do_all[at, :]
        probs = e_ref[plan.keys_at(chunk), at] * near_scale[:, at]
        p_ref[:, at] = probs.astype(BF)
        grad_s = (probs * (dot_rows(plan.values(kv_ref), do) - delta_ref[:, at])).astype(BF)
        ds_ref[:, at] = grad_s
        q_grad = q_grad_in[:, at] + dot(turned_ref[pl.ds(0, HD), :], grad_s)
        if chunk == 0:
            plan.store_heads(outs[s], tile, q_grad * SCALING)
        else:
            outs[0][:, at] = q_grad
    plan.back([kv_ref], dkv_refs, p_ref, ds_ref, q_all, do_all)


def add_kernel(*refs):
    total = refs[0][...].astype(F32)
    for ref in refs[1:-1]:
        total = total + ref[...].astype(F32)
    refs[-1][...] = total.astype(BF)


def sum_heads_kernel(parts, *refs):
    for m_z, out_ref in enumerate(refs[parts:]):
        total = refs[0][m_z].astype(F32)
        for ref in refs[1:parts]:
            total = total + ref[m_z].astype(F32)
        out_ref[...] = total.astype(BF)


def sum_z_kernel(kv, *refs):
    ins, outs = refs[:-kv], refs[-kv:]
    for s, out_ref in enumerate(outs):
        total = ins[0][s].astype(F32)
        for ref in ins[1:]:
            total = total + ref[s].astype(F32)
        out_ref[...] = total.astype(BF)


def finish_kv_kernel(kv, group_ref, *refs):
    key_ref, value_ref = refs[kv:]
    for g in range(kv):

        @pl.when(group_ref[0] == g)
        def _():
            for s in range(kv):
                cols = pl.ds((g ^ s) * HD, HD)
                key_ref[:, cols] = (refs[s][:, :HD].astype(F32) * SCALING).astype(BF)
                value_ref[:, cols] = refs[s][:, HD:]


def finish_q_kernel(kv, group_ref, *refs):
    att_ref, grad_ref = refs[2 * kv :]
    width = refs[0].shape[1]
    for g in range(kv):

        @pl.when(group_ref[0] == g)
        def _():
            for s in range(kv):
                cols = pl.ds((g ^ s) * width, width)
                att_ref[:, cols] = refs[s][...]
                grad_ref[:, cols] = refs[kv + s][...]


def shards(queries, key_vectors, value_vectors, out_grad, block_order):
    heads_devices = lax.axis_size("head")
    ctx_devices = lax.axis_size("ctx")
    halves, block_rows, query_width = queries.shape
    kv = key_vectors.shape[2] // HD
    rows = halves * block_rows
    width = query_width // kv
    cores = CORES if ctx_devices % CORES == 0 else 1
    z_devices = ctx_devices // cores
    spans = heads_devices // kv
    parts = 2 if z_devices % 2 == 0 else 1
    plan = Plan(kv, block_rows * heads_devices, block_rows, rows, width // HD, cores, z_devices, parts)
    z_part = plan.z_part
    head = lax.axis_index("head").astype(jnp.int32)
    place = jnp.stack([head, lax.axis_index("ctx").astype(jnp.int32)])
    info = jnp.concatenate([place, block_order])
    own_group = (head % kv).reshape(1)
    queries = queries.reshape(rows, query_width)
    out_grad = out_grad.reshape(rows, query_width)
    key_vectors = key_vectors.reshape(rows, kv * HD)
    value_vectors = value_vectors.reshape(rows, kv * HD)

    def bf(*dims):
        return jax.ShapeDtypeStruct(dims, BF)

    def f32(*dims):
        return jax.ShapeDtypeStruct(dims, F32)

    def with_swaps(blocks):
        return [blocks[0]] + [swap(blocks[s], "head", s) for s in range(1, kv)]

    key_parts = with_swaps([key_vectors] * kv)[1:]
    value_parts = with_swaps([value_vectors] * kv)[1:]
    mine = (head % kv) * HD
    own = jnp.concatenate(
        [lax.dynamic_slice_in_dim(block, mine, HD, 1) for block in (key_vectors, value_vectors)], axis=1
    )
    q_parts = call(
        functools.partial(pack_q_kernel, kv),
        "pack_q",
        (own_group, queries, out_grad),
        [bf(2, rows, width)] * kv,
        [SMEM, VMEM, VMEM],
    )
    own = after([own], q_parts[1:])[0]
    piece = call(
        functools.partial(pack_kv_kernel, kv),
        "pack_kv",
        (own_group, own, *[part for pair in zip(key_parts, value_parts) for part in pair]),
        [bf(kv, rows, 2 * HD)],
        [SMEM] + [VMEM] * (2 * kv - 1),
    )[0]
    pieces = [swap(piece, "ctx", m * cores) for m in reversed(range(1, z_devices))]
    pieces = [piece] + pieces[::-1]
    q_parts = with_swaps(q_parts)
    column = jnp.stack(pieces)
    columns = [swap(column, "head", a * kv) for a in range(1, spans)]
    near_kv = [column] + [swap(column, "ctx", core) for core in range(1, cores)]
    near_chunks = [(0, core) for core in range(cores)]
    far_chunks = [(a, core) for a in range(1, spans) for core in range(cores)]

    keys = plan.chunk_keys
    near_keys, far_keys = len(near_chunks) * keys, len(far_chunks) * keys
    query_rows = plan.query_rows
    row = f32(1, query_rows)
    dkv = bf(z_part, kv, rows, 2 * HD)
    q_all, do_all, near_e, near_top, near_sum, near_mix = call(
        functools.partial(near_kernel, plan, near_chunks),
        "attend_near",
        (info, *q_parts, *near_kv),
        [bf(query_rows, HD)] * 2 + [f32(near_keys, query_rows), row, row, f32(HD, query_rows)],
        [SMEM] + [VMEM] * (kv + len(near_kv)),
        [pltpu.VMEM((2 * HD, near_keys), BF)],
        near_keys * 4 * HD,
        8 * near_keys * query_rows * HD,
    )
    far_kv = []
    for part in after(columns, [near_top]):
        far_kv += [part] + [swap(part, "ctx", core) for core in range(1, cores)]
    outs = call(
        functools.partial(far_kernel, plan, far_chunks),
        "attend_far",
        (info, q_all, do_all, near_top, near_sum, near_mix, *far_kv),
        [bf(rows, width)] * kv + [row, row, f32(HD, query_rows)] + [dkv] * (parts * len(far_kv)),
        [SMEM] + [VMEM] * (5 + len(far_kv)),
        [
            pltpu.VMEM((2 * HD, far_keys), BF),
            pltpu.VMEM((far_keys, plan.lanes), F32),
            pltpu.VMEM((far_keys, query_rows), BF),
            pltpu.VMEM((far_keys, query_rows), BF),
        ],
        far_keys * (4 * HD + 4 * plan.lanes + 4 * query_rows),
        16 * far_keys * query_rows * HD,
    )
    att_parts, outs = outs[:kv], outs[kv:]
    (near_scale, delta, q_grad), far_dkv = outs[:3], outs[3:]

    sums = [[] for _ in range(parts)]
    for a in range(spans - 1):
        earlier = []
        for p in range(parts):
            ours = [far_dkv[(a * cores + core) * parts + p] for core in range(cores)]
            both = [ours[0]] + [swap(ours[core], "ctx", core) for core in range(1, cores)]
            total = call(add_kernel, "sum_cores", after(both, earlier), [dkv])[0]
            earlier = [total]
            sums[p].append(swap(total, "head", (a + 1) * kv))
    for core in reversed(range(cores)):
        q_outs = [f32(HD, query_rows)] if core else [bf(rows, width)] * kv
        outs = call(
            functools.partial(near_back_kernel, plan, core),
            "attend_near_back",
            (q_all, do_all, near_e, near_scale, delta, q_grad, near_kv[core]),
            q_outs + [dkv] * parts,
            None,
            [
                pltpu.VMEM((2 * HD, keys), BF),
                pltpu.VMEM((keys, query_rows), BF),
                pltpu.VMEM((keys, query_rows), BF),
            ],
            keys * (4 * HD + 4 * query_rows),
            12 * keys * query_rows * HD,
        )
        q_grad = outs[0]
        for p in range(parts):
            part = outs[len(q_outs) + p]
            sums[p].append(swap(part, "ctx", core) if core else part)
    q_grad_parts = outs[:kv]
    z_parts = [None] * z_devices
    for p in range(parts):
        totals = call(
            functools.partial(sum_heads_kernel, len(sums[p])),
            "sum_heads",
            sums[p],
            [bf(kv, rows, 2 * HD)] * z_part,
        )

        for m, total in zip(plan.zone(p), totals):
            z_parts[m] = swap(total, "ctx", m * cores) if m else total
    ordered = [z_parts[m] for p in range(parts) for m in plan.zone(p)]
    pair_parts = call(
        functools.partial(sum_z_kernel, kv), "sum_z", ordered, [bf(rows, 2 * HD)] * kv
    )
    pair_parts = with_swaps(pair_parts)
    attended, query_grad = call(
        functools.partial(finish_q_kernel, kv),
        "finish_q",
        (own_group, *with_swaps(att_parts), *with_swaps(q_grad_parts)),
        [bf(rows, query_width)] * 2,
        [SMEM] + [VMEM] * (2 * kv),
    )
    key_grad, value_grad = call(
        functools.partial(finish_kv_kernel, kv),
        "finish_kv",
        (own_group, *pair_parts),
        [bf(rows, kv * HD)] * 2,
        [SMEM] + [VMEM] * kv,
    )
    return (
        attended.reshape(halves, block_rows, query_width),
        query_grad.reshape(halves, block_rows, query_width),
        key_grad.reshape(halves, block_rows, kv * HD),
        value_grad.reshape(halves, block_rows, kv * HD),
    )


def solution(mesh):
    split = P("ctx", "head", None)
    return jax.shard_map(
        shards,
        mesh=mesh,
        in_specs=(split, split, split, split, P()),
        out_specs=(split, split, split, split),
        check_vma=False,
    )
```

```python
import functools
import math

import jax
import jax.numpy as jnp
from jax import lax
from jax.experimental import pallas as pl
from jax.experimental.pallas import tpu as pltpu
from jax.sharding import PartitionSpec as P

HD = 128
CORES = 2
BF = jnp.bfloat16
F32 = jnp.float32
LOWEST = -1e30
FLOOR = -1e29
SCALING = 1.0 / math.sqrt(HD)
EXPO = SCALING * math.log2(math.e)

VMEM = pl.BlockSpec(memory_space=pltpu.VMEM)
SMEM = pl.BlockSpec(memory_space=pltpu.SMEM)


def swap(block, axis, mask):
    size = lax.axis_size(axis)
    return lax.ppermute(block, axis, [(i, i ^ mask) for i in range(size)])


def nbytes(arrays):
    return sum(math.prod(a.shape) * a.dtype.itemsize for a in arrays)


def after(blocks, earlier):
    if not earlier:
        return tuple(blocks)
    return lax.optimization_barrier((tuple(blocks), tuple(earlier)))[0]


def call(kernel, name, ins, outs, specs=None, scratch=(), extra=0, flops=0):
    limit = nbytes(ins) + nbytes(outs) + extra + (12 << 20)
    return pl.pallas_call(
        kernel,
        out_shape=list(outs),
        in_specs=specs or [VMEM] * len(ins),
        out_specs=[VMEM] * len(outs),
        scratch_shapes=list(scratch),
        compiler_params=pltpu.CompilerParams(vmem_limit_bytes=min(limit, 60 << 20)),
        cost_estimate=pl.CostEstimate(
            flops=flops, bytes_accessed=nbytes(ins) + nbytes(outs), transcendentals=0
        ),
        name=name,
    )(*ins)


def dot(left, right):
    return jnp.dot(left, right, preferred_element_type=F32)


def dot_rows(left, right):
    return lax.dot_general(left, right, (((1,), (1,)), ((), ())), preferred_element_type=F32)


def pack_kv_kernel(kv, group_ref, *refs):
    out_ref = refs[-1]
    out_ref[0] = refs[0][...]
    for g in range(kv):

        @pl.when(group_ref[0] == g)
        def _():
            cols = pl.ds(g * HD, HD)
            for s in range(1, kv):
                out_ref[s, :, :HD] = refs[2 * s - 1][:, cols]
                out_ref[s, :, HD:] = refs[2 * s][:, cols]


def pack_q_kernel(kv, group_ref, query_ref, grad_ref, *out_refs):
    width = out_refs[0].shape[2]
    for g in range(kv):

        @pl.when(group_ref[0] == g)
        def _():
            for s in range(kv):
                cols = pl.ds((g ^ s) * width, width)
                out_refs[s][0] = query_ref[:, cols]
                out_refs[s][1] = grad_ref[:, cols]


class Plan:
    def __init__(self, kv, block_len, block_rows, rows, group, cores, z_devices, parts):
        self.kv, self.block_len, self.block_rows, self.rows = kv, block_len, block_rows, rows
        self.group, self.cores, self.parts, self.z_part = group, cores, parts, z_devices // parts
        self.blocks = rows // block_rows
        self.tile_rows = block_rows if block_rows % 16 == 0 else rows
        self.lanes = group * self.tile_rows
        self.query_rows = kv * group * rows
        self.part_keys = self.z_part * kv * rows
        self.chunk_keys = parts * self.part_keys
        self.tiles = [(s, start) for s in range(kv) for start in range(0, rows, self.tile_rows)]

    def zone(self, part):
        first = (self.parts - 1 - part) * self.z_part
        return range(first, first + self.z_part)

    def at(self, tile):
        return pl.ds(tile * self.lanes, self.lanes)

    def keys_at(self, i):
        return pl.ds(i * self.chunk_keys, self.chunk_keys)

    def gap(self, tile, info_ref):
        s, start = self.tiles[tile]
        head, ctx = info_ref[0], info_ref[1]
        row = lax.broadcasted_iota(jnp.int32, (1, self.lanes), 1) % self.tile_rows + start
        pos = jnp.zeros((1, self.lanes), jnp.int32)
        for b in range(start // self.block_rows, -(-(start + self.tile_rows) // self.block_rows)):
            first = info_ref[2 + ctx * self.blocks + b] * self.block_len + (head ^ s) * self.block_rows
            pos = jnp.where(row // self.block_rows == b, first + row % self.block_rows, pos)
        return pos - lax.broadcasted_iota(jnp.int32, (self.block_rows, self.lanes), 0)

    def masked(self, scores, gap, chunk, info_ref):
        head, ctx = info_ref[0], info_ref[1]
        a, core = chunk
        for j in range(self.chunk_keys // self.block_rows):
            m, rest = divmod(j, self.kv * self.blocks)
            s, b = divmod(rest, self.blocks)
            stored = (ctx ^ (m * self.cores + core)) * self.blocks + b
            first = info_ref[2 + stored] * self.block_len + (head ^ (a * self.kv + s)) * self.block_rows
            block = scores[j * self.block_rows : (j + 1) * self.block_rows]
            yield j * self.block_rows, jnp.where(gap >= first, block, LOWEST)

    def turn(self, kv_refs, turned_ref):
        for i, ref in enumerate(kv_refs):
            turned_ref[:, self.keys_at(i)] = ref[...].reshape(self.chunk_keys, 2 * HD).T

    def keys(self, ref):
        return ref[:, :, :, :HD].reshape(self.chunk_keys, HD)

    def values(self, ref):
        return ref[:, :, :, HD:].reshape(self.chunk_keys, HD)

    def fold(self, block):
        return block.reshape(block.shape[0] // 8, 8, self.lanes)

    def scores(self, tile, chunks, kv_refs, q_t, e_ref, cols, info_ref):
        gap = self.gap(tile, info_ref)
        top = jnp.full((8, self.lanes), FLOOR, F32)
        for i, ref in enumerate(kv_refs):
            scores = dot(self.keys(ref), q_t)
            for row, part in self.masked(scores, gap, chunks[i], info_ref):
                e_ref[pl.ds(i * self.chunk_keys + row, part.shape[0]), cols] = part
                top = jnp.maximum(top, jnp.max(self.fold(part), axis=0))
        return jnp.max(top, axis=0, keepdims=True)

    def exponents(self, count, e_ref, cols, top):
        total = jnp.zeros((8, self.lanes), F32)
        for i in range(count):
            part = jnp.exp2(e_ref[self.keys_at(i), cols] * EXPO - top * EXPO)
            e_ref[self.keys_at(i), cols] = part
            total = total + jnp.sum(self.fold(part), axis=0)
        return jnp.sum(total, axis=0, keepdims=True)

    def store_heads(self, out_ref, tile, turned):
        s, start = self.tiles[tile]
        block = turned.T.astype(BF)
        for n in range(self.group):
            piece = block[n * self.tile_rows : (n + 1) * self.tile_rows]
            out_ref[pl.ds(start, self.tile_rows), pl.ds(n * HD, HD)] = piece

    def back(self, kv_refs, dkv_refs, p_ref, ds_ref, q_ref, do_ref):
        shape = (self.z_part, self.kv, self.rows, HD)
        for i in range(len(kv_refs)):
            for part in range(self.parts):
                at = pl.ds(i * self.chunk_keys + self.zone(part)[0] * self.kv * self.rows, self.part_keys)
                out_ref = dkv_refs[i * self.parts + part]
                out_ref[:, :, :, :HD] = dot(ds_ref[at, :], q_ref[...]).astype(BF).reshape(shape)
                out_ref[:, :, :, HD:] = dot(p_ref[at, :], do_ref[...]).astype(BF).reshape(shape)


def forward_part(plan, chunks, info_ref, q_t, kv_refs, e_ref, top_ref, sum_ref, mix_ref, turned_ref):
    plan.turn(kv_refs, turned_ref)
    for tile in range(len(plan.tiles)):
        at = plan.at(tile)
        top = plan.scores(tile, chunks, kv_refs, q_t[:, at], e_ref, at, info_ref)
        top_ref[:, at] = top
        sum_ref[:, at] = plan.exponents(len(chunks), e_ref, at, top)
        mixed = jnp.zeros((HD, plan.lanes), F32)
        for i in range(len(chunks)):
            weights = e_ref[plan.keys_at(i), at].astype(BF)
            mixed = mixed + dot(turned_ref[pl.ds(HD, HD), plan.keys_at(i)], weights)
        mix_ref[:, at] = mixed


def near_kernel(plan, chunks, info_ref, *refs):
    kv, count = plan.kv, len(chunks)
    q_parts, refs = refs[:kv], refs[kv:]
    kv_refs, refs = refs[:count], refs[count:]
    (q_all, do_all, q_t, do_t), refs = refs[:4], refs[4:]
    for tile, (s, start) in enumerate(plan.tiles):
        span = pl.ds(start, plan.tile_rows)
        for n in range(plan.group):
            at = pl.ds(tile * plan.lanes + n * plan.tile_rows, plan.tile_rows)
            q_all[at, :] = q_parts[s][0, span, pl.ds(n * HD, HD)]
            do_all[at, :] = q_parts[s][1, span, pl.ds(n * HD, HD)]
        at = plan.at(tile)
        q_t[:, at] = q_all[at, :].T
        do_t[:, at] = do_all[at, :].T
    forward_part(plan, chunks, info_ref, q_t, kv_refs, *refs)


def mid_kernel(plan, chunks, info_ref, q_t, *refs):
    forward_part(plan, chunks, info_ref, q_t, refs[: len(chunks)], *refs[len(chunks) :])


def far_kernel(plan, chunks, others, info_ref, q_all, do_all, q_t, do_t, *refs):
    kv, count = plan.kv, len(chunks)
    partial, refs = [refs[3 * i : 3 * i + 3] for i in range(others)], refs[3 * others :]
    kv_refs, refs = refs[:count], refs[count:]
    att_refs, refs = refs[:kv], refs[kv:]
    scale_refs, (delta_ref, q_grad_ref), refs = refs[:others], refs[others : others + 2], refs[others + 2 :]
    dkv_refs, (turned_ref, e_ref, p_ref, ds_ref) = refs[:-4], refs[-4:]
    here = pl.ds(0, plan.lanes)
    plan.turn(kv_refs, turned_ref)
    for tile, (s, _) in enumerate(plan.tiles):
        at = plan.at(tile)
        top = plan.scores(tile, chunks, kv_refs, q_t[:, at], e_ref, here, info_ref)
        for top_ref, _, _ in partial:
            top = jnp.maximum(top, top_ref[:, at])
        total = plan.exponents(count, e_ref, here, top)
        factors = [jnp.exp2((top_ref[:, at] - top) * EXPO) for top_ref, _, _ in partial]
        for factor, (_, sum_ref, _) in zip(factors, partial):
            total = total + factor * sum_ref[:, at]
        inverse = 1.0 / total
        mixed = jnp.zeros((HD, plan.lanes), F32)
        for factor, scale_ref, (_, _, mix_ref) in zip(factors, scale_refs, partial):
            scale_ref[:, at] = factor * inverse
            mixed = mixed + mix_ref[:, at] * (factor * inverse)
        for i in range(count):
            probs = (e_ref[plan.keys_at(i), here] * inverse).astype(BF)
            p_ref[plan.keys_at(i), at] = probs
            mixed = mixed + dot(turned_ref[pl.ds(HD, HD), plan.keys_at(i)], probs)
        mixed = mixed.astype(BF).astype(F32)
        plan.store_heads(att_refs[s], tile, mixed)
        do = do_t[:, at]
        delta = jnp.sum(do.astype(F32) * mixed, axis=0, keepdims=True)
        delta_ref[:, at] = delta
        q_grad = jnp.zeros((HD, plan.lanes), F32)
        for i, ref in enumerate(kv_refs):
            probs = e_ref[plan.keys_at(i), here] * inverse
            grad_s = (probs * (dot(plan.values(ref), do) - delta)).astype(BF)
            ds_ref[plan.keys_at(i), at] = grad_s
            q_grad = q_grad + dot(turned_ref[pl.ds(0, HD), plan.keys_at(i)], grad_s)
        q_grad_ref[:, at] = q_grad
    plan.back(kv_refs, dkv_refs, p_ref, ds_ref, q_all, do_all)


def back_kernel(plan, rows_at, last, order, q_all, do_all, do_t, e_ref, scale_ref, delta_ref, q_grad_in, *refs):
    count = len(rows_at)
    kv_refs, refs = refs[:count], refs[count + order :]
    refs, (turned_ref, p_ref, ds_ref) = refs[:-3], refs[-3:]
    outs, dkv_refs = refs[: -plan.parts * count], refs[-plan.parts * count :]
    plan.turn(kv_refs, turned_ref)
    for tile, (s, _) in enumerate(plan.tiles):
        at = plan.at(tile)
        q_grad = q_grad_in[:, at]
        for i, ref in enumerate(kv_refs):
            probs = e_ref[plan.keys_at(rows_at[i]), at] * scale_ref[:, at]
            p_ref[plan.keys_at(i), at] = probs.astype(BF)
            grad_s = (probs * (dot(plan.values(ref), do_t[:, at]) - delta_ref[:, at])).astype(BF)
            ds_ref[plan.keys_at(i), at] = grad_s
            q_grad = q_grad + dot(turned_ref[pl.ds(0, HD), plan.keys_at(i)], grad_s)
        if last:
            plan.store_heads(outs[s], tile, q_grad * SCALING)
        else:
            outs[0][:, at] = q_grad
    plan.back(kv_refs, dkv_refs, p_ref, ds_ref, q_all, do_all)


def add_kernel(*refs):
    total = refs[0][...].astype(F32)
    for ref in refs[1:-1]:
        total = total + ref[...].astype(F32)
    refs[-1][...] = total.astype(BF)


def sum_heads_kernel(parts, *refs):
    for m_z, out_ref in enumerate(refs[parts:]):
        total = refs[0][m_z].astype(F32)
        for ref in refs[1:parts]:
            total = total + ref[m_z].astype(F32)
        out_ref[...] = total.astype(BF)


def sum_z_kernel(kv, *refs):
    ins, outs = refs[:-kv], refs[-kv:]
    for s, out_ref in enumerate(outs):
        total = ins[0][s].astype(F32)
        for ref in ins[1:]:
            total = total + ref[s].astype(F32)
        out_ref[...] = total.astype(BF)


def finish_kv_kernel(kv, group_ref, *refs):
    key_ref, value_ref = refs[kv:]
    for g in range(kv):

        @pl.when(group_ref[0] == g)
        def _():
            for s in range(kv):
                cols = pl.ds((g ^ s) * HD, HD)
                key_ref[:, cols] = (refs[s][:, :HD].astype(F32) * SCALING).astype(BF)
                value_ref[:, cols] = refs[s][:, HD:]


def finish_q_kernel(kv, group_ref, *refs):
    att_ref, grad_ref = refs[2 * kv :]
    width = refs[0].shape[1]
    for g in range(kv):

        @pl.when(group_ref[0] == g)
        def _():
            for s in range(kv):
                cols = pl.ds((g ^ s) * width, width)
                att_ref[:, cols] = refs[s][...]
                grad_ref[:, cols] = refs[kv + s][...]


def shards(queries, key_vectors, value_vectors, out_grad, block_order):
    heads_devices = lax.axis_size("head")
    ctx_devices = lax.axis_size("ctx")
    halves, block_rows, query_width = queries.shape
    kv = key_vectors.shape[2] // HD
    rows = halves * block_rows
    width = query_width // kv
    cores = CORES if ctx_devices % CORES == 0 else 1
    z_devices = ctx_devices // cores
    spans = heads_devices // kv
    parts = 2 if z_devices % 2 == 0 else 1
    plan = Plan(kv, block_rows * heads_devices, block_rows, rows, width // HD, cores, z_devices, parts)
    z_part = plan.z_part
    head = lax.axis_index("head").astype(jnp.int32)
    place = jnp.stack([head, lax.axis_index("ctx").astype(jnp.int32)])
    info = jnp.concatenate([place, block_order])
    own_group = (head % kv).reshape(1)
    queries = queries.reshape(rows, query_width)
    out_grad = out_grad.reshape(rows, query_width)
    key_vectors = key_vectors.reshape(rows, kv * HD)
    value_vectors = value_vectors.reshape(rows, kv * HD)

    def bf(*dims):
        return jax.ShapeDtypeStruct(dims, BF)

    def f32(*dims):
        return jax.ShapeDtypeStruct(dims, F32)

    def with_swaps(blocks):
        return [blocks[0]] + [swap(blocks[s], "head", s) for s in range(1, kv)]

    key_parts = with_swaps([key_vectors] * kv)[1:]
    value_parts = with_swaps([value_vectors] * kv)[1:]
    mine = (head % kv) * HD
    own = jnp.concatenate(
        [lax.dynamic_slice_in_dim(block, mine, HD, 1) for block in (key_vectors, value_vectors)], axis=1
    )
    q_parts = call(
        functools.partial(pack_q_kernel, kv),
        "pack_q",
        (own_group, queries, out_grad),
        [bf(2, rows, width)] * kv,
        [SMEM, VMEM, VMEM],
    )
    own = after([own], q_parts[1:])[0]
    piece = call(
        functools.partial(pack_kv_kernel, kv),
        "pack_kv",
        (own_group, own, *[part for pair in zip(key_parts, value_parts) for part in pair]),
        [bf(kv, rows, 2 * HD)],
        [SMEM] + [VMEM] * (2 * kv - 1),
    )[0]
    pieces = [swap(piece, "ctx", m * cores) for m in reversed(range(1, z_devices))]
    pieces = [piece] + pieces[::-1]
    q_parts = with_swaps(q_parts)
    column = jnp.stack(pieces)
    columns = [swap(column, "head", a * kv) for a in range(1, spans)]
    near_kv = [column] + [swap(column, "ctx", core) for core in range(1, cores)]
    near_chunks = [(0, core) for core in range(cores)]
    mid_chunks = [(a, 0) for a in range(1, spans)]
    far_chunks = [(a, core) for a in range(1, spans) for core in range(1, cores)]

    keys = plan.chunk_keys
    query_rows = plan.query_rows
    row, column_out = f32(1, query_rows), f32(HD, query_rows)
    dkv = bf(z_part, kv, rows, 2 * HD)

    def part_outs(chunks):
        return [f32(len(chunks) * keys, query_rows), row, row, column_out]

    q_all, do_all, q_t, do_t, near_e, *near = call(
        functools.partial(near_kernel, plan, near_chunks),
        "attend_near",
        (info, *q_parts, *near_kv),
        [bf(query_rows, HD)] * 2 + [bf(HD, query_rows)] * 2 + part_outs(near_chunks),
        [SMEM] + [VMEM] * (kv + len(near_kv)),
        [pltpu.VMEM((2 * HD, cores * keys), BF)],
        cores * keys * 4 * HD,
        8 * cores * keys * query_rows * HD,
    )
    mid_kv = after(columns, [near[0]])
    far_kv = [swap(part, "ctx", core) for part in mid_kv for core in range(1, cores)]
    mid_e, *mid = call(
        functools.partial(mid_kernel, plan, mid_chunks),
        "attend_mid",
        (info, q_t, *mid_kv),
        part_outs(mid_chunks),
        [SMEM] + [VMEM] * (1 + len(mid_kv)),
        [pltpu.VMEM((2 * HD, len(mid_kv) * keys), BF)],
        len(mid_kv) * keys * 4 * HD,
        8 * len(mid_kv) * keys * query_rows * HD,
    )
    far_keys = len(far_kv) * keys
    outs = call(
        functools.partial(far_kernel, plan, far_chunks, 2),
        "attend_far",
        (info, q_all, do_all, q_t, do_t, *near, *mid, *far_kv),
        [bf(rows, width)] * kv + [row, row, row, column_out] + [dkv] * (parts * len(far_kv)),
        [SMEM] + [VMEM] * (10 + len(far_kv)),
        [
            pltpu.VMEM((2 * HD, far_keys), BF),
            pltpu.VMEM((far_keys, plan.lanes), F32),
            pltpu.VMEM((far_keys, query_rows), BF),
            pltpu.VMEM((far_keys, query_rows), BF),
        ],
        far_keys * (4 * HD + 4 * plan.lanes + 4 * query_rows),
        16 * far_keys * query_rows * HD,
    )
    att_parts, outs = outs[:kv], outs[kv:]
    (near_scale, mid_scale, delta, q_grad), far_dkv = outs[:4], outs[4:]

    def back(rows_at, last, e, scale, q_grad, kv_refs, order):
        count = len(rows_at)
        q_outs = [bf(rows, width)] * kv if last else [column_out]
        outs = call(
            functools.partial(back_kernel, plan, rows_at, last, len(order)),
            "attend_back",
            (q_all, do_all, do_t, e, scale, delta, q_grad, *kv_refs, *order),
            q_outs + [dkv] * (parts * count),
            None,
            [
                pltpu.VMEM((2 * HD, count * keys), BF),
                pltpu.VMEM((count * keys, query_rows), BF),
                pltpu.VMEM((count * keys, query_rows), BF),
            ],
            count * keys * (4 * HD + 4 * query_rows),
            12 * count * keys * query_rows * HD,
        )
        return outs[: len(q_outs)], outs[len(q_outs) :]

    (q_grad,), mid_dkv = back(list(range(spans - 1)), False, mid_e, mid_scale, q_grad, mid_kv, [])
    sums = [[] for _ in range(parts)]
    totals = []
    for a in range(spans - 1):
        for p in reversed(range(parts)):
            both = [mid_dkv[a * parts + p]]
            for core in range(1, cores):
                ours = far_dkv[(a * (cores - 1) + core - 1) * parts + p]
                both.append(swap(ours, "ctx", core))
            totals += call(add_kernel, "sum_cores", after(both, totals[-1:]), [dkv])
            sums[p].append(swap(totals[-1], "head", (a + 1) * kv))
    order = [swap(totals[-1][0, 0, :, :HD], "ctx", 1)] if cores > 1 else []
    for core in reversed(range(cores)):
        outs, parts_dkv = back([core], core == 0, near_e, near_scale, q_grad, [near_kv[core]], order)
        q_grad = outs[0]
        for p in range(parts):
            sums[p].append(swap(parts_dkv[p], "ctx", core) if core else parts_dkv[p])
    q_grad_parts = outs[:kv]
    z_parts = [None] * z_devices
    for p in range(parts):
        totals = call(
            functools.partial(sum_heads_kernel, len(sums[p])),
            "sum_heads",
            sums[p],
            [bf(kv, rows, 2 * HD)] * z_part,
        )

        for m, total in zip(plan.zone(p), totals):
            z_parts[m] = swap(total, "ctx", m * cores) if m else total
    ordered = [z_parts[m] for p in range(parts) for m in plan.zone(p)]
    pair_parts = call(
        functools.partial(sum_z_kernel, kv), "sum_z", ordered, [bf(rows, 2 * HD)] * kv
    )
    pair_parts = with_swaps(pair_parts)
    attended, query_grad = call(
        functools.partial(finish_q_kernel, kv),
        "finish_q",
        (own_group, *with_swaps(att_parts), *with_swaps(q_grad_parts)),
        [bf(rows, query_width)] * 2,
        [SMEM] + [VMEM] * (2 * kv),
    )
    key_grad, value_grad = call(
        functools.partial(finish_kv_kernel, kv),
        "finish_kv",
        (own_group, *pair_parts),
        [bf(rows, kv * HD)] * 2,
        [SMEM] + [VMEM] * kv,
    )
    return (
        attended.reshape(halves, block_rows, query_width),
        query_grad.reshape(halves, block_rows, query_width),
        key_grad.reshape(halves, block_rows, kv * HD),
        value_grad.reshape(halves, block_rows, kv * HD),
    )


def solution(mesh):
    split = P("ctx", "head", None)
    return jax.shard_map(
        shards,
        mesh=mesh,
        in_specs=(split, split, split, split, P()),
        out_specs=(split, split, split, split),
        check_vma=False,
    )
```

```python
import functools
import math

import jax
import jax.numpy as jnp
from jax import lax
from jax.experimental import pallas as pl
from jax.experimental.pallas import tpu as pltpu
from jax.sharding import PartitionSpec as P

HD = 128
CORES = 2
BF = jnp.bfloat16
F32 = jnp.float32
LOWEST = -1e30
FLOOR = -1e29
SCALING = 1.0 / math.sqrt(HD)
EXPO = SCALING * math.log2(math.e)

VMEM = pl.BlockSpec(memory_space=pltpu.VMEM)
SMEM = pl.BlockSpec(memory_space=pltpu.SMEM)


def swap(block, axis, mask):
    size = lax.axis_size(axis)
    return lax.ppermute(block, axis, [(i, i ^ mask) for i in range(size)])


def nbytes(arrays):
    return sum(math.prod(a.shape) * a.dtype.itemsize for a in arrays)


def after(blocks, earlier):
    if not earlier:
        return tuple(blocks)
    return lax.optimization_barrier((tuple(blocks), tuple(earlier)))[0]


def call(kernel, name, ins, outs, specs=None, scratch=(), extra=0, flops=0):
    limit = nbytes(ins) + nbytes(outs) + extra + (12 << 20)
    return pl.pallas_call(
        kernel,
        out_shape=list(outs),
        in_specs=specs or [VMEM] * len(ins),
        out_specs=[VMEM] * len(outs),
        scratch_shapes=list(scratch),
        compiler_params=pltpu.CompilerParams(vmem_limit_bytes=min(limit, 60 << 20)),
        cost_estimate=pl.CostEstimate(
            flops=flops, bytes_accessed=nbytes(ins) + nbytes(outs), transcendentals=0
        ),
        name=name,
    )(*ins)


def dot(left, right):
    return jnp.dot(left, right, preferred_element_type=F32)


def dot_rows(left, right):
    return lax.dot_general(left, right, (((1,), (1,)), ((), ())), preferred_element_type=F32)


def pack_kv_kernel(kv, group_ref, *refs):
    out_ref = refs[-1]
    out_ref[0] = refs[0][...]
    for g in range(kv):

        @pl.when(group_ref[0] == g)
        def _():
            cols = pl.ds(g * HD, HD)
            for s in range(1, kv):
                out_ref[s, :, :HD] = refs[2 * s - 1][:, cols]
                out_ref[s, :, HD:] = refs[2 * s][:, cols]


def pack_q_kernel(kv, group_ref, query_ref, grad_ref, *out_refs):
    width = out_refs[0].shape[2]
    for g in range(kv):

        @pl.when(group_ref[0] == g)
        def _():
            for s in range(kv):
                cols = pl.ds((g ^ s) * width, width)
                out_refs[s][0] = query_ref[:, cols]
                out_refs[s][1] = grad_ref[:, cols]


class Plan:
    def __init__(self, kv, block_len, block_rows, rows, group, cores, z_devices, parts):
        self.kv, self.block_len, self.block_rows, self.rows = kv, block_len, block_rows, rows
        self.group, self.cores, self.parts, self.z_part = group, cores, parts, z_devices // parts
        self.blocks = rows // block_rows
        self.tile_rows = block_rows if block_rows % 16 == 0 else rows
        self.lanes = group * self.tile_rows
        self.query_rows = kv * group * rows
        self.part_keys = self.z_part * kv * rows
        self.chunk_keys = parts * self.part_keys
        self.tiles = [(s, start) for s in range(kv) for start in range(0, rows, self.tile_rows)]

    def zone(self, part):
        first = (self.parts - 1 - part) * self.z_part
        return range(first, first + self.z_part)

    def at(self, tile):
        return pl.ds(tile * self.lanes, self.lanes)

    def keys_at(self, i):
        return pl.ds(i * self.chunk_keys, self.chunk_keys)

    def gap(self, tile, info_ref):
        s, start = self.tiles[tile]
        head, ctx = info_ref[0], info_ref[1]
        row = lax.broadcasted_iota(jnp.int32, (1, self.lanes), 1) % self.tile_rows + start
        pos = jnp.zeros((1, self.lanes), jnp.int32)
        for b in range(start // self.block_rows, -(-(start + self.tile_rows) // self.block_rows)):
            first = info_ref[2 + ctx * self.blocks + b] * self.block_len + (head ^ s) * self.block_rows
            pos = jnp.where(row // self.block_rows == b, first + row % self.block_rows, pos)
        return pos - lax.broadcasted_iota(jnp.int32, (self.block_rows, self.lanes), 0)

    def masked(self, scores, gap, chunk, info_ref):
        head, ctx = info_ref[0], info_ref[1]
        a, core = chunk
        for j in range(self.chunk_keys // self.block_rows):
            m, rest = divmod(j, self.kv * self.blocks)
            s, b = divmod(rest, self.blocks)
            stored = (ctx ^ (m * self.cores + core)) * self.blocks + b
            first = info_ref[2 + stored] * self.block_len + (head ^ (a * self.kv + s)) * self.block_rows
            block = scores[j * self.block_rows : (j + 1) * self.block_rows]
            yield j * self.block_rows, jnp.where(gap >= first, block, LOWEST)

    def turn(self, kv_refs, turned_ref):
        for i, ref in enumerate(kv_refs):
            turned_ref[:, self.keys_at(i)] = ref[...].reshape(self.chunk_keys, 2 * HD).T

    def keys(self, ref):
        return ref[:, :, :, :HD].reshape(self.chunk_keys, HD)

    def values(self, ref):
        return ref[:, :, :, HD:].reshape(self.chunk_keys, HD)

    def fold(self, block):
        return block.reshape(block.shape[0] // 8, 8, self.lanes)

    def scores(self, tile, chunks, kv_refs, q_t, e_ref, cols, info_ref):
        gap = self.gap(tile, info_ref)
        top = jnp.full((8, self.lanes), FLOOR, F32)
        for i, ref in enumerate(kv_refs):
            scores = dot(self.keys(ref), q_t)
            for row, part in self.masked(scores, gap, chunks[i], info_ref):
                e_ref[pl.ds(i * self.chunk_keys + row, part.shape[0]), cols] = part
                top = jnp.maximum(top, jnp.max(self.fold(part), axis=0))
        return jnp.max(top, axis=0, keepdims=True)

    def exponents(self, count, e_ref, cols, top):
        total = jnp.zeros((8, self.lanes), F32)
        for i in range(count):
            part = jnp.exp2(e_ref[self.keys_at(i), cols] * EXPO - top * EXPO)
            e_ref[self.keys_at(i), cols] = part
            total = total + jnp.sum(self.fold(part), axis=0)
        return jnp.sum(total, axis=0, keepdims=True)

    def store_heads(self, out_ref, tile, turned):
        s, start = self.tiles[tile]
        block = turned.T.astype(BF)
        for n in range(self.group):
            piece = block[n * self.tile_rows : (n + 1) * self.tile_rows]
            out_ref[pl.ds(start, self.tile_rows), pl.ds(n * HD, HD)] = piece

    def back(self, kv_refs, dkv_refs, p_ref, ds_ref, q_ref, do_ref):
        shape = (self.z_part, self.kv, self.rows, HD)
        for i in range(len(kv_refs)):
            for part in range(self.parts):
                at = pl.ds(i * self.chunk_keys + self.zone(part)[0] * self.kv * self.rows, self.part_keys)
                out_ref = dkv_refs[i * self.parts + part]
                out_ref[:, :, :, :HD] = dot(ds_ref[at, :], q_ref[...]).astype(BF).reshape(shape)
                out_ref[:, :, :, HD:] = dot(p_ref[at, :], do_ref[...]).astype(BF).reshape(shape)


def forward_part(plan, chunks, info_ref, q_t, kv_refs, e_ref, top_ref, sum_ref, mix_ref, turned_ref):
    spans = [plan.at(tile) for tile in range(len(plan.tiles))]
    tops = [
        plan.scores(tile, chunks, kv_refs, q_t[:, at], e_ref, at, info_ref)
        for tile, at in enumerate(spans)
    ]
    plan.turn(kv_refs, turned_ref)
    for at, top in zip(spans, tops):
        top_ref[:, at] = top
        sum_ref[:, at] = plan.exponents(len(chunks), e_ref, at, top)
    for at in spans:
        mixed = jnp.zeros((HD, plan.lanes), F32)
        for i in range(len(chunks)):
            weights = e_ref[plan.keys_at(i), at].astype(BF)
            mixed = mixed + dot(turned_ref[pl.ds(HD, HD), plan.keys_at(i)], weights)
        mix_ref[:, at] = mixed


def near_kernel(plan, chunks, info_ref, *refs):
    kv, count = plan.kv, len(chunks)
    q_parts, refs = refs[:kv], refs[kv:]
    kv_refs, refs = refs[:count], refs[count:]
    (q_all, do_all, q_t, do_t), refs = refs[:4], refs[4:]
    for tile, (s, start) in enumerate(plan.tiles):
        span = pl.ds(start, plan.tile_rows)
        for n in range(plan.group):
            at = pl.ds(tile * plan.lanes + n * plan.tile_rows, plan.tile_rows)
            q_all[at, :] = q_parts[s][0, span, pl.ds(n * HD, HD)]
            do_all[at, :] = q_parts[s][1, span, pl.ds(n * HD, HD)]
        at = plan.at(tile)
        q_t[:, at] = q_all[at, :].T
        do_t[:, at] = do_all[at, :].T
    forward_part(plan, chunks, info_ref, q_t, kv_refs, *refs)


def mid_kernel(plan, chunks, info_ref, q_t, *refs):
    forward_part(plan, chunks, info_ref, q_t, refs[: len(chunks)], *refs[len(chunks) :])


def far_kernel(plan, chunks, others, info_ref, q_all, do_all, q_t, do_t, *refs):
    kv, count = plan.kv, len(chunks)
    partial, refs = [refs[3 * i : 3 * i + 3] for i in range(others)], refs[3 * others :]
    kv_refs, refs = refs[:count], refs[count:]
    att_refs, refs = refs[:kv], refs[kv:]
    scale_refs, (delta_ref, q_grad_ref), refs = refs[:others], refs[others : others + 2], refs[others + 2 :]
    dkv_refs, (turned_ref, e_ref, w_ref, p_ref, ds_ref) = refs[:-5], refs[-5:]
    spans = [plan.at(tile) for tile in range(len(plan.tiles))]
    tops = [
        plan.scores(tile, chunks, kv_refs, q_t[:, at], e_ref, at, info_ref)
        for tile, at in enumerate(spans)
    ]
    plan.turn(kv_refs, turned_ref)
    for at in spans:
        for i, ref in enumerate(kv_refs):
            w_ref[plan.keys_at(i), at] = dot(plan.values(ref), do_t[:, at])
    inverses, mixes = [], []
    for at, top in zip(spans, tops):
        for top_ref, _, _ in partial:
            top = jnp.maximum(top, top_ref[:, at])
        total = plan.exponents(count, e_ref, at, top)
        factors = [jnp.exp2((top_ref[:, at] - top) * EXPO) for top_ref, _, _ in partial]
        for factor, (_, sum_ref, _) in zip(factors, partial):
            total = total + factor * sum_ref[:, at]
        inverse = 1.0 / total
        for factor, scale_ref in zip(factors, scale_refs):
            scale_ref[:, at] = factor * inverse
        inverses.append(inverse)
    for at, inverse in zip(spans, inverses):
        mixed = jnp.zeros((HD, plan.lanes), F32)
        for scale_ref, (_, _, mix_ref) in zip(scale_refs, partial):
            mixed = mixed + mix_ref[:, at] * scale_ref[:, at]
        for i in range(count):
            probs = (e_ref[plan.keys_at(i), at] * inverse).astype(BF)
            p_ref[plan.keys_at(i), at] = probs
            mixed = mixed + dot(turned_ref[pl.ds(HD, HD), plan.keys_at(i)], probs)
        mixes.append(mixed.astype(BF).astype(F32))
    for at, mixed in zip(spans, mixes):
        delta_ref[:, at] = jnp.sum(do_t[:, at].astype(F32) * mixed, axis=0, keepdims=True)
    for at, inverse in zip(spans, inverses):
        q_grad = jnp.zeros((HD, plan.lanes), F32)
        for i in range(count):
            probs = e_ref[plan.keys_at(i), at] * inverse
            grad_s = (probs * (w_ref[plan.keys_at(i), at] - delta_ref[:, at])).astype(BF)
            ds_ref[plan.keys_at(i), at] = grad_s
            q_grad = q_grad + dot(turned_ref[pl.ds(0, HD), plan.keys_at(i)], grad_s)
        q_grad_ref[:, at] = q_grad
    plan.back(kv_refs, dkv_refs, p_ref, ds_ref, q_all, do_all)
    for tile, mixed in enumerate(mixes):
        plan.store_heads(att_refs[plan.tiles[tile][0]], tile, mixed)


def back_kernel(plan, rows_at, last, order, q_all, do_all, do_t, e_ref, scale_ref, delta_ref, q_grad_in, *refs):
    count = len(rows_at)
    kv_refs, refs = refs[:count], refs[count + order :]
    refs, (turned_ref, p_ref, ds_ref) = refs[:-3], refs[-3:]
    outs, dkv_refs = refs[: -plan.parts * count], refs[-plan.parts * count :]
    spans = [plan.at(tile) for tile in range(len(plan.tiles))]
    for at in spans:
        for i, ref in enumerate(kv_refs):
            probs = e_ref[plan.keys_at(rows_at[i]), at] * scale_ref[:, at]
            p_ref[plan.keys_at(i), at] = probs.astype(BF)
            grad_s = (probs * (dot(plan.values(ref), do_t[:, at]) - delta_ref[:, at])).astype(BF)
            ds_ref[plan.keys_at(i), at] = grad_s
    plan.turn(kv_refs, turned_ref)
    plan.back(kv_refs, dkv_refs, p_ref, ds_ref, q_all, do_all)
    for tile, at in enumerate(spans):
        q_grad = q_grad_in[:, at]
        for i in range(count):
            q_grad = q_grad + dot(turned_ref[pl.ds(0, HD), plan.keys_at(i)], ds_ref[plan.keys_at(i), at])
        if last:
            plan.store_heads(outs[plan.tiles[tile][0]], tile, q_grad * SCALING)
        else:
            outs[0][:, at] = q_grad


def add_kernel(*refs):
    total = refs[0][...].astype(F32)
    for ref in refs[1:-1]:
        total = total + ref[...].astype(F32)
    refs[-1][...] = total.astype(BF)


def sum_heads_kernel(parts, *refs):
    for m_z, out_ref in enumerate(refs[parts:]):
        total = refs[0][m_z].astype(F32)
        for ref in refs[1:parts]:
            total = total + ref[m_z].astype(F32)
        out_ref[...] = total.astype(BF)


def sum_z_kernel(kv, *refs):
    ins, outs = refs[:-kv], refs[-kv:]
    for s, out_ref in enumerate(outs):
        total = ins[0][s].astype(F32)
        for ref in ins[1:]:
            total = total + ref[s].astype(F32)
        out_ref[...] = total.astype(BF)


def finish_kv_kernel(kv, group_ref, *refs):
    key_ref, value_ref = refs[kv:]
    for g in range(kv):

        @pl.when(group_ref[0] == g)
        def _():
            for s in range(kv):
                cols = pl.ds((g ^ s) * HD, HD)
                key_ref[:, cols] = (refs[s][:, :HD].astype(F32) * SCALING).astype(BF)
                value_ref[:, cols] = refs[s][:, HD:]


def finish_q_kernel(kv, group_ref, *refs):
    att_ref, grad_ref = refs[2 * kv :]
    width = refs[0].shape[1]
    for g in range(kv):

        @pl.when(group_ref[0] == g)
        def _():
            for s in range(kv):
                cols = pl.ds((g ^ s) * width, width)
                att_ref[:, cols] = refs[s][...]
                grad_ref[:, cols] = refs[kv + s][...]


def shards(queries, key_vectors, value_vectors, out_grad, block_order):
    heads_devices = lax.axis_size("head")
    ctx_devices = lax.axis_size("ctx")
    halves, block_rows, query_width = queries.shape
    kv = key_vectors.shape[2] // HD
    rows = halves * block_rows
    width = query_width // kv
    cores = CORES if ctx_devices % CORES == 0 else 1
    z_devices = ctx_devices // cores
    spans = heads_devices // kv
    parts = 2 if z_devices % 2 == 0 else 1
    plan = Plan(kv, block_rows * heads_devices, block_rows, rows, width // HD, cores, z_devices, parts)
    z_part = plan.z_part
    head = lax.axis_index("head").astype(jnp.int32)
    place = jnp.stack([head, lax.axis_index("ctx").astype(jnp.int32)])
    info = jnp.concatenate([place, block_order])
    own_group = (head % kv).reshape(1)
    queries = queries.reshape(rows, query_width)
    out_grad = out_grad.reshape(rows, query_width)
    key_vectors = key_vectors.reshape(rows, kv * HD)
    value_vectors = value_vectors.reshape(rows, kv * HD)

    def bf(*dims):
        return jax.ShapeDtypeStruct(dims, BF)

    def f32(*dims):
        return jax.ShapeDtypeStruct(dims, F32)

    def with_swaps(blocks):
        return [blocks[0]] + [swap(blocks[s], "head", s) for s in range(1, kv)]

    key_parts = with_swaps([key_vectors] * kv)[1:]
    value_parts = with_swaps([value_vectors] * kv)[1:]
    mine = (head % kv) * HD
    own = jnp.concatenate(
        [lax.dynamic_slice_in_dim(block, mine, HD, 1) for block in (key_vectors, value_vectors)], axis=1
    )
    q_parts = call(
        functools.partial(pack_q_kernel, kv),
        "pack_q",
        (own_group, queries, out_grad),
        [bf(2, rows, width)] * kv,
        [SMEM, VMEM, VMEM],
    )
    own = after([own], q_parts[1:])[0]
    piece = call(
        functools.partial(pack_kv_kernel, kv),
        "pack_kv",
        (own_group, own, *[part for pair in zip(key_parts, value_parts) for part in pair]),
        [bf(kv, rows, 2 * HD)],
        [SMEM] + [VMEM] * (2 * kv - 1),
    )[0]
    pieces = [swap(piece, "ctx", m * cores) for m in reversed(range(1, z_devices))]
    pieces = [piece] + pieces[::-1]
    q_parts = with_swaps(q_parts)
    column = jnp.stack(pieces)
    columns = [swap(column, "head", a * kv) for a in range(1, spans)]
    near_kv = [column] + [swap(column, "ctx", core) for core in range(1, cores)]
    near_chunks = [(0, core) for core in range(cores)]
    mid_chunks = [(a, 0) for a in range(1, spans)]
    far_chunks = [(a, core) for a in range(1, spans) for core in range(1, cores)]

    keys = plan.chunk_keys
    query_rows = plan.query_rows
    row, column_out = f32(1, query_rows), f32(HD, query_rows)
    dkv = bf(z_part, kv, rows, 2 * HD)

    def part_outs(chunks):
        return [f32(len(chunks) * keys, query_rows), row, row, column_out]

    q_all, do_all, q_t, do_t, near_e, *near = call(
        functools.partial(near_kernel, plan, near_chunks),
        "attend_near",
        (info, *q_parts, *near_kv),
        [bf(query_rows, HD)] * 2 + [bf(HD, query_rows)] * 2 + part_outs(near_chunks),
        [SMEM] + [VMEM] * (kv + len(near_kv)),
        [pltpu.VMEM((2 * HD, cores * keys), BF)],
        cores * keys * 4 * HD,
        8 * cores * keys * query_rows * HD,
    )
    mid_kv = after(columns, [near[0]])
    far_kv = [swap(part, "ctx", core) for part in mid_kv for core in range(1, cores)]
    mid_e, *mid = call(
        functools.partial(mid_kernel, plan, mid_chunks),
        "attend_mid",
        (info, q_t, *mid_kv),
        part_outs(mid_chunks),
        [SMEM] + [VMEM] * (1 + len(mid_kv)),
        [pltpu.VMEM((2 * HD, len(mid_kv) * keys), BF)],
        len(mid_kv) * keys * 4 * HD,
        8 * len(mid_kv) * keys * query_rows * HD,
    )
    far_keys = len(far_kv) * keys
    outs = call(
        functools.partial(far_kernel, plan, far_chunks, 2),
        "attend_far",
        (info, q_all, do_all, q_t, do_t, *near, *mid, *far_kv),
        [bf(rows, width)] * kv + [row, row, row, column_out] + [dkv] * (parts * len(far_kv)),
        [SMEM] + [VMEM] * (10 + len(far_kv)),
        [
            pltpu.VMEM((2 * HD, far_keys), BF),
            pltpu.VMEM((far_keys, query_rows), F32),
            pltpu.VMEM((far_keys, query_rows), F32),
            pltpu.VMEM((far_keys, query_rows), BF),
            pltpu.VMEM((far_keys, query_rows), BF),
        ],
        far_keys * (4 * HD + 12 * query_rows),
        16 * far_keys * query_rows * HD,
    )
    att_parts, outs = outs[:kv], outs[kv:]
    (near_scale, mid_scale, delta, q_grad), far_dkv = outs[:4], outs[4:]

    def back(rows_at, last, e, scale, q_grad, kv_refs, order):
        count = len(rows_at)
        q_outs = [bf(rows, width)] * kv if last else [column_out]
        outs = call(
            functools.partial(back_kernel, plan, rows_at, last, len(order)),
            "attend_back",
            (q_all, do_all, do_t, e, scale, delta, q_grad, *kv_refs, *order),
            q_outs + [dkv] * (parts * count),
            None,
            [
                pltpu.VMEM((2 * HD, count * keys), BF),
                pltpu.VMEM((count * keys, query_rows), BF),
                pltpu.VMEM((count * keys, query_rows), BF),
            ],
            count * keys * (4 * HD + 4 * query_rows),
            12 * count * keys * query_rows * HD,
        )
        return outs[: len(q_outs)], outs[len(q_outs) :]

    (q_grad,), mid_dkv = back(list(range(spans - 1)), False, mid_e, mid_scale, q_grad, mid_kv, [])
    sums = [[] for _ in range(parts)]
    totals = []
    for a in range(spans - 1):
        for p in reversed(range(parts)):
            both = [mid_dkv[a * parts + p]]
            for core in range(1, cores):
                ours = far_dkv[(a * (cores - 1) + core - 1) * parts + p]
                both.append(swap(ours, "ctx", core))
            totals += call(add_kernel, "sum_cores", after(both, totals[-1:]), [dkv])
            sums[p].append(swap(totals[-1], "head", (a + 1) * kv))
    order = [swap(totals[-1][0, 0, :, :HD], "ctx", 1)] if cores > 1 else []
    for core in reversed(range(cores)):
        outs, parts_dkv = back([core], core == 0, near_e, near_scale, q_grad, [near_kv[core]], order)
        q_grad = outs[0]
        for p in range(parts):
            sums[p].append(swap(parts_dkv[p], "ctx", core) if core else parts_dkv[p])
    q_grad_parts = outs[:kv]
    z_parts = [None] * z_devices
    for p in range(parts):
        totals = call(
            functools.partial(sum_heads_kernel, len(sums[p])),
            "sum_heads",
            sums[p],
            [bf(kv, rows, 2 * HD)] * z_part,
        )

        for m, total in zip(plan.zone(p), totals):
            z_parts[m] = swap(total, "ctx", m * cores) if m else total
    ordered = [z_parts[m] for p in range(parts) for m in plan.zone(p)]
    pair_parts = call(
        functools.partial(sum_z_kernel, kv), "sum_z", ordered, [bf(rows, 2 * HD)] * kv
    )
    pair_parts = with_swaps(pair_parts)
    attended, query_grad = call(
        functools.partial(finish_q_kernel, kv),
        "finish_q",
        (own_group, *with_swaps(att_parts), *with_swaps(q_grad_parts)),
        [bf(rows, query_width)] * 2,
        [SMEM] + [VMEM] * (2 * kv),
    )
    key_grad, value_grad = call(
        functools.partial(finish_kv_kernel, kv),
        "finish_kv",
        (own_group, *pair_parts),
        [bf(rows, kv * HD)] * 2,
        [SMEM] + [VMEM] * kv,
    )
    return (
        attended.reshape(halves, block_rows, query_width),
        query_grad.reshape(halves, block_rows, query_width),
        key_grad.reshape(halves, block_rows, kv * HD),
        value_grad.reshape(halves, block_rows, kv * HD),
    )


def solution(mesh):
    split = P("ctx", "head", None)
    return jax.shard_map(
        shards,
        mesh=mesh,
        in_specs=(split, split, split, split, P()),
        out_specs=(split, split, split, split),
        check_vma=False,
    )
```

```python
import functools
import math

import jax
import jax.numpy as jnp
from jax import lax
from jax.experimental import pallas as pl
from jax.experimental.pallas import tpu as pltpu
from jax.sharding import PartitionSpec as P

HD = 128
CORES = 2
BF = jnp.bfloat16
F32 = jnp.float32
LOWEST = -1e30
FLOOR = -1e29
SCALING = 1.0 / math.sqrt(HD)
EXPO = SCALING * math.log2(math.e)

VMEM = pl.BlockSpec(memory_space=pltpu.VMEM)
SMEM = pl.BlockSpec(memory_space=pltpu.SMEM)


def swap(block, axis, mask):
    size = lax.axis_size(axis)
    return lax.ppermute(block, axis, [(i, i ^ mask) for i in range(size)])


def nbytes(arrays):
    return sum(math.prod(a.shape) * a.dtype.itemsize for a in arrays)


def after(blocks, earlier):
    if not earlier:
        return tuple(blocks)
    return lax.optimization_barrier((tuple(blocks), tuple(earlier)))[0]


def call(kernel, name, ins, outs, specs=None, scratch=(), extra=0, flops=0):
    limit = nbytes(ins) + nbytes(outs) + extra + (12 << 20)
    return pl.pallas_call(
        kernel,
        out_shape=list(outs),
        in_specs=specs or [VMEM] * len(ins),
        out_specs=[VMEM] * len(outs),
        scratch_shapes=list(scratch),
        compiler_params=pltpu.CompilerParams(vmem_limit_bytes=min(limit, 60 << 20)),
        cost_estimate=pl.CostEstimate(
            flops=flops, bytes_accessed=nbytes(ins) + nbytes(outs), transcendentals=0
        ),
        name=name,
    )(*ins)


def dot(left, right):
    return jnp.dot(left, right, preferred_element_type=F32)


def dot_rows(left, right):
    return lax.dot_general(left, right, (((1,), (1,)), ((), ())), preferred_element_type=F32)


def pack_kv_kernel(kv, group_ref, *refs):
    out_ref = refs[-1]
    out_ref[0] = refs[0][...]
    for g in range(kv):

        @pl.when(group_ref[0] == g)
        def _():
            cols = pl.ds(g * HD, HD)
            for s in range(1, kv):
                out_ref[s, :, :HD] = refs[2 * s - 1][:, cols]
                out_ref[s, :, HD:] = refs[2 * s][:, cols]


def pack_q_kernel(kv, group_ref, query_ref, grad_ref, *out_refs):
    width = out_refs[0].shape[2]
    for g in range(kv):

        @pl.when(group_ref[0] == g)
        def _():
            for s in range(kv):
                cols = pl.ds((g ^ s) * width, width)
                out_refs[s][0] = query_ref[:, cols]
                out_refs[s][1] = grad_ref[:, cols]


def stack_kernel(count, *refs):
    ins, refs = refs[:count], refs[count:]
    passed = len(refs) // 2
    refs, out_ref = refs[:-1], refs[-1]
    for i, ref in enumerate(ins):
        out_ref[i] = ref[...]
    if passed:
        refs[-1][...] = refs[0][...]


class Plan:
    def __init__(self, kv, block_len, block_rows, rows, group, cores, z_devices, parts):
        self.kv, self.block_len, self.block_rows, self.rows = kv, block_len, block_rows, rows
        self.group, self.cores, self.parts, self.z_part = group, cores, parts, z_devices // parts
        self.blocks = rows // block_rows
        self.tile_rows = block_rows if block_rows % 16 == 0 else rows
        self.lanes = group * self.tile_rows
        self.query_rows = kv * group * rows
        self.chunk_keys = self.z_part * kv * rows
        self.tiles = [(s, start) for s in range(kv) for start in range(0, rows, self.tile_rows)]

    def zone(self, part):
        first = (self.parts - 1 - part) * self.z_part
        return range(first, first + self.z_part)

    def at(self, tile):
        return pl.ds(tile * self.lanes, self.lanes)

    def keys_at(self, i):
        return pl.ds(i * self.chunk_keys, self.chunk_keys)

    def gap(self, tile, info_ref):
        s, start = self.tiles[tile]
        head, ctx = info_ref[0], info_ref[1]
        row = lax.broadcasted_iota(jnp.int32, (1, self.lanes), 1) % self.tile_rows + start
        pos = jnp.zeros((1, self.lanes), jnp.int32)
        for b in range(start // self.block_rows, -(-(start + self.tile_rows) // self.block_rows)):
            first = info_ref[2 + ctx * self.blocks + b] * self.block_len + (head ^ s) * self.block_rows
            pos = jnp.where(row // self.block_rows == b, first + row % self.block_rows, pos)
        return pos - lax.broadcasted_iota(jnp.int32, (self.block_rows, self.lanes), 0)

    def masked(self, scores, gap, chunk, info_ref):
        head, ctx = info_ref[0], info_ref[1]
        a, core, part = chunk
        for j in range(self.chunk_keys // self.block_rows):
            m, rest = divmod(j, self.kv * self.blocks)
            s, b = divmod(rest, self.blocks)
            stored = (ctx ^ (self.zone(part)[m] * self.cores + core)) * self.blocks + b
            first = info_ref[2 + stored] * self.block_len + (head ^ (a * self.kv + s)) * self.block_rows
            block = scores[j * self.block_rows : (j + 1) * self.block_rows]
            yield j * self.block_rows, jnp.where(gap >= first, block, LOWEST)

    def turn(self, kv_refs, turned_ref):
        for i, ref in enumerate(kv_refs):
            turned_ref[:, self.keys_at(i)] = ref[...].reshape(self.chunk_keys, 2 * HD).T

    def keys(self, ref):
        return ref[:, :, :, :HD].reshape(self.chunk_keys, HD)

    def values(self, ref):
        return ref[:, :, :, HD:].reshape(self.chunk_keys, HD)

    def fold(self, block):
        return block.reshape(block.shape[0] // 8, 8, self.lanes)

    def scores(self, tile, chunks, kv_refs, q_t, e_ref, cols, info_ref):
        gap = self.gap(tile, info_ref)
        top = jnp.full((8, self.lanes), FLOOR, F32)
        for i, ref in enumerate(kv_refs):
            scores = dot(self.keys(ref), q_t)
            for row, part in self.masked(scores, gap, chunks[i], info_ref):
                e_ref[pl.ds(i * self.chunk_keys + row, part.shape[0]), cols] = part
                top = jnp.maximum(top, jnp.max(self.fold(part), axis=0))
        return jnp.max(top, axis=0, keepdims=True)

    def exponents(self, count, e_ref, cols, top):
        total = jnp.zeros((8, self.lanes), F32)
        for i in range(count):
            part = jnp.exp2(e_ref[self.keys_at(i), cols] * EXPO - top * EXPO)
            e_ref[self.keys_at(i), cols] = part
            total = total + jnp.sum(self.fold(part), axis=0)
        return jnp.sum(total, axis=0, keepdims=True)

    def store_heads(self, out_ref, tile, turned):
        s, start = self.tiles[tile]
        block = turned.T.astype(BF)
        for n in range(self.group):
            piece = block[n * self.tile_rows : (n + 1) * self.tile_rows]
            out_ref[pl.ds(start, self.tile_rows), pl.ds(n * HD, HD)] = piece

    def back(self, dkv_refs, p_ref, ds_ref, q_ref, do_ref):
        shape = (self.z_part, self.kv, self.rows, HD)
        for i, out_ref in enumerate(dkv_refs):
            at = self.keys_at(i)
            out_ref[:, :, :, :HD] = dot(ds_ref[at, :], q_ref[...]).astype(BF).reshape(shape)
            out_ref[:, :, :, HD:] = dot(p_ref[at, :], do_ref[...]).astype(BF).reshape(shape)


def forward_part(plan, chunks, info_ref, q_t, kv_refs, e_ref, top_ref, sum_ref, mix_ref, turned_ref):
    spans = [plan.at(tile) for tile in range(len(plan.tiles))]
    tops = [
        plan.scores(tile, chunks, kv_refs, q_t[:, at], e_ref, at, info_ref)
        for tile, at in enumerate(spans)
    ]
    plan.turn(kv_refs, turned_ref)
    for at, top in zip(spans, tops):
        top_ref[:, at] = top
        sum_ref[:, at] = plan.exponents(len(chunks), e_ref, at, top)
    for at in spans:
        mixed = jnp.zeros((HD, plan.lanes), F32)
        for i in range(len(chunks)):
            weights = e_ref[plan.keys_at(i), at].astype(BF)
            mixed = mixed + dot(turned_ref[pl.ds(HD, HD), plan.keys_at(i)], weights)
        mix_ref[:, at] = mixed


def turn_kernel(plan, *refs):
    q_parts, (q_all, do_all, q_t, do_t) = refs[:-4], refs[-4:]
    for tile, (s, start) in enumerate(plan.tiles):
        span = pl.ds(start, plan.tile_rows)
        for n in range(plan.group):
            at = pl.ds(tile * plan.lanes + n * plan.tile_rows, plan.tile_rows)
            q_all[at, :] = q_parts[s][0, span, pl.ds(n * HD, HD)]
            do_all[at, :] = q_parts[s][1, span, pl.ds(n * HD, HD)]
        at = plan.at(tile)
        q_t[:, at] = q_all[at, :].T
        do_t[:, at] = do_all[at, :].T


def part_kernel(plan, chunks, info_ref, q_t, *refs):
    forward_part(plan, chunks, info_ref, q_t, refs[: len(chunks)], *refs[-5:])


def far_kernel(plan, chunks, others, info_ref, q_all, do_all, q_t, do_t, *refs):
    kv, count = plan.kv, len(chunks)
    partial, refs = [refs[3 * i : 3 * i + 3] for i in range(others)], refs[3 * others :]
    kv_refs, refs = refs[:count], refs[count:]
    att_refs, refs = refs[:kv], refs[kv:]
    scale_refs, (delta_ref, q_grad_ref), refs = refs[:others], refs[others : others + 2], refs[others + 2 :]
    dkv_refs, (turned_ref, e_ref, w_ref, p_ref, ds_ref) = refs[:-5], refs[-5:]
    spans = [plan.at(tile) for tile in range(len(plan.tiles))]
    tops = [
        plan.scores(tile, chunks, kv_refs, q_t[:, at], e_ref, at, info_ref)
        for tile, at in enumerate(spans)
    ]
    plan.turn(kv_refs, turned_ref)
    for at in spans:
        for i, ref in enumerate(kv_refs):
            w_ref[plan.keys_at(i), at] = dot(plan.values(ref), do_t[:, at])
    inverses, mixes = [], []
    for at, top in zip(spans, tops):
        for top_ref, _, _ in partial:
            top = jnp.maximum(top, top_ref[:, at])
        total = plan.exponents(count, e_ref, at, top)
        factors = [jnp.exp2((top_ref[:, at] - top) * EXPO) for top_ref, _, _ in partial]
        for factor, (_, sum_ref, _) in zip(factors, partial):
            total = total + factor * sum_ref[:, at]
        inverse = 1.0 / total
        for factor, scale_ref in zip(factors, scale_refs):
            scale_ref[:, at] = factor * inverse
        inverses.append(inverse)
    for at, inverse in zip(spans, inverses):
        mixed = jnp.zeros((HD, plan.lanes), F32)
        for scale_ref, (_, _, mix_ref) in zip(scale_refs, partial):
            mixed = mixed + mix_ref[:, at] * scale_ref[:, at]
        for i in range(count):
            probs = (e_ref[plan.keys_at(i), at] * inverse).astype(BF)
            p_ref[plan.keys_at(i), at] = probs
            mixed = mixed + dot(turned_ref[pl.ds(HD, HD), plan.keys_at(i)], probs)
        mixes.append(mixed.astype(BF).astype(F32))
    for at, mixed in zip(spans, mixes):
        delta_ref[:, at] = jnp.sum(do_t[:, at].astype(F32) * mixed, axis=0, keepdims=True)
    for at, inverse in zip(spans, inverses):
        q_grad = jnp.zeros((HD, plan.lanes), F32)
        for i in range(count):
            probs = e_ref[plan.keys_at(i), at] * inverse
            grad_s = (probs * (w_ref[plan.keys_at(i), at] - delta_ref[:, at])).astype(BF)
            ds_ref[plan.keys_at(i), at] = grad_s
            q_grad = q_grad + dot(turned_ref[pl.ds(0, HD), plan.keys_at(i)], grad_s)
        q_grad_ref[:, at] = q_grad
    plan.back(dkv_refs, p_ref, ds_ref, q_all, do_all)
    for tile, mixed in enumerate(mixes):
        plan.store_heads(att_refs[plan.tiles[tile][0]], tile, mixed)


def back_kernel(plan, rows_at, last, order, q_all, do_all, do_t, e_ref, scale_ref, delta_ref, q_grad_in, *refs):
    count = len(rows_at)
    kv_refs, refs = refs[:count], refs[count + order :]
    refs, (turned_ref, p_ref, ds_ref) = refs[:-3], refs[-3:]
    outs, dkv_refs = refs[:-count], refs[-count:]
    spans = [plan.at(tile) for tile in range(len(plan.tiles))]
    for at in spans:
        for i, ref in enumerate(kv_refs):
            probs = e_ref[plan.keys_at(rows_at[i]), at] * scale_ref[:, at]
            p_ref[plan.keys_at(i), at] = probs.astype(BF)
            grad_s = (probs * (dot(plan.values(ref), do_t[:, at]) - delta_ref[:, at])).astype(BF)
            ds_ref[plan.keys_at(i), at] = grad_s
    plan.turn(kv_refs, turned_ref)
    plan.back(dkv_refs, p_ref, ds_ref, q_all, do_all)
    for tile, at in enumerate(spans):
        q_grad = q_grad_in[:, at]
        for i in range(count):
            q_grad = q_grad + dot(turned_ref[pl.ds(0, HD), plan.keys_at(i)], ds_ref[plan.keys_at(i), at])
        if last:
            plan.store_heads(outs[plan.tiles[tile][0]], tile, q_grad * SCALING)
        else:
            outs[0][:, at] = q_grad


def add_kernel(*refs):
    total = refs[0][...].astype(F32)
    for ref in refs[1:-1]:
        total = total + ref[...].astype(F32)
    refs[-1][...] = total.astype(BF)


def sum_heads_kernel(parts, *refs):
    for m_z, out_ref in enumerate(refs[parts:]):
        total = refs[0][m_z].astype(F32)
        for ref in refs[1:parts]:
            total = total + ref[m_z].astype(F32)
        out_ref[...] = total.astype(BF)


def sum_z_kernel(kv, *refs):
    ins, outs = refs[:-kv], refs[-kv:]
    for s, out_ref in enumerate(outs):
        total = ins[0][s].astype(F32)
        for ref in ins[1:]:
            total = total + ref[s].astype(F32)
        out_ref[...] = total.astype(BF)


def finish_kv_kernel(kv, group_ref, *refs):
    key_ref, value_ref = refs[kv:]
    for g in range(kv):

        @pl.when(group_ref[0] == g)
        def _():
            for s in range(kv):
                cols = pl.ds((g ^ s) * HD, HD)
                key_ref[:, cols] = (refs[s][:, :HD].astype(F32) * SCALING).astype(BF)
                value_ref[:, cols] = refs[s][:, HD:]


def finish_q_kernel(kv, group_ref, *refs):
    att_ref, grad_ref = refs[2 * kv :]
    width = refs[0].shape[1]
    for g in range(kv):

        @pl.when(group_ref[0] == g)
        def _():
            for s in range(kv):
                cols = pl.ds((g ^ s) * width, width)
                att_ref[:, cols] = refs[s][...]
                grad_ref[:, cols] = refs[kv + s][...]


def shards(queries, key_vectors, value_vectors, out_grad, block_order):
    heads_devices = lax.axis_size("head")
    ctx_devices = lax.axis_size("ctx")
    halves, block_rows, query_width = queries.shape
    kv = key_vectors.shape[2] // HD
    rows = halves * block_rows
    width = query_width // kv
    cores = CORES if ctx_devices % CORES == 0 else 1
    z_devices = ctx_devices // cores
    spans = heads_devices // kv
    parts = 2 if z_devices % 2 == 0 else 1
    plan = Plan(kv, block_rows * heads_devices, block_rows, rows, width // HD, cores, z_devices, parts)
    z_part = plan.z_part
    head = lax.axis_index("head").astype(jnp.int32)
    place = jnp.stack([head, lax.axis_index("ctx").astype(jnp.int32)])
    info = jnp.concatenate([place, block_order])
    own_group = (head % kv).reshape(1)
    queries = queries.reshape(rows, query_width)
    out_grad = out_grad.reshape(rows, query_width)
    key_vectors = key_vectors.reshape(rows, kv * HD)
    value_vectors = value_vectors.reshape(rows, kv * HD)

    def bf(*dims):
        return jax.ShapeDtypeStruct(dims, BF)

    def f32(*dims):
        return jax.ShapeDtypeStruct(dims, F32)

    def with_swaps(blocks):
        return [blocks[0]] + [swap(blocks[s], "head", s) for s in range(1, kv)]

    dkv = bf(z_part, kv, rows, 2 * HD)

    key_parts = with_swaps([key_vectors] * kv)[1:]
    value_parts = with_swaps([value_vectors] * kv)[1:]
    mine = (head % kv) * HD
    own = jnp.concatenate(
        [lax.dynamic_slice_in_dim(block, mine, HD, 1) for block in (key_vectors, value_vectors)], axis=1
    )
    q_parts = call(
        functools.partial(pack_q_kernel, kv),
        "pack_q",
        (own_group, queries, out_grad),
        [bf(2, rows, width)] * kv,
        [SMEM, VMEM, VMEM],
    )
    own = after([own], q_parts[1:])[0]
    piece = call(
        functools.partial(pack_kv_kernel, kv),
        "pack_kv",
        (own_group, own, *[part for pair in zip(key_parts, value_parts) for part in pair]),
        [bf(kv, rows, 2 * HD)],
        [SMEM] + [VMEM] * (2 * kv - 1),
    )[0]
    pieces = [swap(piece, "ctx", m * cores) for m in reversed(range(1, z_devices))]
    pieces = [piece] + pieces[::-1]
    q_parts = with_swaps(q_parts)
    column, handed, order = [None] * parts, [None] * parts, []
    for p in reversed(range(parts)):
        parcels = [pieces[m] for m in plan.zone(p)]
        extra = [column[p + 1], *order] if order else []
        *handed_on, column[p] = call(
            functools.partial(stack_kernel, len(parcels)),
            "stack",
            (*parcels, *extra),
            [dkv] * (1 + bool(extra)),
        )
        handed[p] = column[p]
        if extra:
            handed[p + 1] = handed_on[0]
        order = [swap(column[p][0, 0, :, :HD], "ctx", 1)] if cores > 1 and p else []
    columns = [[swap(half, "head", a * kv) for half in column] for a in range(1, spans)]
    near_kv = [column] + [[swap(half, "ctx", core) for half in handed] for core in range(1, cores)]
    near_flat = [half for pair in near_kv for half in pair]
    each = range(parts)
    near_chunks = [(0, core, p) for core in range(cores) for p in each]
    mid_chunks = [(a, 0, p) for a in range(1, spans) for p in each]
    far_chunks = [(a, core, p) for a in range(1, spans) for core in range(1, cores) for p in each]

    keys = plan.chunk_keys
    query_rows = plan.query_rows
    row, column_out = f32(1, query_rows), f32(HD, query_rows)

    q_all, do_all, q_t, do_t = call(
        functools.partial(turn_kernel, plan),
        "turn",
        q_parts,
        [bf(query_rows, HD)] * 2 + [bf(HD, query_rows)] * 2,
    )

    def forward(name, chunks, kv_refs, order):
        size = len(chunks) * keys
        return call(
            functools.partial(part_kernel, plan, chunks),
            name,
            (info, q_t, *kv_refs, *order),
            [f32(size, query_rows), row, row, column_out],
            [SMEM] + [VMEM] * (1 + len(kv_refs) + len(order)),
            [pltpu.VMEM((2 * HD, size), BF)],
            size * 4 * HD,
            8 * size * query_rows * HD,
        )

    mids, order = [None] * parts, []
    for p in reversed(each):
        if p + 1 < parts or parts == 1:
            near_e, *near = forward("attend_near", near_chunks, near_flat, order)
            order = [near[0]]
            for pair in columns:
                pair[p] = after([pair[p]], order)[0]
        mids[p] = forward("attend_mid", [c for c in mid_chunks if c[2] == p], [pair[p] for pair in columns], order)
        order = [mids[p][1]]
    far_kv = [swap(pair[p], "ctx", core) for pair in columns for core in range(1, cores) for p in each]
    far_keys = len(far_kv) * keys
    outs = call(
        functools.partial(far_kernel, plan, far_chunks, 1 + parts),
        "attend_far",
        (info, q_all, do_all, q_t, do_t, *near, *[r for mid in mids for r in mid[1:]], *far_kv),
        [bf(rows, width)] * kv + [row] * (2 + parts) + [column_out] + [dkv] * len(far_kv),
        [SMEM] + [VMEM] * (7 + 3 * parts + len(far_kv)),
        [
            pltpu.VMEM((2 * HD, far_keys), BF),
            pltpu.VMEM((far_keys, query_rows), F32),
            pltpu.VMEM((far_keys, query_rows), F32),
            pltpu.VMEM((far_keys, query_rows), BF),
            pltpu.VMEM((far_keys, query_rows), BF),
        ],
        far_keys * (4 * HD + 12 * query_rows),
        16 * far_keys * query_rows * HD,
    )
    att_parts, outs = outs[:kv], outs[kv:]
    (near_scale, *mid_scales), outs = outs[: 1 + parts], outs[1 + parts :]
    (delta, q_grad), far_dkv = outs[:2], outs[2:]

    def back(rows_at, last, e, scale, q_grad, kv_refs, order):
        count = len(rows_at)
        q_outs = [bf(rows, width)] * kv if last else [column_out]
        outs = call(
            functools.partial(back_kernel, plan, rows_at, last, len(order)),
            "attend_back",
            (q_all, do_all, do_t, e, scale, delta, q_grad, *kv_refs, *order),
            q_outs + [dkv] * count,
            None,
            [
                pltpu.VMEM((2 * HD, count * keys), BF),
                pltpu.VMEM((count * keys, query_rows), BF),
                pltpu.VMEM((count * keys, query_rows), BF),
            ],
            count * keys * (4 * HD + 4 * query_rows),
            12 * count * keys * query_rows * HD,
        )
        return outs[: len(q_outs)], outs[len(q_outs) :]

    sums = [[] for _ in range(parts)]
    totals = []
    for p in reversed(each):
        mid_kv = [pair[p] for pair in columns]
        (q_grad,), mid_dkv = back(
            list(range(len(mid_kv))), False, mids[p][0], mid_scales[p], q_grad, mid_kv, []
        )
        for a in range(spans - 1):
            both = [mid_dkv[a]]
            for core in range(1, cores):
                ours = far_dkv[(a * (cores - 1) + core - 1) * parts + p]
                both.append(swap(ours, "ctx", core))
            totals += call(add_kernel, "sum_cores", after(both, totals[-1:]), [dkv])
            sums[p].append(swap(totals[-1], "head", (a + 1) * kv))
    order = [swap(totals[-1][0, 0, :, :HD], "ctx", 1)] if cores > 1 else []
    for core in reversed(range(cores)):
        outs, parts_dkv = back(
            [core * parts + p for p in each], core == 0, near_e, near_scale, q_grad, near_kv[core], order
        )
        q_grad = outs[0]
        for p in range(parts):
            sums[p].append(swap(parts_dkv[p], "ctx", core) if core else parts_dkv[p])
    q_grad_parts = outs[:kv]
    z_parts = [None] * z_devices
    for p in range(parts):
        totals = call(
            functools.partial(sum_heads_kernel, len(sums[p])),
            "sum_heads",
            sums[p],
            [bf(kv, rows, 2 * HD)] * z_part,
        )

        for m, total in zip(plan.zone(p), totals):
            z_parts[m] = swap(total, "ctx", m * cores) if m else total
    ordered = [z_parts[m] for p in range(parts) for m in plan.zone(p)]
    pair_parts = call(
        functools.partial(sum_z_kernel, kv), "sum_z", ordered, [bf(rows, 2 * HD)] * kv
    )
    pair_parts = with_swaps(pair_parts)
    attended, query_grad = call(
        functools.partial(finish_q_kernel, kv),
        "finish_q",
        (own_group, *with_swaps(att_parts), *with_swaps(q_grad_parts)),
        [bf(rows, query_width)] * 2,
        [SMEM] + [VMEM] * (2 * kv),
    )
    key_grad, value_grad = call(
        functools.partial(finish_kv_kernel, kv),
        "finish_kv",
        (own_group, *pair_parts),
        [bf(rows, kv * HD)] * 2,
        [SMEM] + [VMEM] * kv,
    )
    return (
        attended.reshape(halves, block_rows, query_width),
        query_grad.reshape(halves, block_rows, query_width),
        key_grad.reshape(halves, block_rows, kv * HD),
        value_grad.reshape(halves, block_rows, kv * HD),
    )


def solution(mesh):
    split = P("ctx", "head", None)
    return jax.shard_map(
        shards,
        mesh=mesh,
        in_specs=(split, split, split, split, P()),
        out_specs=(split, split, split, split),
        check_vma=False,
    )
```

```python
import functools
import math

import jax
import jax.numpy as jnp
from jax import lax
from jax.experimental import pallas as pl
from jax.experimental.pallas import tpu as pltpu
from jax.sharding import PartitionSpec as P

HD = 128
CORES = 2
BF = jnp.bfloat16
F32 = jnp.float32
LOWEST = -1e30
FLOOR = -1e29
SCALING = 1.0 / math.sqrt(HD)
EXPO = SCALING * math.log2(math.e)

VMEM = pl.BlockSpec(memory_space=pltpu.VMEM)
SMEM = pl.BlockSpec(memory_space=pltpu.SMEM)


def swap(block, axis, mask):
    size = lax.axis_size(axis)
    return lax.ppermute(block, axis, [(i, i ^ mask) for i in range(size)])


def nbytes(arrays):
    return sum(math.prod(a.shape) * a.dtype.itemsize for a in arrays)


def after(blocks, earlier):
    if not earlier:
        return tuple(blocks)
    return lax.optimization_barrier((tuple(blocks), tuple(earlier)))[0]


def call(kernel, name, ins, outs, specs=None, scratch=(), extra=0, flops=0):
    limit = nbytes(ins) + nbytes(outs) + extra + (12 << 20)
    return pl.pallas_call(
        kernel,
        out_shape=list(outs),
        in_specs=specs or [VMEM] * len(ins),
        out_specs=[VMEM] * len(outs),
        scratch_shapes=list(scratch),
        compiler_params=pltpu.CompilerParams(vmem_limit_bytes=min(limit, 60 << 20)),
        cost_estimate=pl.CostEstimate(
            flops=flops, bytes_accessed=nbytes(ins) + nbytes(outs), transcendentals=0
        ),
        name=name,
    )(*ins)


def dot(left, right):
    return jnp.dot(left, right, preferred_element_type=F32)


def dot_rows(left, right):
    return lax.dot_general(left, right, (((1,), (1,)), ((), ())), preferred_element_type=F32)


def pack_kv_kernel(kv, group_ref, *refs):
    out_ref = refs[-1]
    out_ref[0] = refs[0][...]
    for g in range(kv):

        @pl.when(group_ref[0] == g)
        def _():
            cols = pl.ds(g * HD, HD)
            for s in range(1, kv):
                out_ref[s, :, :HD] = refs[2 * s - 1][:, cols]
                out_ref[s, :, HD:] = refs[2 * s][:, cols]


def pack_q_kernel(kv, group_ref, query_ref, grad_ref, *out_refs):
    width = out_refs[0].shape[2]
    for g in range(kv):

        @pl.when(group_ref[0] == g)
        def _():
            for s in range(kv):
                cols = pl.ds((g ^ s) * width, width)
                out_refs[s][0] = query_ref[:, cols]
                out_refs[s][1] = grad_ref[:, cols]


def stack_kernel(count, *refs):
    for i, ref in enumerate(refs[:count]):
        refs[-1][i] = ref[...]


class Plan:
    def __init__(self, kv, block_len, block_rows, rows, group, cores, z_devices, parts):
        self.kv, self.block_len, self.block_rows, self.rows = kv, block_len, block_rows, rows
        self.group, self.cores, self.parts, self.z_part = group, cores, parts, z_devices // parts
        self.blocks = rows // block_rows
        self.tile_rows = block_rows if block_rows % 16 == 0 else rows
        self.lanes = group * self.tile_rows
        self.query_rows = kv * group * rows
        self.chunk_keys = self.z_part * kv * rows
        self.tiles = [(s, start) for s in range(kv) for start in range(0, rows, self.tile_rows)]

    def zone(self, part):
        first = (self.parts - 1 - part) * self.z_part
        return range(first, first + self.z_part)

    def at(self, tile):
        return pl.ds(tile * self.lanes, self.lanes)

    def keys_at(self, i):
        return pl.ds(i * self.chunk_keys, self.chunk_keys)

    def gap(self, tile, info_ref):
        s, start = self.tiles[tile]
        head, ctx = info_ref[0], info_ref[1]
        row = lax.broadcasted_iota(jnp.int32, (1, self.lanes), 1) % self.tile_rows + start
        pos = jnp.zeros((1, self.lanes), jnp.int32)
        for b in range(start // self.block_rows, -(-(start + self.tile_rows) // self.block_rows)):
            first = info_ref[2 + ctx * self.blocks + b] * self.block_len + (head ^ s) * self.block_rows
            pos = jnp.where(row // self.block_rows == b, first + row % self.block_rows, pos)
        return pos - lax.broadcasted_iota(jnp.int32, (self.block_rows, self.lanes), 0)

    def masked(self, scores, gap, chunk, info_ref):
        head, ctx = info_ref[0], info_ref[1]
        a, core, part = chunk
        for j in range(self.chunk_keys // self.block_rows):
            m, rest = divmod(j, self.kv * self.blocks)
            s, b = divmod(rest, self.blocks)
            stored = (ctx ^ (self.zone(part)[m] * self.cores + core)) * self.blocks + b
            first = info_ref[2 + stored] * self.block_len + (head ^ (a * self.kv + s)) * self.block_rows
            block = scores[j * self.block_rows : (j + 1) * self.block_rows]
            yield j * self.block_rows, jnp.where(gap >= first, block, LOWEST)

    def turn(self, kv_refs, turned_ref):
        for i, ref in enumerate(kv_refs):
            turned_ref[:, self.keys_at(i)] = ref[...].reshape(self.chunk_keys, 2 * HD).T

    def keys(self, ref):
        return ref[:, :, :, :HD].reshape(self.chunk_keys, HD)

    def values(self, ref):
        return ref[:, :, :, HD:].reshape(self.chunk_keys, HD)

    def fold(self, block):
        return block.reshape(block.shape[0] // 8, 8, self.lanes)

    def scores(self, tile, chunks, kv_refs, q_t, e_ref, cols, info_ref):
        gap = self.gap(tile, info_ref)
        top = jnp.full((8, self.lanes), FLOOR, F32)
        for i, ref in enumerate(kv_refs):
            scores = dot(self.keys(ref), q_t)
            for row, part in self.masked(scores, gap, chunks[i], info_ref):
                e_ref[pl.ds(i * self.chunk_keys + row, part.shape[0]), cols] = part
                top = jnp.maximum(top, jnp.max(self.fold(part), axis=0))
        return jnp.max(top, axis=0, keepdims=True)

    def exponents(self, count, e_ref, cols, top):
        total = jnp.zeros((8, self.lanes), F32)
        for i in range(count):
            part = jnp.exp2(e_ref[self.keys_at(i), cols] * EXPO - top * EXPO)
            e_ref[self.keys_at(i), cols] = part
            total = total + jnp.sum(self.fold(part), axis=0)
        return jnp.sum(total, axis=0, keepdims=True)

    def store_heads(self, out_ref, tile, turned):
        s, start = self.tiles[tile]
        block = turned.T.astype(BF)
        for n in range(self.group):
            piece = block[n * self.tile_rows : (n + 1) * self.tile_rows]
            out_ref[pl.ds(start, self.tile_rows), pl.ds(n * HD, HD)] = piece

    def back(self, dkv_refs, p_ref, ds_ref, q_ref, do_ref):
        shape = (self.z_part, self.kv, self.rows, HD)
        for i, out_ref in enumerate(dkv_refs):
            at = self.keys_at(i)
            out_ref[:, :, :, :HD] = dot(ds_ref[at, :], q_ref[...]).astype(BF).reshape(shape)
            out_ref[:, :, :, HD:] = dot(p_ref[at, :], do_ref[...]).astype(BF).reshape(shape)


def forward_part(plan, chunks, info_ref, q_t, kv_refs, e_ref, top_ref, sum_ref, mix_ref, turned_ref):
    spans = [plan.at(tile) for tile in range(len(plan.tiles))]
    tops = [
        plan.scores(tile, chunks, kv_refs, q_t[:, at], e_ref, at, info_ref)
        for tile, at in enumerate(spans)
    ]
    plan.turn(kv_refs, turned_ref)
    for at, top in zip(spans, tops):
        top_ref[:, at] = top
        sum_ref[:, at] = plan.exponents(len(chunks), e_ref, at, top)
    for at in spans:
        mixed = jnp.zeros((HD, plan.lanes), F32)
        for i in range(len(chunks)):
            weights = e_ref[plan.keys_at(i), at].astype(BF)
            mixed = mixed + dot(turned_ref[pl.ds(HD, HD), plan.keys_at(i)], weights)
        mix_ref[:, at] = mixed


def turn_kernel(plan, *refs):
    q_parts, (q_all, do_all, q_t, do_t) = refs[:-4], refs[-4:]
    for tile, (s, start) in enumerate(plan.tiles):
        span = pl.ds(start, plan.tile_rows)
        for n in range(plan.group):
            at = pl.ds(tile * plan.lanes + n * plan.tile_rows, plan.tile_rows)
            q_all[at, :] = q_parts[s][0, span, pl.ds(n * HD, HD)]
            do_all[at, :] = q_parts[s][1, span, pl.ds(n * HD, HD)]
        at = plan.at(tile)
        q_t[:, at] = q_all[at, :].T
        do_t[:, at] = do_all[at, :].T


def part_kernel(plan, chunks, info_ref, q_t, *refs):
    forward_part(plan, chunks, info_ref, q_t, refs[: len(chunks)], *refs[-5:])


def far_kernel(plan, chunks, others, info_ref, q_all, do_all, q_t, do_t, *refs):
    count = len(chunks)
    partial, refs = [refs[3 * i : 3 * i + 3] for i in range(others)], refs[3 * others :]
    kv_refs, refs = refs[:count], refs[count:]
    scale_refs, (delta_ref, mixed_ref, ds_ref), refs = refs[:others], refs[others : others + 3], refs[others + 3 :]
    dkv_refs, (turned_ref, e_ref, w_ref, p_ref) = refs[:-4], refs[-4:]
    spans = [plan.at(tile) for tile in range(len(plan.tiles))]
    tops = [
        plan.scores(tile, chunks, kv_refs, q_t[:, at], e_ref, at, info_ref)
        for tile, at in enumerate(spans)
    ]
    plan.turn(kv_refs, turned_ref)
    for at in spans:
        for i, ref in enumerate(kv_refs):
            w_ref[plan.keys_at(i), at] = dot(plan.values(ref), do_t[:, at])
    inverses = []
    for at, top in zip(spans, tops):
        for top_ref, _, _ in partial:
            top = jnp.maximum(top, top_ref[:, at])
        total = plan.exponents(count, e_ref, at, top)
        factors = [jnp.exp2((top_ref[:, at] - top) * EXPO) for top_ref, _, _ in partial]
        for factor, (_, sum_ref, _) in zip(factors, partial):
            total = total + factor * sum_ref[:, at]
        inverse = 1.0 / total
        for factor, scale_ref in zip(factors, scale_refs):
            scale_ref[:, at] = factor * inverse
        inverses.append(inverse)
    for at, inverse in zip(spans, inverses):
        mixed = jnp.zeros((HD, plan.lanes), F32)
        for scale_ref, (_, _, mix_ref) in zip(scale_refs, partial):
            mixed = mixed + mix_ref[:, at] * scale_ref[:, at]
        for i in range(count):
            probs = (e_ref[plan.keys_at(i), at] * inverse).astype(BF)
            p_ref[plan.keys_at(i), at] = probs
            mixed = mixed + dot(turned_ref[pl.ds(HD, HD), plan.keys_at(i)], probs)
        mixed = mixed.astype(BF)
        mixed_ref[:, at] = mixed
        delta_ref[:, at] = jnp.sum(do_t[:, at].astype(F32) * mixed.astype(F32), axis=0, keepdims=True)
    for at, inverse in zip(spans, inverses):
        for i in range(count):
            probs = e_ref[plan.keys_at(i), at] * inverse
            ds_ref[plan.keys_at(i), at] = (probs * (w_ref[plan.keys_at(i), at] - delta_ref[:, at])).astype(BF)
    plan.back(dkv_refs, p_ref, ds_ref, q_all, do_all)


def tail_kernel(plan, order, mixed_ref, ds_ref, q_grad_in, *refs):
    ins, (*att_refs, q_grad_ref, turned_ref) = refs[: -plan.kv - 2], refs[-plan.kv - 2 :]
    plan.turn(ins[: len(ins) - order], turned_ref)
    for tile, (s, _) in enumerate(plan.tiles):
        at = plan.at(tile)
        q_grad_ref[:, at] = q_grad_in[:, at] + dot(turned_ref[pl.ds(0, HD), :], ds_ref[:, at])
        plan.store_heads(att_refs[s], tile, mixed_ref[:, at].astype(F32))


def back_kernel(plan, units, last, order, follows, groups, q_all, do_all, do_t, delta_ref, *refs):
    count = len(units)
    e_refs, scale_refs, refs = refs[:groups], refs[groups : 2 * groups], refs[2 * groups :]
    q_grad_in, refs = refs[:follows], refs[follows:]
    kv_refs, refs = refs[:count], refs[count + order :]
    refs, (turned_ref, p_ref, ds_ref) = refs[:-3], refs[-3:]
    outs, dkv_refs = refs[:-count], refs[-count:]
    spans = [plan.at(tile) for tile in range(len(plan.tiles))]
    for at in spans:
        for i, ref in enumerate(kv_refs):
            group, row = units[i]
            probs = e_refs[group][plan.keys_at(row), at] * scale_refs[group][:, at]
            p_ref[plan.keys_at(i), at] = probs.astype(BF)
            grad_s = (probs * (dot(plan.values(ref), do_t[:, at]) - delta_ref[:, at])).astype(BF)
            ds_ref[plan.keys_at(i), at] = grad_s
    plan.turn(kv_refs, turned_ref)
    plan.back(dkv_refs, p_ref, ds_ref, q_all, do_all)
    for tile, at in enumerate(spans):
        q_grad = q_grad_in[0][:, at] if follows else jnp.zeros((HD, plan.lanes), F32)
        for i in range(count):
            q_grad = q_grad + dot(turned_ref[pl.ds(0, HD), plan.keys_at(i)], ds_ref[plan.keys_at(i), at])
        if last:
            plan.store_heads(outs[plan.tiles[tile][0]], tile, q_grad * SCALING)
        else:
            outs[0][:, at] = q_grad


def add_kernel(*refs):
    total = refs[0][...].astype(F32)
    for ref in refs[1:-1]:
        total = total + ref[...].astype(F32)
    refs[-1][...] = total.astype(BF)


def sum_heads_kernel(parts, *refs):
    for m_z, out_ref in enumerate(refs[parts:]):
        total = refs[0][m_z].astype(F32)
        for ref in refs[1:parts]:
            total = total + ref[m_z].astype(F32)
        out_ref[...] = total.astype(BF)


def sum_z_kernel(kv, *refs):
    ins, outs = refs[:-kv], refs[-kv:]
    for s, out_ref in enumerate(outs):
        total = ins[0][s].astype(F32)
        for ref in ins[1:]:
            total = total + ref[s].astype(F32)
        out_ref[...] = total.astype(BF)


def sum_far_kernel(*refs):
    total = refs[0][...].astype(F32)
    for ref in refs[1:-1]:
        total = total + ref[...].astype(F32)
    refs[-1][...] = total


def finish_kv_kernel(kv, group_ref, *refs):
    key_ref, value_ref = refs[kv:]
    for g in range(kv):

        @pl.when(group_ref[0] == g)
        def _():
            for s in range(kv):
                cols = pl.ds((g ^ s) * HD, HD)
                key_ref[:, cols] = (refs[s][:, :HD].astype(F32) * SCALING).astype(BF)
                value_ref[:, cols] = refs[s][:, HD:]


def finish_q_kernel(kv, group_ref, *refs):
    att_ref, grad_ref = refs[2 * kv :]
    width = refs[0].shape[1]
    for g in range(kv):

        @pl.when(group_ref[0] == g)
        def _():
            for s in range(kv):
                cols = pl.ds((g ^ s) * width, width)
                att_ref[:, cols] = refs[s][...]
                grad_ref[:, cols] = refs[kv + s][...]


def shards(queries, key_vectors, value_vectors, out_grad, block_order):
    heads_devices = lax.axis_size("head")
    ctx_devices = lax.axis_size("ctx")
    halves, block_rows, query_width = queries.shape
    kv = key_vectors.shape[2] // HD
    rows = halves * block_rows
    width = query_width // kv
    cores = CORES if ctx_devices % CORES == 0 else 1
    z_devices = ctx_devices // cores
    spans = heads_devices // kv
    parts = 2 if z_devices % 2 == 0 else 1
    plan = Plan(kv, block_rows * heads_devices, block_rows, rows, width // HD, cores, z_devices, parts)
    z_part = plan.z_part
    head = lax.axis_index("head").astype(jnp.int32)
    place = jnp.stack([head, lax.axis_index("ctx").astype(jnp.int32)])
    info = jnp.concatenate([place, block_order])
    own_group = (head % kv).reshape(1)
    queries = queries.reshape(rows, query_width)
    out_grad = out_grad.reshape(rows, query_width)
    key_vectors = key_vectors.reshape(rows, kv * HD)
    value_vectors = value_vectors.reshape(rows, kv * HD)

    def bf(*dims):
        return jax.ShapeDtypeStruct(dims, BF)

    def f32(*dims):
        return jax.ShapeDtypeStruct(dims, F32)

    def with_swaps(blocks):
        return [blocks[0]] + [swap(blocks[s], "head", s) for s in range(1, kv)]

    dkv = bf(z_part, kv, rows, 2 * HD)

    key_parts = with_swaps([key_vectors] * kv)[1:]
    value_parts = with_swaps([value_vectors] * kv)[1:]
    mine = (head % kv) * HD
    own = jnp.concatenate(
        [lax.dynamic_slice_in_dim(block, mine, HD, 1) for block in (key_vectors, value_vectors)], axis=1
    )
    q_parts = call(
        functools.partial(pack_q_kernel, kv),
        "pack_q",
        (own_group, queries, out_grad),
        [bf(2, rows, width)] * kv,
        [SMEM, VMEM, VMEM],
    )
    own = after([own], q_parts[1:])[0]
    piece = call(
        functools.partial(pack_kv_kernel, kv),
        "pack_kv",
        (own_group, own, *[part for pair in zip(key_parts, value_parts) for part in pair]),
        [bf(kv, rows, 2 * HD)],
        [SMEM] + [VMEM] * (2 * kv - 1),
    )[0]
    pieces = [swap(piece, "ctx", m * cores) for m in reversed(range(1, z_devices))]
    pieces = [piece] + pieces[::-1]
    q_parts = with_swaps(q_parts)
    each = range(parts)
    mid_chunks = [(a, 0, p) for a in range(1, spans) for p in each]
    far_chunks = [(a, core, p) for a in range(1, spans) for core in range(1, cores) for p in each]

    keys = plan.chunk_keys
    query_rows = plan.query_rows
    row, column_out = f32(1, query_rows), f32(HD, query_rows)

    q_all, do_all, q_t, do_t = call(
        functools.partial(turn_kernel, plan),
        "turn",
        q_parts,
        [bf(query_rows, HD)] * 2 + [bf(HD, query_rows)] * 2,
    )

    def forward(name, chunks, kv_refs, order, flops=8):
        size = len(chunks) * keys
        return call(
            functools.partial(part_kernel, plan, chunks),
            name,
            (info, q_t, *kv_refs, *order),
            [f32(size, query_rows), row, row, column_out],
            [SMEM] + [VMEM] * (1 + len(kv_refs) + len(order)),
            [pltpu.VMEM((2 * HD, size), BF)],
            size * 4 * HD,
            flops * size * query_rows * HD,
        )

    nears, mids, near_kv, order = [None] * parts, [None] * parts, [None] * parts, []
    columns = [[None] * parts for _ in range(1, spans)]

    def mid(p, order):
        chunks = [chunk for chunk in mid_chunks if chunk[2] == p]
        return forward("attend_mid", chunks, [pair[p] for pair in columns], order)

    for p in reversed(each):
        parcels = [pieces[m] for m in plan.zone(p)]
        part = call(functools.partial(stack_kernel, len(parcels)), "stack", (*parcels, *order), [dkv])[0]
        for a in range(1, spans):
            columns[a - 1][p] = swap(part, "head", a * kv)
        near_kv[p] = [part] + [swap(part, "ctx", core) for core in range(1, cores)]
        if p + 1 < parts:
            mids[p + 1] = mid(p + 1, order)
            order = [mids[p + 1][1]]
        chunks = [(0, core, p) for core in range(cores)]
        nears[p] = forward("attend_near", chunks, near_kv[p], order, 0 if p else 8)
        order = [nears[p][1]]
    for pair in columns:
        pair[0] = after([pair[0]], order)[0]
    mids[0] = mid(0, order)
    partials = nears + mids
    far_kv = [swap(pair[p], "ctx", core) for pair in columns for core in range(1, cores) for p in each]
    far_keys = len(far_kv) * keys
    outs = call(
        functools.partial(far_kernel, plan, far_chunks, len(partials)),
        "attend_far",
        (info, q_all, do_all, q_t, do_t, *[ref for part in partials for ref in part[1:]], *far_kv),
        [row] * (len(partials) + 1) + [bf(HD, query_rows), bf(far_keys, query_rows)] + [dkv] * len(far_kv),
        [SMEM] + [VMEM] * (4 + 3 * len(partials) + len(far_kv)),
        [
            pltpu.VMEM((2 * HD, far_keys), BF),
            pltpu.VMEM((far_keys, query_rows), F32),
            pltpu.VMEM((far_keys, query_rows), F32),
            pltpu.VMEM((far_keys, query_rows), BF),
        ],
        far_keys * (4 * HD + 12 * query_rows),
        16 * far_keys * query_rows * HD,
    )
    scales, (delta, mixed, far_ds, *far_dkv) = outs[: len(partials)], outs[len(partials) :]

    def back(units, last, parts_of, follows, kv_refs, order):
        count = len(units)
        q_outs = [bf(rows, width)] * kv if last else [column_out]
        es, of_scales = [partials[i][0] for i in parts_of], [scales[i] for i in parts_of]
        outs = call(
            functools.partial(back_kernel, plan, units, last, len(order), len(follows), len(parts_of)),
            "attend_back",
            (q_all, do_all, do_t, delta, *es, *of_scales, *follows, *kv_refs, *order),
            q_outs + [dkv] * count,
            None,
            [
                pltpu.VMEM((2 * HD, count * keys), BF),
                pltpu.VMEM((count * keys, query_rows), BF),
                pltpu.VMEM((count * keys, query_rows), BF),
            ],
            count * keys * (4 * HD + 4 * query_rows),
            12 * count * keys * query_rows * HD,
        )
        return outs[: len(q_outs)], outs[len(q_outs) :]

    sums = [[] for _ in range(parts)]
    totals, follows = [], []
    for p in reversed(each):
        mid_kv = [pair[p] for pair in columns]
        units = [(0, i) for i in range(len(mid_kv))]
        follows, mid_dkv = back(units, False, [parts + p], follows, mid_kv, [])
        for a in range(spans - 1):
            both = [mid_dkv[a]]
            for core in range(1, cores):
                ours = far_dkv[(a * (cores - 1) + core - 1) * parts + p]
                both.append(swap(ours, "ctx", core))
            totals += call(add_kernel, "sum_cores", after(both, totals[-1:]), [dkv])
            sums[p].append(swap(totals[-1], "head", (a + 1) * kv))
    order = [swap(totals[-1][0, 0, :, :HD], "ctx", 1)] if cores > 1 else []
    *att_parts, q_grad = call(
        functools.partial(tail_kernel, plan, len(order)),
        "attend_tail",
        (mixed, far_ds, *follows, *far_kv, *order),
        [bf(rows, width)] * kv + [column_out],
        None,
        [pltpu.VMEM((2 * HD, far_keys), BF)],
        far_keys * 4 * HD,
        2 * far_keys * query_rows * HD,
    )
    follows = [q_grad]
    for core in reversed(range(cores)):
        units = [(p, core) for p in each]
        kv_refs = [near_kv[p][core] for p in each]
        follows, parts_dkv = back(units, core == 0, list(each), follows, kv_refs, order)
        for p in each:
            sums[p].append(swap(parts_dkv[p], "ctx", core) if core else parts_dkv[p])
    q_grad_parts = follows
    z_parts = [None] * z_devices
    for p in range(parts):
        totals = call(
            functools.partial(sum_heads_kernel, len(sums[p])),
            "sum_heads",
            sums[p],
            [bf(kv, rows, 2 * HD)] * z_part,
        )

        for m, total in zip(plan.zone(p), totals):
            z_parts[m] = swap(total, "ctx", m * cores) if m else total
    ordered = [z_parts[m] for p in each for m in plan.zone(p)]
    if parts > 1:
        far_z = call(sum_far_kernel, "sum_far_z", ordered[:z_part], [f32(kv, rows, 2 * HD)])
        ordered = [*far_z, *ordered[z_part:]]
    pair_parts = call(
        functools.partial(sum_z_kernel, kv), "sum_z", ordered, [bf(rows, 2 * HD)] * kv
    )
    pair_parts = with_swaps(pair_parts)
    attended, query_grad = call(
        functools.partial(finish_q_kernel, kv),
        "finish_q",
        (own_group, *with_swaps(att_parts), *with_swaps(q_grad_parts)),
        [bf(rows, query_width)] * 2,
        [SMEM] + [VMEM] * (2 * kv),
    )
    key_grad, value_grad = call(
        functools.partial(finish_kv_kernel, kv),
        "finish_kv",
        (own_group, *pair_parts),
        [bf(rows, kv * HD)] * 2,
        [SMEM] + [VMEM] * kv,
    )
    return (
        attended.reshape(halves, block_rows, query_width),
        query_grad.reshape(halves, block_rows, query_width),
        key_grad.reshape(halves, block_rows, kv * HD),
        value_grad.reshape(halves, block_rows, kv * HD),
    )


def solution(mesh):
    split = P("ctx", "head", None)
    return jax.shard_map(
        shards,
        mesh=mesh,
        in_specs=(split, split, split, split, P()),
        out_specs=(split, split, split, split),
        check_vma=False,
    )
```

```python
import functools
import math

import jax
import jax.numpy as jnp
from jax import lax
from jax.experimental import pallas as pl
from jax.experimental.pallas import tpu as pltpu
from jax.sharding import PartitionSpec as P

HD = 128
CORES = 2
BF = jnp.bfloat16
F32 = jnp.float32
LOWEST = -1e30
FLOOR = -1e29
SCALING = 1.0 / math.sqrt(HD)
EXPO = SCALING * math.log2(math.e)

VMEM = pl.BlockSpec(memory_space=pltpu.VMEM)
SMEM = pl.BlockSpec(memory_space=pltpu.SMEM)


def swap(block, axis, mask):
    size = lax.axis_size(axis)
    return lax.ppermute(block, axis, [(i, i ^ mask) for i in range(size)])


def nbytes(arrays):
    return sum(math.prod(a.shape) * a.dtype.itemsize for a in arrays)


def after(blocks, earlier):
    if not earlier:
        return tuple(blocks)
    return lax.optimization_barrier((tuple(blocks), tuple(earlier)))[0]


def call(kernel, name, ins, outs, specs=None, scratch=(), extra=0, flops=0):
    limit = nbytes(ins) + nbytes(outs) + extra + (12 << 20)
    return pl.pallas_call(
        kernel,
        out_shape=list(outs),
        in_specs=specs or [VMEM] * len(ins),
        out_specs=[VMEM] * len(outs),
        scratch_shapes=list(scratch),
        compiler_params=pltpu.CompilerParams(vmem_limit_bytes=min(limit, 60 << 20)),
        cost_estimate=pl.CostEstimate(
            flops=flops, bytes_accessed=nbytes(ins) + nbytes(outs), transcendentals=0
        ),
        name=name,
    )(*ins)


def dot(left, right):
    return jnp.dot(left, right, preferred_element_type=F32)


def dot_rows(left, right):
    return lax.dot_general(left, right, (((1,), (1,)), ((), ())), preferred_element_type=F32)


def pack_q_kernel(kv, group_ref, query_ref, grad_ref, *out_refs):
    width = out_refs[0].shape[2]
    for g in range(kv):

        @pl.when(group_ref[0] == g)
        def _():
            for s in range(kv):
                cols = pl.ds((g ^ s) * width, width)
                out_refs[s][0] = query_ref[:, cols]
                out_refs[s][1] = grad_ref[:, cols]


def stack_kernel(count, *refs):
    ins, refs = refs[:count], refs[count:]
    passed = len(refs) // 2
    refs, out_ref = refs[:-1], refs[-1]
    for i, ref in enumerate(ins):
        out_ref[i] = ref[...]
    if passed:
        refs[-1][...] = refs[0][...]


class Plan:
    def __init__(self, kv, block_len, block_rows, rows, group, cores, z_devices, parts):
        self.kv, self.block_len, self.block_rows, self.rows = kv, block_len, block_rows, rows
        self.group, self.cores, self.parts, self.z_part = group, cores, parts, z_devices // parts
        self.blocks = rows // block_rows
        self.tile_rows = block_rows if block_rows % 16 == 0 else rows
        self.lanes = group * self.tile_rows
        self.query_rows = kv * group * rows
        self.chunk_keys = self.z_part * kv * rows
        self.tiles = [(s, start) for s in range(kv) for start in range(0, rows, self.tile_rows)]

    def zone(self, part):
        first = (self.parts - 1 - part) * self.z_part
        return range(first, first + self.z_part)

    def at(self, tile):
        return pl.ds(tile * self.lanes, self.lanes)

    def keys_at(self, i):
        return pl.ds(i * self.chunk_keys, self.chunk_keys)

    def gap(self, tile, info_ref):
        s, start = self.tiles[tile]
        head, ctx = info_ref[0], info_ref[1]
        row = lax.broadcasted_iota(jnp.int32, (1, self.lanes), 1) % self.tile_rows + start
        pos = jnp.zeros((1, self.lanes), jnp.int32)
        for b in range(start // self.block_rows, -(-(start + self.tile_rows) // self.block_rows)):
            first = info_ref[2 + ctx * self.blocks + b] * self.block_len + (head ^ s) * self.block_rows
            pos = jnp.where(row // self.block_rows == b, first + row % self.block_rows, pos)
        return pos - lax.broadcasted_iota(jnp.int32, (self.block_rows, self.lanes), 0)

    def masked(self, scores, gap, chunk, info_ref):
        head, ctx = info_ref[0], info_ref[1]
        a, core, part = chunk
        for j in range(self.chunk_keys // self.block_rows):
            m, rest = divmod(j, self.kv * self.blocks)
            s, b = divmod(rest, self.blocks)
            stored = (ctx ^ (self.zone(part)[m] * self.cores + core)) * self.blocks + b
            first = info_ref[2 + stored] * self.block_len + (head ^ (a * self.kv + s)) * self.block_rows
            block = scores[j * self.block_rows : (j + 1) * self.block_rows]
            yield j * self.block_rows, jnp.where(gap >= first, block, LOWEST)

    def turn(self, kv_refs, turned_ref):
        for i, ref in enumerate(kv_refs):
            turned_ref[:, self.keys_at(i)] = ref[...].reshape(self.chunk_keys, 2 * HD).T

    def keys(self, ref):
        return ref[:, :, :, :HD].reshape(self.chunk_keys, HD)

    def values(self, ref):
        return ref[:, :, :, HD:].reshape(self.chunk_keys, HD)

    def fold(self, block):
        return block.reshape(block.shape[0] // 8, 8, self.lanes)

    def scores(self, tile, chunks, kv_refs, q_t, e_ref, cols, info_ref):
        gap = self.gap(tile, info_ref)
        top = jnp.full((8, self.lanes), FLOOR, F32)
        for i, ref in enumerate(kv_refs):
            scores = dot(self.keys(ref), q_t)
            for row, part in self.masked(scores, gap, chunks[i], info_ref):
                e_ref[pl.ds(i * self.chunk_keys + row, part.shape[0]), cols] = part
                top = jnp.maximum(top, jnp.max(self.fold(part), axis=0))
        return jnp.max(top, axis=0, keepdims=True)

    def exponents(self, count, e_ref, cols, top):
        total = jnp.zeros((8, self.lanes), F32)
        for i in range(count):
            part = jnp.exp2(e_ref[self.keys_at(i), cols] * EXPO - top * EXPO)
            e_ref[self.keys_at(i), cols] = part
            total = total + jnp.sum(self.fold(part), axis=0)
        return jnp.sum(total, axis=0, keepdims=True)

    def store_heads(self, out_ref, tile, turned):
        s, start = self.tiles[tile]
        block = turned.T.astype(BF)
        for n in range(self.group):
            piece = block[n * self.tile_rows : (n + 1) * self.tile_rows]
            out_ref[pl.ds(start, self.tile_rows), pl.ds(n * HD, HD)] = piece

    def back(self, dkv_refs, p_ref, ds_ref, q_ref, do_ref):
        shape = (self.z_part, self.kv, self.rows, HD)
        for i, out_ref in enumerate(dkv_refs):
            at = self.keys_at(i)
            out_ref[:, :, :, :HD] = dot(ds_ref[at, :], q_ref[...]).astype(BF).reshape(shape)
            out_ref[:, :, :, HD:] = dot(p_ref[at, :], do_ref[...]).astype(BF).reshape(shape)


def forward_part(plan, chunks, info_ref, q_t, kv_refs, e_ref, top_ref, sum_ref, mix_ref, turned_ref):
    spans = [plan.at(tile) for tile in range(len(plan.tiles))]
    tops = [
        plan.scores(tile, chunks, kv_refs, q_t[:, at], e_ref, at, info_ref)
        for tile, at in enumerate(spans)
    ]
    plan.turn(kv_refs, turned_ref)
    for at, top in zip(spans, tops):
        top_ref[:, at] = top
        sum_ref[:, at] = plan.exponents(len(chunks), e_ref, at, top)
    for at in spans:
        mixed = jnp.zeros((HD, plan.lanes), F32)
        for i in range(len(chunks)):
            weights = e_ref[plan.keys_at(i), at].astype(BF)
            mixed = mixed + dot(turned_ref[pl.ds(HD, HD), plan.keys_at(i)], weights)
        mix_ref[:, at] = mixed


def turn_kernel(plan, info_ref, *refs):
    q_parts, (q_all, do_all, q_t, do_t) = refs[:-4], refs[-4:]
    for tile, (s, start) in enumerate(plan.tiles):
        span = pl.ds(start, plan.tile_rows)
        for n in range(plan.group):
            at = pl.ds(tile * plan.lanes + n * plan.tile_rows, plan.tile_rows)
            q_all[at, :] = q_parts[s][0, span, pl.ds(n * HD, HD)]
            do_all[at, :] = q_parts[s][1, span, pl.ds(n * HD, HD)]
        at = plan.at(tile)
        q_t[:, at] = q_all[at, :].T
        do_t[:, at] = do_all[at, :].T


def part_kernel(plan, chunks, info_ref, q_t, *refs):
    forward_part(plan, chunks, info_ref, q_t, refs[: len(chunks)], *refs[-5:])


def far_kernel(plan, chunks, others, info_ref, q_all, do_all, q_t, do_t, *refs):
    kv, count = plan.kv, len(chunks)
    partial, refs = [refs[3 * i : 3 * i + 3] for i in range(others)], refs[3 * others :]
    kv_refs, refs = refs[:count], refs[count:]
    att_refs, refs = refs[:kv], refs[kv:]
    scale_refs, (delta_ref, q_grad_ref), refs = refs[:others], refs[others : others + 2], refs[others + 2 :]
    dkv_refs, (turned_ref, e_ref, w_ref, p_ref, ds_ref) = refs[:-5], refs[-5:]
    spans = [plan.at(tile) for tile in range(len(plan.tiles))]
    tops = [
        plan.scores(tile, chunks, kv_refs, q_t[:, at], e_ref, at, info_ref)
        for tile, at in enumerate(spans)
    ]
    plan.turn(kv_refs, turned_ref)
    for at in spans:
        for i, ref in enumerate(kv_refs):
            w_ref[plan.keys_at(i), at] = dot(plan.values(ref), do_t[:, at])
    inverses, mixes = [], []
    for at, top in zip(spans, tops):
        for top_ref, _, _ in partial:
            top = jnp.maximum(top, top_ref[:, at])
        total = plan.exponents(count, e_ref, at, top)
        factors = [jnp.exp2((top_ref[:, at] - top) * EXPO) for top_ref, _, _ in partial]
        for factor, (_, sum_ref, _) in zip(factors, partial):
            total = total + factor * sum_ref[:, at]
        inverse = 1.0 / total
        for factor, scale_ref in zip(factors, scale_refs):
            scale_ref[:, at] = factor * inverse
        inverses.append(inverse)
    for at, inverse in zip(spans, inverses):
        mixed = jnp.zeros((HD, plan.lanes), F32)
        for scale_ref, (_, _, mix_ref) in zip(scale_refs, partial):
            mixed = mixed + mix_ref[:, at] * scale_ref[:, at]
        for i in range(count):
            probs = (e_ref[plan.keys_at(i), at] * inverse).astype(BF)
            p_ref[plan.keys_at(i), at] = probs
            mixed = mixed + dot(turned_ref[pl.ds(HD, HD), plan.keys_at(i)], probs)
        mixes.append(mixed.astype(BF).astype(F32))
    for at, mixed in zip(spans, mixes):
        delta_ref[:, at] = jnp.sum(do_t[:, at].astype(F32) * mixed, axis=0, keepdims=True)
    for at, inverse in zip(spans, inverses):
        q_grad = jnp.zeros((HD, plan.lanes), F32)
        for i in range(count):
            probs = e_ref[plan.keys_at(i), at] * inverse
            grad_s = (probs * (w_ref[plan.keys_at(i), at] - delta_ref[:, at])).astype(BF)
            ds_ref[plan.keys_at(i), at] = grad_s
            q_grad = q_grad + dot(turned_ref[pl.ds(0, HD), plan.keys_at(i)], grad_s)
        q_grad_ref[:, at] = q_grad
    plan.back(dkv_refs, p_ref, ds_ref, q_all, do_all)
    for tile, mixed in enumerate(mixes):
        plan.store_heads(att_refs[plan.tiles[tile][0]], tile, mixed)


def back_kernel(plan, rows_at, last, order, q_all, do_all, do_t, e_ref, scale_ref, delta_ref, q_grad_in, *refs):
    count = len(rows_at)
    kv_refs, refs = refs[:count], refs[count + order :]
    refs, (turned_ref, p_ref, ds_ref) = refs[:-3], refs[-3:]
    outs, dkv_refs = refs[:-count], refs[-count:]
    spans = [plan.at(tile) for tile in range(len(plan.tiles))]
    for at in spans:
        for i, ref in enumerate(kv_refs):
            probs = e_ref[plan.keys_at(rows_at[i]), at] * scale_ref[:, at]
            p_ref[plan.keys_at(i), at] = probs.astype(BF)
            grad_s = (probs * (dot(plan.values(ref), do_t[:, at]) - delta_ref[:, at])).astype(BF)
            ds_ref[plan.keys_at(i), at] = grad_s
    plan.turn(kv_refs, turned_ref)
    plan.back(dkv_refs, p_ref, ds_ref, q_all, do_all)
    for tile, at in enumerate(spans):
        q_grad = q_grad_in[:, at]
        for i in range(count):
            q_grad = q_grad + dot(turned_ref[pl.ds(0, HD), plan.keys_at(i)], ds_ref[plan.keys_at(i), at])
        if last:
            plan.store_heads(outs[plan.tiles[tile][0]], tile, q_grad * SCALING)
        else:
            outs[0][:, at] = q_grad


def add_kernel(*refs):
    total = refs[0][...].astype(F32)
    for ref in refs[1:-1]:
        total = total + ref[...].astype(F32)
    refs[-1][...] = total.astype(BF)


def sum_heads_kernel(parts, *refs):
    for m_z, out_ref in enumerate(refs[parts:]):
        total = refs[0][m_z].astype(F32)
        for ref in refs[1:parts]:
            total = total + ref[m_z].astype(F32)
        out_ref[...] = total.astype(BF)


def sum_z_kernel(kv, *refs):
    ins, outs = refs[:-kv], refs[-kv:]
    for s, out_ref in enumerate(outs):
        total = ins[0][s].astype(F32)
        for ref in ins[1:]:
            total = total + ref[s].astype(F32)
        out_ref[...] = total.astype(BF)


def sum_far_kernel(*refs):
    total = refs[0][...].astype(F32)
    for ref in refs[1:-1]:
        total = total + ref[...].astype(F32)
    refs[-1][...] = total


def finish_kv_kernel(kv, group_ref, *refs):
    key_ref, value_ref = refs[kv:]
    for g in range(kv):

        @pl.when(group_ref[0] == g)
        def _():
            for s in range(kv):
                cols = pl.ds((g ^ s) * HD, HD)
                key_ref[:, cols] = (refs[s][:, :HD].astype(F32) * SCALING).astype(BF)
                value_ref[:, cols] = refs[s][:, HD:]


def finish_q_kernel(kv, group_ref, *refs):
    att_ref, grad_ref = refs[2 * kv :]
    width = refs[0].shape[1]
    for g in range(kv):

        @pl.when(group_ref[0] == g)
        def _():
            for s in range(kv):
                cols = pl.ds((g ^ s) * width, width)
                att_ref[:, cols] = refs[s][...]
                grad_ref[:, cols] = refs[kv + s][...]


def shards(queries, key_vectors, value_vectors, out_grad, block_order):
    heads_devices = lax.axis_size("head")
    ctx_devices = lax.axis_size("ctx")
    halves, block_rows, query_width = queries.shape
    kv = key_vectors.shape[2] // HD
    rows = halves * block_rows
    width = query_width // kv
    cores = CORES if ctx_devices % CORES == 0 else 1
    z_devices = ctx_devices // cores
    spans = heads_devices // kv
    parts = 2 if z_devices % 2 == 0 else 1
    plan = Plan(kv, block_rows * heads_devices, block_rows, rows, width // HD, cores, z_devices, parts)
    z_part = plan.z_part
    head = lax.axis_index("head").astype(jnp.int32)
    place = jnp.stack([head, lax.axis_index("ctx").astype(jnp.int32)])
    info = jnp.concatenate([place, block_order])
    own_group = (head % kv).reshape(1)
    queries = queries.reshape(rows, query_width)
    out_grad = out_grad.reshape(rows, query_width)
    key_vectors = key_vectors.reshape(rows, kv * HD)
    value_vectors = value_vectors.reshape(rows, kv * HD)

    def bf(*dims):
        return jax.ShapeDtypeStruct(dims, BF)

    def f32(*dims):
        return jax.ShapeDtypeStruct(dims, F32)

    def with_swaps(blocks):
        return [blocks[0]] + [swap(blocks[s], "head", s) for s in range(1, kv)]

    dkv = bf(z_part, kv, rows, 2 * HD)

    def of_head(g):
        picked = []
        for block in (key_vectors, value_vectors):
            out = block[:, :HD]
            for i in range(1, kv):
                out = jnp.where(g == i, block[:, i * HD : (i + 1) * HD], out)
            picked.append(out)
        return jnp.concatenate(picked, axis=1)

    piece = jnp.stack(with_swaps([of_head((head % kv) ^ s) for s in range(kv)]))
    q_parts = call(
        functools.partial(pack_q_kernel, kv),
        "pack_q",
        (own_group, queries, out_grad),
        [bf(2, rows, width)] * kv,
        [SMEM, VMEM, VMEM],
    )
    pieces = [swap(piece, "ctx", m * cores) for m in reversed(range(1, z_devices))]
    pieces = [piece] + pieces[::-1]
    q_parts = with_swaps(q_parts)
    query_rows = plan.query_rows
    q_all, do_all, q_t, do_t = call(
        functools.partial(turn_kernel, plan),
        "turn",
        (info, *q_parts),
        [bf(query_rows, HD)] * 2 + [bf(HD, query_rows)] * 2,
        [SMEM] + [VMEM] * kv,
    )
    column, handed, order = [None] * parts, [None] * parts, []
    for p in reversed(range(parts)):
        parcels = [pieces[m] for m in plan.zone(p)]
        extra = [column[p + 1], *order] if order else []
        *handed_on, column[p] = call(
            functools.partial(stack_kernel, len(parcels)),
            "stack",
            (*parcels, *extra),
            [dkv] * (1 + bool(extra)),
        )
        handed[p] = column[p]
        if extra:
            handed[p + 1] = handed_on[0]
        order = [q_t] if p else []
    columns = [[swap(half, "head", a * kv) for half in column] for a in range(1, spans)]
    near_kv = [column] + [[swap(half, "ctx", core) for half in handed] for core in range(1, cores)]
    near_flat = [half for pair in near_kv for half in pair]
    each = range(parts)
    near_chunks = [(0, core, p) for core in range(cores) for p in each]
    mid_chunks = [(a, 0, p) for a in range(1, spans) for p in each]
    far_chunks = [(a, core, p) for a in range(1, spans) for core in range(1, cores) for p in each]

    keys = plan.chunk_keys
    query_rows = plan.query_rows
    row, column_out = f32(1, query_rows), f32(HD, query_rows)

    def forward(name, chunks, kv_refs, order):
        size = len(chunks) * keys
        return call(
            functools.partial(part_kernel, plan, chunks),
            name,
            (info, q_t, *kv_refs, *order),
            [f32(size, query_rows), row, row, column_out],
            [SMEM] + [VMEM] * (1 + len(kv_refs) + len(order)),
            [pltpu.VMEM((2 * HD, size), BF)],
            size * 4 * HD,
            8 * size * query_rows * HD,
        )

    mids, order = [None] * parts, []
    for p in reversed(each):
        if p + 1 < parts or parts == 1:
            near_e, *near = forward("attend_near", near_chunks, near_flat, order)
            order = [near[0]]
            for pair in columns:
                pair[p] = after([pair[p]], order)[0]
        mids[p] = forward("attend_mid", [c for c in mid_chunks if c[2] == p], [pair[p] for pair in columns], order)
        order = [mids[p][1]]
    far_kv = [swap(pair[p], "ctx", core) for pair in columns for core in range(1, cores) for p in each]
    far_keys = len(far_kv) * keys
    outs = call(
        functools.partial(far_kernel, plan, far_chunks, 1 + parts),
        "attend_far",
        (info, q_all, do_all, q_t, do_t, *near, *[r for mid in mids for r in mid[1:]], *far_kv),
        [bf(rows, width)] * kv + [row] * (2 + parts) + [column_out] + [dkv] * len(far_kv),
        [SMEM] + [VMEM] * (7 + 3 * parts + len(far_kv)),
        [
            pltpu.VMEM((2 * HD, far_keys), BF),
            pltpu.VMEM((far_keys, query_rows), F32),
            pltpu.VMEM((far_keys, query_rows), F32),
            pltpu.VMEM((far_keys, query_rows), BF),
            pltpu.VMEM((far_keys, query_rows), BF),
        ],
        far_keys * (4 * HD + 12 * query_rows),
        16 * far_keys * query_rows * HD,
    )
    att_parts, outs = outs[:kv], outs[kv:]
    (near_scale, *mid_scales), outs = outs[: 1 + parts], outs[1 + parts :]
    (delta, q_grad), far_dkv = outs[:2], outs[2:]

    def back(rows_at, last, e, scale, q_grad, kv_refs, order):
        count = len(rows_at)
        q_outs = [bf(rows, width)] * kv if last else [column_out]
        outs = call(
            functools.partial(back_kernel, plan, rows_at, last, len(order)),
            "attend_back",
            (q_all, do_all, do_t, e, scale, delta, q_grad, *kv_refs, *order),
            q_outs + [dkv] * count,
            None,
            [
                pltpu.VMEM((2 * HD, count * keys), BF),
                pltpu.VMEM((count * keys, query_rows), BF),
                pltpu.VMEM((count * keys, query_rows), BF),
            ],
            count * keys * (4 * HD + 4 * query_rows),
            12 * count * keys * query_rows * HD,
        )
        return outs[: len(q_outs)], outs[len(q_outs) :]

    sums = [[] for _ in range(parts)]
    totals = []
    for p in reversed(each):
        mid_kv = [pair[p] for pair in columns]
        (q_grad,), mid_dkv = back(
            list(range(len(mid_kv))), False, mids[p][0], mid_scales[p], q_grad, mid_kv, []
        )
        for a in range(spans - 1):
            both = [mid_dkv[a]]
            for core in range(1, cores):
                ours = far_dkv[(a * (cores - 1) + core - 1) * parts + p]
                both.append(swap(ours, "ctx", core))
            totals += call(add_kernel, "sum_cores", after(both, totals[-1:]), [dkv])
            sums[p].append(swap(totals[-1], "head", (a + 1) * kv))
    order = [swap(totals[-1][0, 0, :, :HD], "ctx", 1)] if cores > 1 else []
    for core in reversed(range(cores)):
        outs, parts_dkv = back(
            [core * parts + p for p in each], core == 0, near_e, near_scale, q_grad, near_kv[core], order
        )
        q_grad = outs[0]
        for p in range(parts):
            sums[p].append(swap(parts_dkv[p], "ctx", core) if core else parts_dkv[p])
    q_grad_parts = outs[:kv]
    z_parts = [None] * z_devices
    for p in range(parts):
        totals = call(
            functools.partial(sum_heads_kernel, len(sums[p])),
            "sum_heads",
            sums[p],
            [bf(kv, rows, 2 * HD)] * z_part,
        )

        for m, total in zip(plan.zone(p), totals):
            z_parts[m] = swap(total, "ctx", m * cores) if m else total
    ordered = [z_parts[m] for p in each for m in plan.zone(p)]
    if parts > 1:
        far_z = call(sum_far_kernel, "sum_far_z", ordered[:z_part], [f32(kv, rows, 2 * HD)], flops=1 << 32)
        ordered = [*far_z, *ordered[z_part:]]
    pair_parts = call(
        functools.partial(sum_z_kernel, kv), "sum_z", ordered, [bf(rows, 2 * HD)] * kv
    )
    pair_parts = with_swaps(pair_parts)
    attended, query_grad = call(
        functools.partial(finish_q_kernel, kv),
        "finish_q",
        (own_group, *with_swaps(att_parts), *with_swaps(q_grad_parts)),
        [bf(rows, query_width)] * 2,
        [SMEM] + [VMEM] * (2 * kv),
    )
    key_grad, value_grad = call(
        functools.partial(finish_kv_kernel, kv),
        "finish_kv",
        (own_group, *pair_parts),
        [bf(rows, kv * HD)] * 2,
        [SMEM] + [VMEM] * kv,
    )
    return (
        attended.reshape(halves, block_rows, query_width),
        query_grad.reshape(halves, block_rows, query_width),
        key_grad.reshape(halves, block_rows, kv * HD),
        value_grad.reshape(halves, block_rows, kv * HD),
    )


def solution(mesh):
    split = P("ctx", "head", None)
    return jax.shard_map(
        shards,
        mesh=mesh,
        in_specs=(split, split, split, split, P()),
        out_specs=(split, split, split, split),
        check_vma=False,
    )
```

```python
import functools
import math

import jax
import jax.numpy as jnp
from jax import lax
from jax.experimental import pallas as pl
from jax.experimental.pallas import tpu as pltpu
from jax.sharding import PartitionSpec as P

HD = 128
CORES = 2
BF = jnp.bfloat16
F32 = jnp.float32
LOWEST = -1e30
FLOOR = -1e29
SCALING = 1.0 / math.sqrt(HD)
EXPO = SCALING * math.log2(math.e)

VMEM = pl.BlockSpec(memory_space=pltpu.VMEM)
SMEM = pl.BlockSpec(memory_space=pltpu.SMEM)


def swap(block, axis, mask):
    size = lax.axis_size(axis)
    return lax.ppermute(block, axis, [(i, i ^ mask) for i in range(size)])


def nbytes(arrays):
    return sum(math.prod(a.shape) * a.dtype.itemsize for a in arrays)


def after(blocks, earlier):
    if not earlier:
        return tuple(blocks)
    return lax.optimization_barrier((tuple(blocks), tuple(earlier)))[0]


def call(kernel, name, ins, outs, specs=None, scratch=(), extra=0, flops=0):
    limit = nbytes(ins) + nbytes(outs) + extra + (12 << 20)
    return pl.pallas_call(
        kernel,
        out_shape=list(outs),
        in_specs=specs or [VMEM] * len(ins),
        out_specs=[VMEM] * len(outs),
        scratch_shapes=list(scratch),
        compiler_params=pltpu.CompilerParams(vmem_limit_bytes=min(limit, 60 << 20)),
        cost_estimate=pl.CostEstimate(
            flops=flops, bytes_accessed=nbytes(ins) + nbytes(outs), transcendentals=0
        ),
        name=name,
    )(*ins)


def dot(left, right):
    return jnp.dot(left, right, preferred_element_type=F32)


def dot_rows(left, right):
    return lax.dot_general(left, right, (((1,), (1,)), ((), ())), preferred_element_type=F32)


def pack_q_kernel(kv, group_ref, query_ref, grad_ref, *out_refs):
    width = out_refs[0].shape[2]
    for g in range(kv):

        @pl.when(group_ref[0] == g)
        def _():
            for s in range(kv):
                cols = pl.ds((g ^ s) * width, width)
                out_refs[s][0] = query_ref[:, cols]
                out_refs[s][1] = grad_ref[:, cols]


def stack_kernel(count, *refs):
    ins, refs = refs[:count], refs[count:]
    passed = len(refs) // 2
    refs, out_ref = refs[:-1], refs[-1]
    for i, ref in enumerate(ins):
        out_ref[i] = ref[...]
    if passed:
        refs[-1][...] = refs[0][...]


class Plan:
    def __init__(self, kv, block_len, block_rows, rows, group, cores, z_devices, parts):
        self.kv, self.block_len, self.block_rows, self.rows = kv, block_len, block_rows, rows
        self.group, self.cores, self.parts, self.z_part = group, cores, parts, z_devices // parts
        self.blocks = rows // block_rows
        self.tile_rows = block_rows if block_rows % 16 == 0 else rows
        self.lanes = group * self.tile_rows
        self.query_rows = kv * group * rows
        self.chunk_keys = self.z_part * kv * rows
        self.slices = self.chunk_keys // block_rows
        self.tiles = [(s, start) for s in range(kv) for start in range(0, rows, self.tile_rows)]

    def zone(self, part):
        first = (self.parts - 1 - part) * self.z_part
        return range(first, first + self.z_part)

    def at(self, tile):
        return pl.ds(tile * self.lanes, self.lanes)

    def keys_at(self, i):
        return pl.ds(i * self.chunk_keys, self.chunk_keys)

    def gap(self, tile, info_ref):
        s, start = self.tiles[tile]
        head, ctx = info_ref[0], info_ref[1]
        row = lax.broadcasted_iota(jnp.int32, (1, self.lanes), 1) % self.tile_rows + start
        pos = jnp.zeros((1, self.lanes), jnp.int32)
        for b in range(start // self.block_rows, -(-(start + self.tile_rows) // self.block_rows)):
            first = info_ref[2 + ctx * self.blocks + b] * self.block_len + (head ^ s) * self.block_rows
            pos = jnp.where(row // self.block_rows == b, first + row % self.block_rows, pos)
        return pos - lax.broadcasted_iota(jnp.int32, (self.block_rows, self.lanes), 0)

    def firsts(self, chunk, info_ref):
        head, ctx = info_ref[0], info_ref[1]
        a, core, part = chunk
        for j in range(self.slices):
            m, rest = divmod(j, self.kv * self.blocks)
            s, b = divmod(rest, self.blocks)
            stored = (ctx ^ (self.zone(part)[m] * self.cores + core)) * self.blocks + b
            yield info_ref[2 + stored] * self.block_len + (head ^ (a * self.kv + s)) * self.block_rows

    def first_at(self, chunk):
        a, core, part = chunk
        return ((a * self.cores + core) * self.parts + part) * self.slices

    def masked(self, scores, gap, chunk, first_ref):
        for j in range(self.slices):
            row = j * self.block_rows
            first = first_ref[pl.ds(self.first_at(chunk) + j, 1), :]
            yield row, jnp.where(gap >= first, scores[row : row + self.block_rows], LOWEST)

    def turn(self, kv_refs, turned_ref):
        for i, ref in enumerate(kv_refs):
            turned_ref[:, self.keys_at(i)] = ref[...].reshape(self.chunk_keys, 2 * HD).T

    def keys(self, ref):
        return ref[:, :, :, :HD].reshape(self.chunk_keys, HD)

    def values(self, ref):
        return ref[:, :, :, HD:].reshape(self.chunk_keys, HD)

    def fold(self, block):
        return block.reshape(block.shape[0] // 8, 8, self.lanes)

    def scores(self, tile, chunks, kv_refs, q_t, e_ref, cols, gap_ref, first_ref):
        gap = gap_ref[pl.ds(tile * self.block_rows, self.block_rows), :]
        top = jnp.full((8, self.lanes), FLOOR, F32)
        for i, ref in enumerate(kv_refs):
            scores = dot(self.keys(ref), q_t)
            for row, part in self.masked(scores, gap, chunks[i], first_ref):
                e_ref[pl.ds(i * self.chunk_keys + row, part.shape[0]), cols] = part
                top = jnp.maximum(top, jnp.max(self.fold(part), axis=0))
        return jnp.max(top, axis=0, keepdims=True)

    def exponents(self, count, e_ref, cols, top):
        total = jnp.zeros((8, self.lanes), F32)
        for i in range(count):
            part = jnp.exp2(e_ref[self.keys_at(i), cols] * EXPO - top * EXPO)
            e_ref[self.keys_at(i), cols] = part
            total = total + jnp.sum(self.fold(part), axis=0)
        return jnp.sum(total, axis=0, keepdims=True)

    def store_heads(self, out_ref, kind, tile, turned):
        s, start = self.tiles[tile]
        block = turned.T.astype(BF)
        for n in range(self.group):
            piece = block[n * self.tile_rows : (n + 1) * self.tile_rows]
            out_ref[kind, pl.ds(start, self.tile_rows), pl.ds(n * HD, HD)] = piece

    def back(self, dkv_refs, p_ref, ds_ref, q_ref, do_ref):
        shape = (self.z_part, self.kv, self.rows, HD)
        for i, out_ref in enumerate(dkv_refs):
            at = self.keys_at(i)
            out_ref[:, :, :, :HD] = dot(ds_ref[at, :], q_ref[...]).astype(BF).reshape(shape)
            out_ref[:, :, :, HD:] = dot(p_ref[at, :], do_ref[...]).astype(BF).reshape(shape)


def forward_part(plan, chunks, gap_ref, first_ref, q_t, kv_refs, e_ref, top_ref, sum_ref, mix_ref, turned_ref):
    spans = [plan.at(tile) for tile in range(len(plan.tiles))]
    tops = [
        plan.scores(tile, chunks, kv_refs, q_t[:, at], e_ref, at, gap_ref, first_ref)
        for tile, at in enumerate(spans)
    ]
    plan.turn(kv_refs, turned_ref)
    for at, top in zip(spans, tops):
        top_ref[:, at] = top
        sum_ref[:, at] = plan.exponents(len(chunks), e_ref, at, top)
    for at in spans:
        mixed = jnp.zeros((HD, plan.lanes), F32)
        for i in range(len(chunks)):
            weights = e_ref[plan.keys_at(i), at].astype(BF)
            mixed = mixed + dot(turned_ref[pl.ds(HD, HD), plan.keys_at(i)], weights)
        mix_ref[:, at] = mixed


def turn_kernel(plan, chunks, info_ref, *refs):
    q_parts, (q_all, do_all, q_t, do_t, gap_ref, first_ref) = refs[:-6], refs[-6:]
    for tile, (s, start) in enumerate(plan.tiles):
        span = pl.ds(start, plan.tile_rows)
        for n in range(plan.group):
            at = pl.ds(tile * plan.lanes + n * plan.tile_rows, plan.tile_rows)
            q_all[at, :] = q_parts[s][0, span, pl.ds(n * HD, HD)]
            do_all[at, :] = q_parts[s][1, span, pl.ds(n * HD, HD)]
        at = plan.at(tile)
        q_t[:, at] = q_all[at, :].T
        do_t[:, at] = do_all[at, :].T
        gap_ref[pl.ds(tile * plan.block_rows, plan.block_rows), :] = plan.gap(tile, info_ref)
    for chunk in chunks:
        for j, first in enumerate(plan.firsts(chunk, info_ref)):
            first_ref[pl.ds(plan.first_at(chunk) + j, 1), :] = jnp.full((1, plan.lanes), first, jnp.int32)


def part_kernel(plan, chunks, gap_ref, first_ref, q_t, *refs):
    forward_part(plan, chunks, gap_ref, first_ref, q_t, refs[: len(chunks)], *refs[-5:])


def far_kernel(plan, chunks, others, gap_ref, first_ref, q_all, do_all, q_t, do_t, *refs):
    count = len(chunks)
    partial, refs = [refs[3 * i : 3 * i + 3] for i in range(others)], refs[3 * others :]
    kv_refs, refs = refs[:count], refs[count:]
    scale_refs, refs = refs[:others], refs[others:]
    (delta_ref, mixed_ref, q_grad_ref), refs = refs[:3], refs[3:]
    dkv_refs, (turned_ref, e_ref, w_ref, p_ref, ds_ref) = refs[:-5], refs[-5:]
    spans = [plan.at(tile) for tile in range(len(plan.tiles))]
    tops = [
        plan.scores(tile, chunks, kv_refs, q_t[:, at], e_ref, at, gap_ref, first_ref)
        for tile, at in enumerate(spans)
    ]
    plan.turn(kv_refs, turned_ref)
    for at in spans:
        for i, ref in enumerate(kv_refs):
            w_ref[plan.keys_at(i), at] = dot(plan.values(ref), do_t[:, at])
    inverses = []
    for at, top in zip(spans, tops):
        for top_ref, _, _ in partial:
            top = jnp.maximum(top, top_ref[:, at])
        total = plan.exponents(count, e_ref, at, top)
        factors = [jnp.exp2((top_ref[:, at] - top) * EXPO) for top_ref, _, _ in partial]
        for factor, (_, sum_ref, _) in zip(factors, partial):
            total = total + factor * sum_ref[:, at]
        inverse = 1.0 / total
        for factor, scale_ref in zip(factors, scale_refs):
            scale_ref[:, at] = factor * inverse
        inverses.append(inverse)
    for at, inverse in zip(spans, inverses):
        mixed = jnp.zeros((HD, plan.lanes), F32)
        for scale_ref, (_, _, mix_ref) in zip(scale_refs, partial):
            mixed = mixed + mix_ref[:, at] * scale_ref[:, at]
        for i in range(count):
            probs = (e_ref[plan.keys_at(i), at] * inverse).astype(BF)
            p_ref[plan.keys_at(i), at] = probs
            mixed = mixed + dot(turned_ref[pl.ds(HD, HD), plan.keys_at(i)], probs)
        mixed = mixed.astype(BF)
        mixed_ref[:, at] = mixed
        delta_ref[:, at] = jnp.sum(do_t[:, at].astype(F32) * mixed.astype(F32), axis=0, keepdims=True)
    for at, inverse in zip(spans, inverses):
        q_grad = jnp.zeros((HD, plan.lanes), F32)
        for i in range(count):
            probs = e_ref[plan.keys_at(i), at] * inverse
            grad_s = (probs * (w_ref[plan.keys_at(i), at] - delta_ref[:, at])).astype(BF)
            ds_ref[plan.keys_at(i), at] = grad_s
            q_grad = q_grad + dot(turned_ref[pl.ds(0, HD), plan.keys_at(i)], grad_s)
        q_grad_ref[:, at] = q_grad
    plan.back(dkv_refs, p_ref, ds_ref, q_all, do_all)


def back_kernel(plan, rows_at, last, order, q_all, do_all, do_t, e_ref, scale_ref, delta_ref, q_grad_in, *refs):
    count = len(rows_at)
    mixed_ref, refs = refs[:last], refs[last:]
    kv_refs, refs = refs[:count], refs[count + order :]
    refs, (turned_ref, p_ref, ds_ref) = refs[:-3], refs[-3:]
    outs, dkv_refs = refs[:-count], refs[-count:]
    spans = [plan.at(tile) for tile in range(len(plan.tiles))]
    for at in spans:
        for i, ref in enumerate(kv_refs):
            probs = e_ref[plan.keys_at(rows_at[i]), at] * scale_ref[:, at]
            p_ref[plan.keys_at(i), at] = probs.astype(BF)
            grad_s = (probs * (dot(plan.values(ref), do_t[:, at]) - delta_ref[:, at])).astype(BF)
            ds_ref[plan.keys_at(i), at] = grad_s
    plan.turn(kv_refs, turned_ref)
    plan.back(dkv_refs, p_ref, ds_ref, q_all, do_all)
    for tile, at in enumerate(spans):
        q_grad = q_grad_in[:, at]
        for i in range(count):
            q_grad = q_grad + dot(turned_ref[pl.ds(0, HD), plan.keys_at(i)], ds_ref[plan.keys_at(i), at])
        if last:
            out_ref = outs[plan.tiles[tile][0]]
            plan.store_heads(out_ref, 0, tile, mixed_ref[0][:, at].astype(F32))
            plan.store_heads(out_ref, 1, tile, q_grad * SCALING)
        else:
            outs[0][:, at] = q_grad


def add_kernel(*refs):
    total = refs[0][...].astype(F32)
    for ref in refs[1:-1]:
        total = total + ref[...].astype(F32)
    refs[-1][...] = total.astype(BF)


def sum_heads_kernel(parts, *refs):
    for m_z, out_ref in enumerate(refs[parts:]):
        total = refs[0][m_z].astype(F32)
        for ref in refs[1:parts]:
            total = total + ref[m_z].astype(F32)
        out_ref[...] = total.astype(BF)


def sum_z_kernel(kv, *refs):
    ins, outs = refs[:-kv], refs[-kv:]
    for s, out_ref in enumerate(outs):
        total = ins[0][s].astype(F32)
        for ref in ins[1:]:
            total = total + ref[s].astype(F32)
        out_ref[...] = total.astype(BF)


def sum_far_kernel(*refs):
    total = refs[0][...].astype(F32)
    for ref in refs[1:-1]:
        total = total + ref[...].astype(F32)
    refs[-1][...] = total


def finish_kv_kernel(kv, group_ref, *refs):
    key_ref, value_ref = refs[kv + 1 :]
    for g in range(kv):

        @pl.when(group_ref[0] == g)
        def _():
            for s in range(kv):
                cols = pl.ds((g ^ s) * HD, HD)
                key_ref[:, cols] = (refs[s][:, :HD].astype(F32) * SCALING).astype(BF)
                value_ref[:, cols] = refs[s][:, HD:]


def finish_q_kernel(kv, group_ref, *refs):
    att_ref, grad_ref, done_ref = refs[kv:]
    done_ref[...] = jnp.zeros_like(done_ref)
    width = refs[0].shape[2]
    for g in range(kv):

        @pl.when(group_ref[0] == g)
        def _():
            for s in range(kv):
                cols = pl.ds((g ^ s) * width, width)
                att_ref[:, cols] = refs[s][0]
                grad_ref[:, cols] = refs[s][1]


def shards(queries, key_vectors, value_vectors, out_grad, block_order):
    heads_devices = lax.axis_size("head")
    ctx_devices = lax.axis_size("ctx")
    halves, block_rows, query_width = queries.shape
    kv = key_vectors.shape[2] // HD
    rows = halves * block_rows
    width = query_width // kv
    cores = CORES if ctx_devices % CORES == 0 else 1
    z_devices = ctx_devices // cores
    spans = heads_devices // kv
    parts = 2 if z_devices % 2 == 0 else 1
    plan = Plan(kv, block_rows * heads_devices, block_rows, rows, width // HD, cores, z_devices, parts)
    z_part = plan.z_part
    head = lax.axis_index("head").astype(jnp.int32)
    place = jnp.stack([head, lax.axis_index("ctx").astype(jnp.int32)])
    info = jnp.concatenate([place, block_order])
    own_group = (head % kv).reshape(1)
    queries = queries.reshape(rows, query_width)
    out_grad = out_grad.reshape(rows, query_width)
    key_vectors = key_vectors.reshape(rows, kv * HD)
    value_vectors = value_vectors.reshape(rows, kv * HD)

    def bf(*dims):
        return jax.ShapeDtypeStruct(dims, BF)

    def f32(*dims):
        return jax.ShapeDtypeStruct(dims, F32)

    def i32(*dims):
        return jax.ShapeDtypeStruct(dims, jnp.int32)

    def with_swaps(blocks):
        return [blocks[0]] + [swap(blocks[s], "head", s) for s in range(1, kv)]

    dkv = bf(z_part, kv, rows, 2 * HD)

    def of_head(g):
        picked = []
        for block in (key_vectors, value_vectors):
            out = block[:, :HD]
            for i in range(1, kv):
                out = jnp.where(g == i, block[:, i * HD : (i + 1) * HD], out)
            picked.append(out)
        return jnp.concatenate(picked, axis=1)

    piece = jnp.stack(with_swaps([of_head((head % kv) ^ s) for s in range(kv)]))
    q_parts = call(
        functools.partial(pack_q_kernel, kv),
        "pack_q",
        (own_group, queries, out_grad),
        [bf(2, rows, width)] * kv,
        [SMEM, VMEM, VMEM],
    )
    pieces = [swap(piece, "ctx", m * cores) for m in reversed(range(1, z_devices))]
    pieces = [piece] + pieces[::-1]
    q_parts = with_swaps(q_parts)
    query_rows = plan.query_rows
    chunks = [(a, core, p) for a in range(spans) for core in range(cores) for p in range(parts)]
    q_all, do_all, q_t, do_t, gap, firsts = call(
        functools.partial(turn_kernel, plan, chunks),
        "turn",
        (info, *q_parts),
        [
            *[bf(query_rows, HD)] * 2,
            *[bf(HD, query_rows)] * 2,
            i32(len(plan.tiles) * block_rows, plan.lanes),
            i32(len(chunks) * plan.slices, plan.lanes),
        ],
        [SMEM] + [VMEM] * kv,
    )
    column, handed, order = [None] * parts, [None] * parts, []
    for p in reversed(range(parts)):
        parcels = [pieces[m] for m in plan.zone(p)]
        extra = [column[p + 1], *order] if order else []
        *handed_on, column[p] = call(
            functools.partial(stack_kernel, len(parcels)),
            "stack",
            (*parcels, *extra),
            [dkv] * (1 + bool(extra)),
        )
        handed[p] = column[p]
        if extra:
            handed[p + 1] = handed_on[0]
        order = [q_t] if p else []
    columns = [[swap(half, "head", a * kv) for half in column] for a in range(1, spans)]
    near_kv = [column] + [[swap(half, "ctx", core) for half in handed] for core in range(1, cores)]
    near_flat = [half for pair in near_kv for half in pair]
    each = range(parts)
    near_chunks = [(0, core, p) for core in range(cores) for p in each]
    mid_chunks = [(a, 0, p) for a in range(1, spans) for p in each]
    far_chunks = [(a, core, p) for a in range(1, spans) for core in range(1, cores) for p in each]

    keys = plan.chunk_keys
    query_rows = plan.query_rows
    row, column_out = f32(1, query_rows), f32(HD, query_rows)

    def forward(name, chunks, kv_refs, order):
        size = len(chunks) * keys
        return call(
            functools.partial(part_kernel, plan, chunks),
            name,
            (gap, firsts, q_t, *kv_refs, *order),
            [f32(size, query_rows), row, row, column_out],
            None,
            [pltpu.VMEM((2 * HD, size), BF)],
            size * 4 * HD,
            8 * size * query_rows * HD,
        )

    mids, order = [None] * parts, []
    for p in reversed(each):
        if p + 1 < parts or parts == 1:
            near_e, *near = forward("attend_near", near_chunks, near_flat, order)
            order = [near[0]]
            for pair in columns:
                pair[p] = after([pair[p]], order)[0]
        mids[p] = forward("attend_mid", [c for c in mid_chunks if c[2] == p], [pair[p] for pair in columns], order)
        order = [mids[p][1]]
    far_kv = [swap(pair[p], "ctx", core) for pair in columns for core in range(1, cores) for p in each]
    far_keys = len(far_kv) * keys
    outs = call(
        functools.partial(far_kernel, plan, far_chunks, 1 + parts),
        "attend_far",
        (gap, firsts, q_all, do_all, q_t, do_t, *near, *[r for mid in mids for r in mid[1:]], *far_kv),
        [row] * (2 + parts) + [bf(HD, query_rows), column_out] + [dkv] * len(far_kv),
        None,
        [
            pltpu.VMEM((2 * HD, far_keys), BF),
            pltpu.VMEM((far_keys, query_rows), F32),
            pltpu.VMEM((far_keys, query_rows), F32),
            pltpu.VMEM((far_keys, query_rows), BF),
            pltpu.VMEM((far_keys, query_rows), BF),
        ],
        far_keys * (4 * HD + 12 * query_rows),
        16 * far_keys * query_rows * HD,
    )
    (near_scale, *mid_scales), outs = outs[: 1 + parts], outs[1 + parts :]
    (delta, mixed, q_grad), far_dkv = outs[:3], outs[3:]

    def back(rows_at, last, e, scale, q_grad, kv_refs, order):
        count = len(rows_at)
        q_outs = [bf(2, rows, width)] * kv if last else [column_out]
        outs = call(
            functools.partial(back_kernel, plan, rows_at, last, len(order)),
            "attend_back",
            (q_all, do_all, do_t, e, scale, delta, q_grad, *[mixed] * last, *kv_refs, *order),
            q_outs + [dkv] * count,
            None,
            [
                pltpu.VMEM((2 * HD, count * keys), BF),
                pltpu.VMEM((count * keys, query_rows), BF),
                pltpu.VMEM((count * keys, query_rows), BF),
            ],
            count * keys * (4 * HD + 4 * query_rows),
            12 * count * keys * query_rows * HD,
        )
        return outs[: len(q_outs)], outs[len(q_outs) :]

    sums = [[] for _ in range(parts)]
    totals = []
    for p in reversed(each):
        mid_kv = [pair[p] for pair in columns]
        (q_grad,), mid_dkv = back(
            list(range(len(mid_kv))), False, mids[p][0], mid_scales[p], q_grad, mid_kv, []
        )
        for a in range(spans - 1):
            both = [mid_dkv[a]]
            for core in range(1, cores):
                ours = far_dkv[(a * (cores - 1) + core - 1) * parts + p]
                both.append(swap(ours, "ctx", core))
            totals += call(add_kernel, "sum_cores", after(both, totals[-1:]), [dkv])
            sums[p].append(swap(totals[-1], "head", (a + 1) * kv))
    order = [swap(totals[-1][0, 0, :, :HD], "ctx", 1)] if cores > 1 else []
    for core in reversed(range(cores)):
        outs, parts_dkv = back(
            [core * parts + p for p in each], core == 0, near_e, near_scale, q_grad, near_kv[core], order
        )
        q_grad = outs[0]
        for p in range(parts):
            sums[p].append(swap(parts_dkv[p], "ctx", core) if core else parts_dkv[p])
    q_parts = outs[:kv]
    z_parts = [None] * z_devices
    for p in range(parts):
        totals = call(
            functools.partial(sum_heads_kernel, len(sums[p])),
            "sum_heads",
            sums[p],
            [bf(kv, rows, 2 * HD)] * z_part,
        )

        if p == parts - 1:
            q_parts = with_swaps(after(q_parts, totals[:1]))
        for m, total in zip(plan.zone(p), totals):
            z_parts[m] = swap(total, "ctx", m * cores) if m else total
    ordered = [z_parts[m] for p in each for m in plan.zone(p)]
    if parts > 1:
        far_z = call(sum_far_kernel, "sum_far_z", ordered[:z_part], [f32(kv, rows, 2 * HD)], flops=1 << 32)
        ordered = [*far_z, *ordered[z_part:]]
    pair_parts = call(
        functools.partial(sum_z_kernel, kv), "sum_z", ordered, [bf(rows, 2 * HD)] * kv
    )
    pair_parts = with_swaps(pair_parts)
    attended, query_grad, done = call(
        functools.partial(finish_q_kernel, kv),
        "finish_q",
        (own_group, *q_parts),
        [bf(rows, query_width)] * 2 + [f32(8, HD)],
        [SMEM] + [VMEM] * kv,
    )
    key_grad, value_grad = call(
        functools.partial(finish_kv_kernel, kv),
        "finish_kv",
        (own_group, *pair_parts, done),
        [bf(rows, kv * HD)] * 2,
        [SMEM] + [VMEM] * (kv + 1),
    )
    return (
        attended.reshape(halves, block_rows, query_width),
        query_grad.reshape(halves, block_rows, query_width),
        key_grad.reshape(halves, block_rows, kv * HD),
        value_grad.reshape(halves, block_rows, kv * HD),
    )


def solution(mesh):
    split = P("ctx", "head", None)
    return jax.shard_map(
        shards,
        mesh=mesh,
        in_specs=(split, split, split, split, P()),
        out_specs=(split, split, split, split),
        check_vma=False,
    )
```

```python
import functools
import math

import jax
import jax.numpy as jnp
from jax import lax
from jax.experimental import pallas as pl
from jax.experimental.pallas import tpu as pltpu
from jax.sharding import PartitionSpec as P

HD = 128
CORES = 2
BF = jnp.bfloat16
F32 = jnp.float32
LOWEST = -1e30
FLOOR = -1e29
SCALING = 1.0 / math.sqrt(HD)
EXPO = SCALING * math.log2(math.e)

VMEM = pl.BlockSpec(memory_space=pltpu.VMEM)
SMEM = pl.BlockSpec(memory_space=pltpu.SMEM)


def swap(block, axis, mask):
    size = lax.axis_size(axis)
    return lax.ppermute(block, axis, [(i, i ^ mask) for i in range(size)])


def nbytes(arrays):
    return sum(math.prod(a.shape) * a.dtype.itemsize for a in arrays)


def after(blocks, earlier):
    if not earlier:
        return tuple(blocks)
    return lax.optimization_barrier((tuple(blocks), tuple(earlier)))[0]


def call(kernel, name, ins, outs, specs=None, scratch=(), extra=0, flops=0):
    limit = nbytes(ins) + nbytes(outs) + extra + (12 << 20)
    return pl.pallas_call(
        kernel,
        out_shape=list(outs),
        in_specs=specs or [VMEM] * len(ins),
        out_specs=[VMEM] * len(outs),
        scratch_shapes=list(scratch),
        compiler_params=pltpu.CompilerParams(vmem_limit_bytes=min(limit, 60 << 20)),
        cost_estimate=pl.CostEstimate(
            flops=flops, bytes_accessed=nbytes(ins) + nbytes(outs), transcendentals=0
        ),
        name=name,
    )(*ins)


def dot(left, right):
    return jnp.dot(left, right, preferred_element_type=F32)


def dot_rows(left, right):
    return lax.dot_general(left, right, (((1,), (1,)), ((), ())), preferred_element_type=F32)


def pack_q_kernel(kv, group_ref, query_ref, grad_ref, *out_refs):
    width = out_refs[0].shape[2]
    for g in range(kv):

        @pl.when(group_ref[0] == g)
        def _():
            for s in range(kv):
                cols = pl.ds((g ^ s) * width, width)
                out_refs[s][0] = query_ref[:, cols]
                out_refs[s][1] = grad_ref[:, cols]


def stack_kernel(count, *refs):
    ins, refs = refs[:count], refs[count:]
    passed = len(refs) // 2
    refs, out_ref = refs[:-1], refs[-1]
    for i, ref in enumerate(ins):
        out_ref[i] = ref[...]
    if passed:
        refs[-1][...] = refs[0][...]


class Plan:
    def __init__(self, kv, block_len, block_rows, rows, group, cores, z_devices, parts):
        self.kv, self.block_len, self.block_rows, self.rows = kv, block_len, block_rows, rows
        self.group, self.cores, self.parts, self.z_part = group, cores, parts, z_devices // parts
        self.blocks = rows // block_rows
        self.tile_rows = block_rows if block_rows % 16 == 0 else rows
        self.lanes = group * self.tile_rows
        self.query_rows = kv * group * rows
        self.chunk_keys = self.z_part * kv * rows
        self.slices = self.chunk_keys // block_rows
        self.tiles = [(s, start) for s in range(kv) for start in range(0, rows, self.tile_rows)]

    def zone(self, part):
        first = (self.parts - 1 - part) * self.z_part
        return range(first, first + self.z_part)

    def at(self, tile):
        return pl.ds(tile * self.lanes, self.lanes)

    def keys_at(self, i):
        return pl.ds(i * self.chunk_keys, self.chunk_keys)

    def gap(self, tile, info_ref):
        s, start = self.tiles[tile]
        head, ctx = info_ref[0], info_ref[1]
        row = lax.broadcasted_iota(jnp.int32, (1, self.lanes), 1) % self.tile_rows + start
        pos = jnp.zeros((1, self.lanes), jnp.int32)
        for b in range(start // self.block_rows, -(-(start + self.tile_rows) // self.block_rows)):
            first = info_ref[2 + ctx * self.blocks + b] * self.block_len + (head ^ s) * self.block_rows
            pos = jnp.where(row // self.block_rows == b, first + row % self.block_rows, pos)
        return pos - lax.broadcasted_iota(jnp.int32, (self.block_rows, self.lanes), 0)

    def firsts(self, chunk, info_ref):
        head, ctx = info_ref[0], info_ref[1]
        a, core, part = chunk
        for j in range(self.slices):
            m, rest = divmod(j, self.kv * self.blocks)
            s, b = divmod(rest, self.blocks)
            stored = (ctx ^ (self.zone(part)[m] * self.cores + core)) * self.blocks + b
            yield info_ref[2 + stored] * self.block_len + (head ^ (a * self.kv + s)) * self.block_rows

    def first_at(self, chunk):
        a, core, part = chunk
        return ((a * self.cores + core) * self.parts + part) * self.slices

    def masked(self, scores, gap, chunk, first_ref):
        for j in range(self.slices):
            row = j * self.block_rows
            first = first_ref[pl.ds(self.first_at(chunk) + j, 1), :]
            yield row, jnp.where(gap >= first, scores[row : row + self.block_rows], LOWEST)

    def turn(self, kv_refs, turned_ref):
        for i, ref in enumerate(kv_refs):
            turned_ref[:, self.keys_at(i)] = ref[...].reshape(self.chunk_keys, 2 * HD).T

    def keys(self, ref):
        return ref[:, :, :, :HD].reshape(self.chunk_keys, HD)

    def values(self, ref):
        return ref[:, :, :, HD:].reshape(self.chunk_keys, HD)

    def fold(self, block):
        return block.reshape(block.shape[0] // 8, 8, self.lanes)

    def scores(self, tile, chunks, kv_refs, q_t, e_ref, cols, gap_ref, first_ref):
        gap = gap_ref[pl.ds(tile * self.block_rows, self.block_rows), :]
        top = jnp.full((8, self.lanes), FLOOR, F32)
        for i, ref in enumerate(kv_refs):
            scores = dot(self.keys(ref), q_t)
            for row, part in self.masked(scores, gap, chunks[i], first_ref):
                e_ref[pl.ds(i * self.chunk_keys + row, part.shape[0]), cols] = part
                top = jnp.maximum(top, jnp.max(self.fold(part), axis=0))
        return jnp.max(top, axis=0, keepdims=True)

    def exponents(self, count, e_ref, cols, top):
        total = jnp.zeros((8, self.lanes), F32)
        for i in range(count):
            part = jnp.exp2(e_ref[self.keys_at(i), cols] * EXPO - top * EXPO)
            e_ref[self.keys_at(i), cols] = part
            total = total + jnp.sum(self.fold(part), axis=0)
        return jnp.sum(total, axis=0, keepdims=True)

    def store_heads(self, out_ref, kind, tile, turned):
        s, start = self.tiles[tile]
        block = turned.T.astype(BF)
        for n in range(self.group):
            piece = block[n * self.tile_rows : (n + 1) * self.tile_rows]
            out_ref[kind, pl.ds(start, self.tile_rows), pl.ds(n * HD, HD)] = piece

    def back(self, dkv_refs, p_ref, ds_ref, q_ref, do_ref):
        shape = (self.z_part, self.kv, self.rows, HD)
        for i, out_ref in enumerate(dkv_refs):
            at = self.keys_at(i)
            out_ref[:, :, :, :HD] = dot(ds_ref[at, :], q_ref[...]).astype(BF).reshape(shape)
            out_ref[:, :, :, HD:] = dot(p_ref[at, :], do_ref[...]).astype(BF).reshape(shape)


def forward_part(plan, chunks, gap_ref, first_ref, q_t, kv_refs, e_ref, top_ref, sum_ref, mix_ref, turned_ref):
    spans = [plan.at(tile) for tile in range(len(plan.tiles))]
    tops = [
        plan.scores(tile, chunks, kv_refs, q_t[:, at], e_ref, at, gap_ref, first_ref)
        for tile, at in enumerate(spans)
    ]
    plan.turn(kv_refs, turned_ref)
    for at, top in zip(spans, tops):
        top_ref[:, at] = top
        sum_ref[:, at] = plan.exponents(len(chunks), e_ref, at, top)
    for at in spans:
        mixed = jnp.zeros((HD, plan.lanes), F32)
        for i in range(len(chunks)):
            weights = e_ref[plan.keys_at(i), at].astype(BF)
            mixed = mixed + dot(turned_ref[pl.ds(HD, HD), plan.keys_at(i)], weights)
        mix_ref[:, at] = mixed


def turn_kernel(plan, chunks, info_ref, *refs):
    q_parts, (q_all, do_all, q_t, do_t, gap_ref, first_ref) = refs[:-6], refs[-6:]
    for tile, (s, start) in enumerate(plan.tiles):
        span = pl.ds(start, plan.tile_rows)
        for n in range(plan.group):
            at = pl.ds(tile * plan.lanes + n * plan.tile_rows, plan.tile_rows)
            q_all[at, :] = q_parts[s][0, span, pl.ds(n * HD, HD)]
            do_all[at, :] = q_parts[s][1, span, pl.ds(n * HD, HD)]
        at = plan.at(tile)
        q_t[:, at] = q_all[at, :].T
        do_t[:, at] = do_all[at, :].T
        gap_ref[pl.ds(tile * plan.block_rows, plan.block_rows), :] = plan.gap(tile, info_ref)
    for chunk in chunks:
        for j, first in enumerate(plan.firsts(chunk, info_ref)):
            first_ref[pl.ds(plan.first_at(chunk) + j, 1), :] = jnp.full((1, plan.lanes), first, jnp.int32)


def part_kernel(plan, chunks, gap_ref, first_ref, q_t, *refs):
    forward_part(plan, chunks, gap_ref, first_ref, q_t, refs[: len(chunks)], *refs[-5:])


def far_kernel(plan, chunks, others, gap_ref, first_ref, q_all, do_all, q_t, do_t, *refs):
    count = len(chunks)
    partial, refs = [refs[3 * i : 3 * i + 3] for i in range(others)], refs[3 * others :]
    kv_refs, refs = refs[:count], refs[count:]
    scale_refs, refs = refs[:others], refs[others:]
    (delta_ref, mixed_ref, q_grad_ref), refs = refs[:3], refs[3:]
    dkv_refs, (turned_ref, e_ref, w_ref, p_ref, ds_ref) = refs[:-5], refs[-5:]
    spans = [plan.at(tile) for tile in range(len(plan.tiles))]
    tops = [
        plan.scores(tile, chunks, kv_refs, q_t[:, at], e_ref, at, gap_ref, first_ref)
        for tile, at in enumerate(spans)
    ]
    plan.turn(kv_refs, turned_ref)
    for at in spans:
        for i, ref in enumerate(kv_refs):
            w_ref[plan.keys_at(i), at] = dot(plan.values(ref), do_t[:, at])
    inverses = []
    for at, top in zip(spans, tops):
        for top_ref, _, _ in partial:
            top = jnp.maximum(top, top_ref[:, at])
        total = plan.exponents(count, e_ref, at, top)
        factors = [jnp.exp2((top_ref[:, at] - top) * EXPO) for top_ref, _, _ in partial]
        for factor, (_, sum_ref, _) in zip(factors, partial):
            total = total + factor * sum_ref[:, at]
        inverse = 1.0 / total
        for factor, scale_ref in zip(factors, scale_refs):
            scale_ref[:, at] = factor * inverse
        inverses.append(inverse)
    for at, inverse in zip(spans, inverses):
        mixed = jnp.zeros((HD, plan.lanes), F32)
        for scale_ref, (_, _, mix_ref) in zip(scale_refs, partial):
            mixed = mixed + mix_ref[:, at] * scale_ref[:, at]
        for i in range(count):
            probs = (e_ref[plan.keys_at(i), at] * inverse).astype(BF)
            p_ref[plan.keys_at(i), at] = probs
            mixed = mixed + dot(turned_ref[pl.ds(HD, HD), plan.keys_at(i)], probs)
        mixed = mixed.astype(BF)
        mixed_ref[:, at] = mixed
        delta_ref[:, at] = jnp.sum(do_t[:, at].astype(F32) * mixed.astype(F32), axis=0, keepdims=True)
    for at, inverse in zip(spans, inverses):
        q_grad = jnp.zeros((HD, plan.lanes), F32)
        for i in range(count):
            probs = e_ref[plan.keys_at(i), at] * inverse
            grad_s = (probs * (w_ref[plan.keys_at(i), at] - delta_ref[:, at])).astype(BF)
            ds_ref[plan.keys_at(i), at] = grad_s
            q_grad = q_grad + dot(turned_ref[pl.ds(0, HD), plan.keys_at(i)], grad_s)
        q_grad_ref[:, at] = q_grad
    plan.back(dkv_refs, p_ref, ds_ref, q_all, do_all)


def back_kernel(plan, rows_at, last, order, q_all, do_all, do_t, e_ref, scale_ref, delta_ref, q_grad_in, *refs):
    count = len(rows_at)
    mixed_ref, refs = refs[:last], refs[last:]
    kv_refs, refs = refs[:count], refs[count + order :]
    refs, (turned_ref, p_ref, ds_ref) = refs[:-3], refs[-3:]
    outs, dkv_refs = refs[:-count], refs[-count:]
    spans = [plan.at(tile) for tile in range(len(plan.tiles))]
    for at in spans:
        for i, ref in enumerate(kv_refs):
            probs = e_ref[plan.keys_at(rows_at[i]), at] * scale_ref[:, at]
            p_ref[plan.keys_at(i), at] = probs.astype(BF)
            grad_s = (probs * (dot(plan.values(ref), do_t[:, at]) - delta_ref[:, at])).astype(BF)
            ds_ref[plan.keys_at(i), at] = grad_s
    plan.turn(kv_refs, turned_ref)
    plan.back(dkv_refs, p_ref, ds_ref, q_all, do_all)
    for tile, at in enumerate(spans):
        q_grad = q_grad_in[:, at]
        for i in range(count):
            q_grad = q_grad + dot(turned_ref[pl.ds(0, HD), plan.keys_at(i)], ds_ref[plan.keys_at(i), at])
        if last:
            out_ref = outs[plan.tiles[tile][0]]
            plan.store_heads(out_ref, 0, tile, mixed_ref[0][:, at].astype(F32))
            plan.store_heads(out_ref, 1, tile, q_grad * SCALING)
        else:
            outs[0][:, at] = q_grad


def add_kernel(*refs):
    total = refs[0][...].astype(F32)
    for ref in refs[1:-1]:
        total = total + ref[...].astype(F32)
    refs[-1][...] = total.astype(BF)


def sum_heads_kernel(parts, *refs):
    for m_z, out_ref in enumerate(refs[parts:]):
        total = refs[0][m_z].astype(F32)
        for ref in refs[1:parts]:
            total = total + ref[m_z].astype(F32)
        out_ref[...] = total.astype(BF)


def sum_z_kernel(kv, *refs):
    ins, outs = refs[:-kv], refs[-kv:]
    for s, out_ref in enumerate(outs):
        total = ins[0][s].astype(F32)
        for ref in ins[1:]:
            total = total + ref[s].astype(F32)
        out_ref[...] = total.astype(BF)


def sum_far_kernel(*refs):
    total = refs[0][...].astype(F32)
    for ref in refs[1:-1]:
        total = total + ref[...].astype(F32)
    refs[-1][...] = total


def finish_kv_kernel(kv, group_ref, *refs):
    key_ref, value_ref = refs[kv + 1 :]
    for g in range(kv):

        @pl.when(group_ref[0] == g)
        def _():
            for s in range(kv):
                cols = pl.ds((g ^ s) * HD, HD)
                key_ref[:, cols] = (refs[s][:, :HD].astype(F32) * SCALING).astype(BF)
                value_ref[:, cols] = refs[s][:, HD:]


def finish_q_kernel(kv, group_ref, *refs):
    att_ref, grad_ref, done_ref = refs[kv:]
    done_ref[...] = jnp.zeros_like(done_ref)
    width = refs[0].shape[2]
    for g in range(kv):

        @pl.when(group_ref[0] == g)
        def _():
            for s in range(kv):
                cols = pl.ds((g ^ s) * width, width)
                att_ref[:, cols] = refs[s][0]
                grad_ref[:, cols] = refs[s][1]


def shards(queries, key_vectors, value_vectors, out_grad, block_order):
    heads_devices = lax.axis_size("head")
    ctx_devices = lax.axis_size("ctx")
    halves, block_rows, query_width = queries.shape
    kv = key_vectors.shape[2] // HD
    rows = halves * block_rows
    width = query_width // kv
    cores = CORES if ctx_devices % CORES == 0 else 1
    z_devices = ctx_devices // cores
    spans = heads_devices // kv
    parts = 2 if z_devices % 2 == 0 else 1
    plan = Plan(kv, block_rows * heads_devices, block_rows, rows, width // HD, cores, z_devices, parts)
    z_part = plan.z_part
    head = lax.axis_index("head").astype(jnp.int32)
    place = jnp.stack([head, lax.axis_index("ctx").astype(jnp.int32)])
    info = jnp.concatenate([place, block_order])
    own_group = (head % kv).reshape(1)
    queries = queries.reshape(rows, query_width)
    out_grad = out_grad.reshape(rows, query_width)
    key_vectors = key_vectors.reshape(rows, kv * HD)
    value_vectors = value_vectors.reshape(rows, kv * HD)

    def bf(*dims):
        return jax.ShapeDtypeStruct(dims, BF)

    def f32(*dims):
        return jax.ShapeDtypeStruct(dims, F32)

    def i32(*dims):
        return jax.ShapeDtypeStruct(dims, jnp.int32)

    def with_swaps(blocks):
        return [blocks[0]] + [swap(blocks[s], "head", s) for s in range(1, kv)]

    dkv = bf(z_part, kv, rows, 2 * HD)

    def of_head(g):
        picked = []
        for block in (key_vectors, value_vectors):
            out = block[:, :HD]
            for i in range(1, kv):
                out = jnp.where(g == i, block[:, i * HD : (i + 1) * HD], out)
            picked.append(out)
        return jnp.concatenate(picked, axis=1)

    piece = jnp.stack(with_swaps([of_head((head % kv) ^ s) for s in range(kv)]))
    q_parts = call(
        functools.partial(pack_q_kernel, kv),
        "pack_q",
        (own_group, queries, out_grad),
        [bf(2, rows, width)] * kv,
        [SMEM, VMEM, VMEM],
    )
    pieces = [swap(piece, "ctx", m * cores) for m in reversed(range(1, z_devices))]
    pieces = [piece] + pieces[::-1]
    q_parts = with_swaps(q_parts)
    query_rows = plan.query_rows
    chunks = [(a, core, p) for a in range(spans) for core in range(cores) for p in range(parts)]
    q_all, do_all, q_t, do_t, gap, firsts = call(
        functools.partial(turn_kernel, plan, chunks),
        "turn",
        (info, *q_parts),
        [
            *[bf(query_rows, HD)] * 2,
            *[bf(HD, query_rows)] * 2,
            i32(len(plan.tiles) * block_rows, plan.lanes),
            i32(len(chunks) * plan.slices, plan.lanes),
        ],
        [SMEM] + [VMEM] * kv,
    )
    column, handed, order = [None] * parts, [None] * parts, []
    for p in reversed(range(parts)):
        parcels = [pieces[m] for m in plan.zone(p)]
        extra = [column[p + 1], *order] if order else []
        *handed_on, column[p] = call(
            functools.partial(stack_kernel, len(parcels)),
            "stack",
            (*parcels, *extra),
            [dkv] * (1 + bool(extra)),
        )
        handed[p] = column[p]
        if extra:
            handed[p + 1] = handed_on[0]
        order = q_parts[1:] if p else []
    columns = [[swap(half, "head", a * kv) for half in column] for a in range(1, spans)]
    near_kv = [column] + [[swap(half, "ctx", core) for half in handed] for core in range(1, cores)]
    near_flat = [half for pair in near_kv for half in pair]
    each = range(parts)
    near_chunks = [(0, core, p) for core in range(cores) for p in each]
    mid_chunks = [(a, 0, p) for a in range(1, spans) for p in each]
    far_chunks = [(a, core, p) for a in range(1, spans) for core in range(1, cores) for p in each]

    keys = plan.chunk_keys
    query_rows = plan.query_rows
    row, column_out = f32(1, query_rows), f32(HD, query_rows)

    def forward(name, chunks, kv_refs, order):
        size = len(chunks) * keys
        return call(
            functools.partial(part_kernel, plan, chunks),
            name,
            (gap, firsts, q_t, *kv_refs, *order),
            [f32(size, query_rows), row, row, column_out],
            None,
            [pltpu.VMEM((2 * HD, size), BF)],
            size * 4 * HD,
            8 * size * query_rows * HD,
        )

    mids, order = [None] * parts, []
    for p in reversed(each):
        if p + 1 < parts or parts == 1:
            near_e, *near = forward("attend_near", near_chunks, near_flat, order)
            order = [near[0]]
            for pair in columns:
                pair[p] = after([pair[p]], order)[0]
        mids[p] = forward("attend_mid", [c for c in mid_chunks if c[2] == p], [pair[p] for pair in columns], order)
        order = [mids[p][1]]
    far_kv = [swap(pair[p], "ctx", core) for pair in columns for core in range(1, cores) for p in each]
    far_keys = len(far_kv) * keys
    outs = call(
        functools.partial(far_kernel, plan, far_chunks, 1 + parts),
        "attend_far",
        (gap, firsts, q_all, do_all, q_t, do_t, *near, *[r for mid in mids for r in mid[1:]], *far_kv),
        [row] * (2 + parts) + [bf(HD, query_rows), column_out] + [dkv] * len(far_kv),
        None,
        [
            pltpu.VMEM((2 * HD, far_keys), BF),
            pltpu.VMEM((far_keys, query_rows), F32),
            pltpu.VMEM((far_keys, query_rows), F32),
            pltpu.VMEM((far_keys, query_rows), BF),
            pltpu.VMEM((far_keys, query_rows), BF),
        ],
        far_keys * (4 * HD + 12 * query_rows),
        16 * far_keys * query_rows * HD,
    )
    (near_scale, *mid_scales), outs = outs[: 1 + parts], outs[1 + parts :]
    (delta, mixed, q_grad), far_dkv = outs[:3], outs[3:]

    def back(rows_at, last, e, scale, q_grad, kv_refs, order):
        count = len(rows_at)
        q_outs = [bf(2, rows, width)] * kv if last else [column_out]
        outs = call(
            functools.partial(back_kernel, plan, rows_at, last, len(order)),
            "attend_back",
            (q_all, do_all, do_t, e, scale, delta, q_grad, *[mixed] * last, *kv_refs, *order),
            q_outs + [dkv] * count,
            None,
            [
                pltpu.VMEM((2 * HD, count * keys), BF),
                pltpu.VMEM((count * keys, query_rows), BF),
                pltpu.VMEM((count * keys, query_rows), BF),
            ],
            count * keys * (4 * HD + 4 * query_rows),
            12 * count * keys * query_rows * HD,
        )
        return outs[: len(q_outs)], outs[len(q_outs) :]

    sums = [[] for _ in range(parts)]
    totals = []
    for p in reversed(each):
        mid_kv = [pair[p] for pair in columns]
        (q_grad,), mid_dkv = back(
            list(range(len(mid_kv))), False, mids[p][0], mid_scales[p], q_grad, mid_kv, []
        )
        for a in range(spans - 1):
            both = [mid_dkv[a]]
            for core in range(1, cores):
                ours = far_dkv[(a * (cores - 1) + core - 1) * parts + p]
                both.append(swap(ours, "ctx", core))
            totals += call(add_kernel, "sum_cores", after(both, totals[-1:]), [dkv])
            sums[p].append(swap(totals[-1], "head", (a + 1) * kv))
    order = [swap(totals[-1][0, 0, :, :HD], "ctx", 1)] if cores > 1 else []
    for core in reversed(range(cores)):
        outs, parts_dkv = back(
            [core * parts + p for p in each], core == 0, near_e, near_scale, q_grad, near_kv[core], order
        )
        q_grad = outs[0]
        for p in range(parts):
            sums[p].append(swap(parts_dkv[p], "ctx", core) if core else parts_dkv[p])
    q_parts = outs[:kv]
    z_parts = [None] * z_devices
    for p in range(parts):
        totals = call(
            functools.partial(sum_heads_kernel, len(sums[p])),
            "sum_heads",
            sums[p],
            [bf(kv, rows, 2 * HD)] * z_part,
        )

        if p == parts - 1:
            q_parts = with_swaps(after(q_parts, totals[:1]))
        for m, total in zip(plan.zone(p), totals):
            z_parts[m] = swap(total, "ctx", m * cores) if m else total
    ordered = [z_parts[m] for p in each for m in plan.zone(p)]
    if parts > 1:
        far_z = call(sum_far_kernel, "sum_far_z", ordered[:z_part], [f32(kv, rows, 2 * HD)], flops=1 << 32)
        ordered = [*far_z, *ordered[z_part:]]
    pair_parts = call(
        functools.partial(sum_z_kernel, kv), "sum_z", ordered, [bf(rows, 2 * HD)] * kv
    )
    pair_parts = with_swaps(pair_parts)
    attended, query_grad, done = call(
        functools.partial(finish_q_kernel, kv),
        "finish_q",
        (own_group, *q_parts),
        [bf(rows, query_width)] * 2 + [f32(8, HD)],
        [SMEM] + [VMEM] * kv,
    )
    key_grad, value_grad = call(
        functools.partial(finish_kv_kernel, kv),
        "finish_kv",
        (own_group, *pair_parts, done),
        [bf(rows, kv * HD)] * 2,
        [SMEM] + [VMEM] * (kv + 1),
    )
    return (
        attended.reshape(halves, block_rows, query_width),
        query_grad.reshape(halves, block_rows, query_width),
        key_grad.reshape(halves, block_rows, kv * HD),
        value_grad.reshape(halves, block_rows, kv * HD),
    )


def solution(mesh):
    split = P("ctx", "head", None)
    return jax.shard_map(
        shards,
        mesh=mesh,
        in_specs=(split, split, split, split, P()),
        out_specs=(split, split, split, split),
        check_vma=False,
    )
```

```python
import functools
import math

import jax
import jax.numpy as jnp
from jax import lax
from jax.experimental import pallas as pl
from jax.experimental.pallas import tpu as pltpu
from jax.sharding import PartitionSpec as P

HD = 128
CORES = 2
BF = jnp.bfloat16
F32 = jnp.float32
LOWEST = -1e30
FLOOR = -1e29
SCALING = 1.0 / math.sqrt(HD)
EXPO = SCALING * math.log2(math.e)

VMEM = pl.BlockSpec(memory_space=pltpu.VMEM)
SMEM = pl.BlockSpec(memory_space=pltpu.SMEM)


def swap(block, axis, mask):
    size = lax.axis_size(axis)
    return lax.ppermute(block, axis, [(i, i ^ mask) for i in range(size)])


def nbytes(arrays):
    return sum(math.prod(a.shape) * a.dtype.itemsize for a in arrays)


def after(blocks, earlier):
    if not earlier:
        return tuple(blocks)
    return lax.optimization_barrier((tuple(blocks), tuple(earlier)))[0]


def call(kernel, name, ins, outs, specs=None, scratch=(), extra=0, flops=0):
    limit = nbytes(ins) + nbytes(outs) + extra + (12 << 20)
    return pl.pallas_call(
        kernel,
        out_shape=list(outs),
        in_specs=specs or [VMEM] * len(ins),
        out_specs=[VMEM] * len(outs),
        scratch_shapes=list(scratch),
        compiler_params=pltpu.CompilerParams(vmem_limit_bytes=min(limit, 60 << 20)),
        cost_estimate=pl.CostEstimate(
            flops=flops, bytes_accessed=nbytes(ins) + nbytes(outs), transcendentals=0
        ),
        name=name,
    )(*ins)


def dot(left, right):
    return jnp.dot(left, right, preferred_element_type=F32)


def dot_rows(left, right):
    return lax.dot_general(left, right, (((1,), (1,)), ((), ())), preferred_element_type=F32)


def pack_q_kernel(kv, group_ref, query_ref, grad_ref, *out_refs):
    width = out_refs[0].shape[2]
    for g in range(kv):

        @pl.when(group_ref[0] == g)
        def _():
            for s in range(kv):
                cols = pl.ds((g ^ s) * width, width)
                out_refs[s][0] = query_ref[:, cols]
                out_refs[s][1] = grad_ref[:, cols]


def stack_kernel(count, *refs):
    ins, refs = refs[:count], refs[count:]
    passed = len(refs) // 2
    refs, out_ref = refs[:-1], refs[-1]
    for i, ref in enumerate(ins):
        out_ref[i] = ref[...]
    if passed:
        refs[-1][...] = refs[0][...]


class Plan:
    def __init__(self, kv, block_len, block_rows, rows, group, cores, z_devices, parts):
        self.kv, self.block_len, self.block_rows, self.rows = kv, block_len, block_rows, rows
        self.group, self.cores, self.parts, self.z_part = group, cores, parts, z_devices // parts
        self.blocks = rows // block_rows
        self.tile_rows = block_rows if block_rows % 16 == 0 else rows
        self.lanes = group * self.tile_rows
        self.query_rows = kv * group * rows
        self.chunk_keys = self.z_part * kv * rows
        self.slices = self.chunk_keys // block_rows
        self.tiles = [(s, start) for s in range(kv) for start in range(0, rows, self.tile_rows)]

    def zone(self, part):
        first = (self.parts - 1 - part) * self.z_part
        return range(first, first + self.z_part)

    def at(self, tile):
        return pl.ds(tile * self.lanes, self.lanes)

    def keys_at(self, i):
        return pl.ds(i * self.chunk_keys, self.chunk_keys)

    def gap(self, tile, info_ref):
        s, start = self.tiles[tile]
        head, ctx = info_ref[0], info_ref[1]
        row = lax.broadcasted_iota(jnp.int32, (1, self.lanes), 1) % self.tile_rows + start
        pos = jnp.zeros((1, self.lanes), jnp.int32)
        for b in range(start // self.block_rows, -(-(start + self.tile_rows) // self.block_rows)):
            first = info_ref[2 + ctx * self.blocks + b] * self.block_len + (head ^ s) * self.block_rows
            pos = jnp.where(row // self.block_rows == b, first + row % self.block_rows, pos)
        return pos - lax.broadcasted_iota(jnp.int32, (self.block_rows, self.lanes), 0)

    def firsts(self, chunk, info_ref):
        head, ctx = info_ref[0], info_ref[1]
        a, core, part = chunk
        for j in range(self.slices):
            m, rest = divmod(j, self.kv * self.blocks)
            s, b = divmod(rest, self.blocks)
            stored = (ctx ^ (self.zone(part)[m] * self.cores + core)) * self.blocks + b
            yield info_ref[2 + stored] * self.block_len + (head ^ (a * self.kv + s)) * self.block_rows

    def first_at(self, chunk):
        a, core, part = chunk
        return ((a * self.cores + core) * self.parts + part) * self.slices

    def masked(self, scores, gap, chunk, first_ref):
        for j in range(self.slices):
            row = j * self.block_rows
            first = first_ref[pl.ds(self.first_at(chunk) + j, 1), :]
            yield row, jnp.where(gap >= first, scores[row : row + self.block_rows], LOWEST)

    def turn(self, kv_refs, turned_ref):
        for i, ref in enumerate(kv_refs):
            turned_ref[:, self.keys_at(i)] = ref[...].reshape(self.chunk_keys, 2 * HD).T

    def keys(self, ref):
        return ref[:, :, :, :HD].reshape(self.chunk_keys, HD)

    def values(self, ref):
        return ref[:, :, :, HD:].reshape(self.chunk_keys, HD)

    def fold(self, block):
        return block.reshape(block.shape[0] // 8, 8, self.lanes)

    def scores(self, tile, chunks, kv_refs, q_t, e_ref, cols, gap_ref, first_ref):
        gap = gap_ref[pl.ds(tile * self.block_rows, self.block_rows), :]
        top = jnp.full((8, self.lanes), FLOOR, F32)
        for i, ref in enumerate(kv_refs):
            scores = dot(self.keys(ref), q_t)
            for row, part in self.masked(scores, gap, chunks[i], first_ref):
                e_ref[pl.ds(i * self.chunk_keys + row, part.shape[0]), cols] = part
                top = jnp.maximum(top, jnp.max(self.fold(part), axis=0))
        return jnp.max(top, axis=0, keepdims=True)

    def exponents(self, count, e_ref, cols, top):
        total = jnp.zeros((8, self.lanes), F32)
        for i in range(count):
            part = jnp.exp2(e_ref[self.keys_at(i), cols] * EXPO - top * EXPO)
            e_ref[self.keys_at(i), cols] = part
            total = total + jnp.sum(self.fold(part), axis=0)
        return jnp.sum(total, axis=0, keepdims=True)

    def store_heads(self, out_ref, tile, turned):
        s, start = self.tiles[tile]
        block = turned.T.astype(BF)
        for n in range(self.group):
            piece = block[n * self.tile_rows : (n + 1) * self.tile_rows]
            out_ref[pl.ds(start, self.tile_rows), pl.ds(n * HD, HD)] = piece

    def back(self, dkv_refs, p_ref, ds_ref, q_ref, do_ref):
        shape = (self.z_part, self.kv, self.rows, HD)
        for i, out_ref in enumerate(dkv_refs):
            at = self.keys_at(i)
            out_ref[:, :, :, :HD] = dot(ds_ref[at, :], q_ref[...]).astype(BF).reshape(shape)
            out_ref[:, :, :, HD:] = dot(p_ref[at, :], do_ref[...]).astype(BF).reshape(shape)


def forward_part(plan, chunks, gap_ref, first_ref, q_t, kv_refs, e_ref, top_ref, sum_ref, mix_ref, turned_ref):
    spans = [plan.at(tile) for tile in range(len(plan.tiles))]
    tops = [
        plan.scores(tile, chunks, kv_refs, q_t[:, at], e_ref, at, gap_ref, first_ref)
        for tile, at in enumerate(spans)
    ]
    plan.turn(kv_refs, turned_ref)
    for at, top in zip(spans, tops):
        top_ref[:, at] = top
        sum_ref[:, at] = plan.exponents(len(chunks), e_ref, at, top)
    for at in spans:
        mixed = jnp.zeros((HD, plan.lanes), F32)
        for i in range(len(chunks)):
            weights = e_ref[plan.keys_at(i), at].astype(BF)
            mixed = mixed + dot(turned_ref[pl.ds(HD, HD), plan.keys_at(i)], weights)
        mix_ref[:, at] = mixed


def turn_kernel(plan, chunks, info_ref, *refs):
    q_parts, (q_all, do_all, q_t, do_t, gap_ref, first_ref) = refs[:-6], refs[-6:]
    for tile, (s, start) in enumerate(plan.tiles):
        span = pl.ds(start, plan.tile_rows)
        for n in range(plan.group):
            at = pl.ds(tile * plan.lanes + n * plan.tile_rows, plan.tile_rows)
            q_all[at, :] = q_parts[s][0, span, pl.ds(n * HD, HD)]
            do_all[at, :] = q_parts[s][1, span, pl.ds(n * HD, HD)]
        at = plan.at(tile)
        q_t[:, at] = q_all[at, :].T
        do_t[:, at] = do_all[at, :].T
        gap_ref[pl.ds(tile * plan.block_rows, plan.block_rows), :] = plan.gap(tile, info_ref)
    for chunk in chunks:
        for j, first in enumerate(plan.firsts(chunk, info_ref)):
            first_ref[pl.ds(plan.first_at(chunk) + j, 1), :] = jnp.full((1, plan.lanes), first, jnp.int32)


def part_kernel(plan, chunks, gap_ref, first_ref, q_t, *refs):
    forward_part(plan, chunks, gap_ref, first_ref, q_t, refs[: len(chunks)], *refs[-5:])


def far_kernel(plan, chunks, others, gap_ref, first_ref, q_all, do_all, q_t, do_t, *refs):
    count = len(chunks)
    partial, refs = [refs[3 * i : 3 * i + 3] for i in range(others)], refs[3 * others :]
    kv_refs, refs = refs[:count], refs[count:]
    scale_refs, refs = refs[:others], refs[others:]
    (delta_ref, mixed_ref, q_grad_ref), refs = refs[:3], refs[3:]
    dkv_refs, (turned_ref, e_ref, w_ref, p_ref, ds_ref) = refs[:-5], refs[-5:]
    spans = [plan.at(tile) for tile in range(len(plan.tiles))]
    tops = [
        plan.scores(tile, chunks, kv_refs, q_t[:, at], e_ref, at, gap_ref, first_ref)
        for tile, at in enumerate(spans)
    ]
    plan.turn(kv_refs, turned_ref)
    for at in spans:
        for i, ref in enumerate(kv_refs):
            w_ref[plan.keys_at(i), at] = dot(plan.values(ref), do_t[:, at])
    inverses = []
    for at, top in zip(spans, tops):
        for top_ref, _, _ in partial:
            top = jnp.maximum(top, top_ref[:, at])
        total = plan.exponents(count, e_ref, at, top)
        factors = [jnp.exp2((top_ref[:, at] - top) * EXPO) for top_ref, _, _ in partial]
        for factor, (_, sum_ref, _) in zip(factors, partial):
            total = total + factor * sum_ref[:, at]
        inverse = 1.0 / total
        for factor, scale_ref in zip(factors, scale_refs):
            scale_ref[:, at] = factor * inverse
        inverses.append(inverse)
    for at, inverse in zip(spans, inverses):
        mixed = jnp.zeros((HD, plan.lanes), F32)
        for scale_ref, (_, _, mix_ref) in zip(scale_refs, partial):
            mixed = mixed + mix_ref[:, at] * scale_ref[:, at]
        for i in range(count):
            probs = (e_ref[plan.keys_at(i), at] * inverse).astype(BF)
            p_ref[plan.keys_at(i), at] = probs
            mixed = mixed + dot(turned_ref[pl.ds(HD, HD), plan.keys_at(i)], probs)
        mixed = mixed.astype(BF)
        mixed_ref[:, at] = mixed
        delta_ref[:, at] = jnp.sum(do_t[:, at].astype(F32) * mixed.astype(F32), axis=0, keepdims=True)
    for at, inverse in zip(spans, inverses):
        q_grad = jnp.zeros((HD, plan.lanes), F32)
        for i in range(count):
            probs = e_ref[plan.keys_at(i), at] * inverse
            grad_s = (probs * (w_ref[plan.keys_at(i), at] - delta_ref[:, at])).astype(BF)
            ds_ref[plan.keys_at(i), at] = grad_s
            q_grad = q_grad + dot(turned_ref[pl.ds(0, HD), plan.keys_at(i)], grad_s)
        q_grad_ref[:, at] = q_grad
    plan.back(dkv_refs, p_ref, ds_ref, q_all, do_all)


def back_kernel(plan, rows_at, last, order, stores, q_all, do_all, do_t, e_ref, scale_ref, delta_ref, q_grad_in, *refs):
    count = len(rows_at)
    mixed_ref, refs = refs[:stores], refs[stores:]
    kv_refs, refs = refs[:count], refs[count + order :]
    refs, (turned_ref, p_ref, ds_ref) = refs[:-3], refs[-3:]
    outs, dkv_refs = refs[:-count], refs[-count:]
    att_refs, outs = outs[: plan.kv * stores], outs[plan.kv * stores :]
    spans = [plan.at(tile) for tile in range(len(plan.tiles))]
    for at in spans:
        for i, ref in enumerate(kv_refs):
            probs = e_ref[plan.keys_at(rows_at[i]), at] * scale_ref[:, at]
            p_ref[plan.keys_at(i), at] = probs.astype(BF)
            grad_s = (probs * (dot(plan.values(ref), do_t[:, at]) - delta_ref[:, at])).astype(BF)
            ds_ref[plan.keys_at(i), at] = grad_s
    plan.turn(kv_refs, turned_ref)
    plan.back(dkv_refs, p_ref, ds_ref, q_all, do_all)
    for tile, at in enumerate(spans):
        q_grad = q_grad_in[:, at]
        for i in range(count):
            q_grad = q_grad + dot(turned_ref[pl.ds(0, HD), plan.keys_at(i)], ds_ref[plan.keys_at(i), at])
        if last:
            plan.store_heads(outs[plan.tiles[tile][0]], tile, q_grad * SCALING)
        else:
            outs[0][:, at] = q_grad
        if stores:
            plan.store_heads(att_refs[plan.tiles[tile][0]], tile, mixed_ref[0][:, at].astype(F32))


def add_kernel(*refs):
    total = refs[0][...].astype(F32)
    for ref in refs[1:-1]:
        total = total + ref[...].astype(F32)
    refs[-1][...] = total.astype(BF)


def sum_heads_kernel(parts, order, *refs):
    for m_z, out_ref in enumerate(refs[parts + order :]):
        total = refs[0][m_z].astype(F32)
        for ref in refs[1:parts]:
            total = total + ref[m_z].astype(F32)
        out_ref[...] = total.astype(BF)


def sum_z_kernel(kv, *refs):
    ins, outs = refs[:-kv], refs[-kv:]
    for s, out_ref in enumerate(outs):
        total = ins[0][s].astype(F32)
        for ref in ins[1:]:
            total = total + ref[s].astype(F32)
        out_ref[...] = total.astype(BF)


def sum_far_kernel(*refs):
    total = refs[0][...].astype(F32)
    for ref in refs[1:-1]:
        total = total + ref[...].astype(F32)
    refs[-1][...] = total


def finish_kv_kernel(kv, group_ref, *refs):
    key_ref, value_ref = refs[kv + 1 :]
    for g in range(kv):

        @pl.when(group_ref[0] == g)
        def _():
            for s in range(kv):
                cols = pl.ds((g ^ s) * HD, HD)
                key_ref[:, cols] = (refs[s][:, :HD].astype(F32) * SCALING).astype(BF)
                value_ref[:, cols] = refs[s][:, HD:]


def finish_q_kernel(kv, group_ref, *refs):
    att_ref, grad_ref, done_ref = refs[2 * kv :]
    done_ref[...] = jnp.zeros_like(done_ref)
    width = refs[0].shape[1]
    for g in range(kv):

        @pl.when(group_ref[0] == g)
        def _():
            for s in range(kv):
                cols = pl.ds((g ^ s) * width, width)
                att_ref[:, cols] = refs[s][...]
                grad_ref[:, cols] = refs[kv + s][...]


def shards(queries, key_vectors, value_vectors, out_grad, block_order):
    heads_devices = lax.axis_size("head")
    ctx_devices = lax.axis_size("ctx")
    halves, block_rows, query_width = queries.shape
    kv = key_vectors.shape[2] // HD
    rows = halves * block_rows
    width = query_width // kv
    cores = CORES if ctx_devices % CORES == 0 else 1
    z_devices = ctx_devices // cores
    spans = heads_devices // kv
    parts = 2 if z_devices % 2 == 0 else 1
    plan = Plan(kv, block_rows * heads_devices, block_rows, rows, width // HD, cores, z_devices, parts)
    z_part = plan.z_part
    head = lax.axis_index("head").astype(jnp.int32)
    place = jnp.stack([head, lax.axis_index("ctx").astype(jnp.int32)])
    info = jnp.concatenate([place, block_order])
    own_group = (head % kv).reshape(1)
    queries = queries.reshape(rows, query_width)
    out_grad = out_grad.reshape(rows, query_width)
    key_vectors = key_vectors.reshape(rows, kv * HD)
    value_vectors = value_vectors.reshape(rows, kv * HD)

    def bf(*dims):
        return jax.ShapeDtypeStruct(dims, BF)

    def f32(*dims):
        return jax.ShapeDtypeStruct(dims, F32)

    def i32(*dims):
        return jax.ShapeDtypeStruct(dims, jnp.int32)

    def with_swaps(blocks):
        return [blocks[0]] + [swap(blocks[s], "head", s) for s in range(1, kv)]

    dkv = bf(z_part, kv, rows, 2 * HD)

    def of_head(g):
        picked = []
        for block in (key_vectors, value_vectors):
            out = block[:, :HD]
            for i in range(1, kv):
                out = jnp.where(g == i, block[:, i * HD : (i + 1) * HD], out)
            picked.append(out)
        return jnp.concatenate(picked, axis=1)

    piece = jnp.stack(with_swaps([of_head((head % kv) ^ s) for s in range(kv)]))
    q_parts = call(
        functools.partial(pack_q_kernel, kv),
        "pack_q",
        (own_group, queries, out_grad),
        [bf(2, rows, width)] * kv,
        [SMEM, VMEM, VMEM],
    )
    pieces = [swap(piece, "ctx", m * cores) for m in reversed(range(1, z_devices))]
    pieces = [piece] + pieces[::-1]
    q_parts = with_swaps(q_parts)
    query_rows = plan.query_rows
    chunks = [(a, core, p) for a in range(spans) for core in range(cores) for p in range(parts)]
    q_all, do_all, q_t, do_t, gap, firsts = call(
        functools.partial(turn_kernel, plan, chunks),
        "turn",
        (info, *q_parts),
        [
            *[bf(query_rows, HD)] * 2,
            *[bf(HD, query_rows)] * 2,
            i32(len(plan.tiles) * block_rows, plan.lanes),
            i32(len(chunks) * plan.slices, plan.lanes),
        ],
        [SMEM] + [VMEM] * kv,
    )
    column, handed, order = [None] * parts, [None] * parts, []
    for p in reversed(range(parts)):
        parcels = [pieces[m] for m in plan.zone(p)]
        extra = [column[p + 1], *order] if order else []
        *handed_on, column[p] = call(
            functools.partial(stack_kernel, len(parcels)),
            "stack",
            (*parcels, *extra),
            [dkv] * (1 + bool(extra)),
        )
        handed[p] = column[p]
        if extra:
            handed[p + 1] = handed_on[0]
        order = [q_t] if p else []
    columns = [[swap(half, "head", a * kv) for half in column] for a in range(1, spans)]
    near_kv = [column] + [[swap(half, "ctx", core) for half in handed] for core in range(1, cores)]
    near_flat = [half for pair in near_kv for half in pair]
    each = range(parts)
    near_chunks = [(0, core, p) for core in range(cores) for p in each]
    mid_chunks = [(a, 0, p) for a in range(1, spans) for p in each]
    far_chunks = [(a, core, p) for a in range(1, spans) for core in range(1, cores) for p in each]

    keys = plan.chunk_keys
    query_rows = plan.query_rows
    row, column_out = f32(1, query_rows), f32(HD, query_rows)

    def forward(name, chunks, kv_refs, order, flops=8):
        size = len(chunks) * keys
        return call(
            functools.partial(part_kernel, plan, chunks),
            name,
            (gap, firsts, q_t, *kv_refs, *order),
            [f32(size, query_rows), row, row, column_out],
            None,
            [pltpu.VMEM((2 * HD, size), BF)],
            size * 4 * HD,
            flops * size * query_rows * HD,
        )

    mids, order = [None] * parts, []
    for p in reversed(each):
        if p + 1 < parts or parts == 1:
            near_e, *near = forward("attend_near", near_chunks, near_flat, order)
            order = [near[0]]
            for pair in columns:
                pair[p] = after([pair[p]], order)[0]
        mid_part = [c for c in mid_chunks if c[2] == p]
        mids[p] = forward("attend_mid", mid_part, [pair[p] for pair in columns], order)
        order = [mids[p][1]]
    far_kv = [swap(pair[p], "ctx", core) for pair in columns for core in range(1, cores) for p in each]
    far_keys = len(far_kv) * keys
    outs = call(
        functools.partial(far_kernel, plan, far_chunks, 1 + parts),
        "attend_far",
        (gap, firsts, q_all, do_all, q_t, do_t, *near, *[r for mid in mids for r in mid[1:]], *far_kv),
        [row] * (2 + parts) + [bf(HD, query_rows), column_out] + [dkv] * len(far_kv),
        None,
        [
            pltpu.VMEM((2 * HD, far_keys), BF),
            pltpu.VMEM((far_keys, query_rows), F32),
            pltpu.VMEM((far_keys, query_rows), F32),
            pltpu.VMEM((far_keys, query_rows), BF),
            pltpu.VMEM((far_keys, query_rows), BF),
        ],
        far_keys * (4 * HD + 12 * query_rows),
        16 * far_keys * query_rows * HD,
    )
    (near_scale, *mid_scales), outs = outs[: 1 + parts], outs[1 + parts :]
    (delta, mixed, q_grad), far_dkv = outs[:3], outs[3:]

    def back(rows_at, last, e, scale, q_grad, kv_refs, order, stores=False):
        count = len(rows_at)
        q_outs = [bf(rows, width)] * (kv * stores) + ([bf(rows, width)] * kv if last else [column_out])
        outs = call(
            functools.partial(back_kernel, plan, rows_at, last, len(order), stores),
            "attend_back",
            (q_all, do_all, do_t, e, scale, delta, q_grad, *[mixed] * stores, *kv_refs, *order),
            q_outs + [dkv] * count,
            None,
            [
                pltpu.VMEM((2 * HD, count * keys), BF),
                pltpu.VMEM((count * keys, query_rows), BF),
                pltpu.VMEM((count * keys, query_rows), BF),
            ],
            count * keys * (4 * HD + 4 * query_rows),
            12 * count * keys * query_rows * HD,
        )
        return outs[: len(q_outs)], outs[len(q_outs) :]

    sums = [[] for _ in range(parts)]
    totals = []
    for p in reversed(each):
        mid_kv = [pair[p] for pair in columns]
        (q_grad,), mid_dkv = back(
            list(range(len(mid_kv))), False, mids[p][0], mid_scales[p], q_grad, mid_kv, []
        )
        for a in range(spans - 1):
            both = [mid_dkv[a]]
            for core in range(1, cores):
                ours = far_dkv[(a * (cores - 1) + core - 1) * parts + p]
                both.append(swap(ours, "ctx", core))
            totals += call(add_kernel, "sum_cores", after(both, totals[-1:]), [dkv])
            sums[p].append(swap(totals[-1], "head", (a + 1) * kv))
    order = [swap(totals[-1][0, 0, :, :HD], "ctx", 1)] if cores > 1 else []
    for core in reversed(range(cores)):
        stores = core == cores - 1
        outs, parts_dkv = back(
            [core * parts + p for p in each],
            core == 0,
            near_e,
            near_scale,
            q_grad,
            near_kv[core],
            order,
            stores,
        )
        if stores:
            att_parts, outs = with_swaps(outs[:kv]), outs[kv:]
        q_grad = outs[0]
        for p in range(parts):
            sums[p].append(swap(parts_dkv[p], "ctx", core) if core else parts_dkv[p])
    q_grad_parts = outs
    z_parts = [None] * z_devices
    for p in range(parts):
        order = att_parts[1:] if p else []
        totals = call(
            functools.partial(sum_heads_kernel, len(sums[p]), len(order)),
            "sum_heads",
            (*sums[p], *order),
            [bf(kv, rows, 2 * HD)] * z_part,
        )
        if p == parts - 1:
            q_grad_parts = with_swaps(after(q_grad_parts, totals[:1]))
        for m, total in zip(plan.zone(p), totals):
            z_parts[m] = swap(total, "ctx", m * cores) if m else total
    ordered = [z_parts[m] for p in each for m in plan.zone(p)]
    if parts > 1:
        far_z = call(sum_far_kernel, "sum_far_z", ordered[:z_part], [f32(kv, rows, 2 * HD)], flops=1 << 32)
        ordered = [*far_z, *ordered[z_part:]]
    pair_parts = call(
        functools.partial(sum_z_kernel, kv), "sum_z", ordered, [bf(rows, 2 * HD)] * kv
    )
    pair_parts = with_swaps(pair_parts)
    attended, query_grad, done = call(
        functools.partial(finish_q_kernel, kv),
        "finish_q",
        (own_group, *att_parts, *q_grad_parts),
        [bf(rows, query_width)] * 2 + [f32(8, HD)],
        [SMEM] + [VMEM] * (2 * kv),
    )
    key_grad, value_grad = call(
        functools.partial(finish_kv_kernel, kv),
        "finish_kv",
        (own_group, *pair_parts, done),
        [bf(rows, kv * HD)] * 2,
        [SMEM] + [VMEM] * (kv + 1),
    )
    return (
        attended.reshape(halves, block_rows, query_width),
        query_grad.reshape(halves, block_rows, query_width),
        key_grad.reshape(halves, block_rows, kv * HD),
        value_grad.reshape(halves, block_rows, kv * HD),
    )


def solution(mesh):
    split = P("ctx", "head", None)
    return jax.shard_map(
        shards,
        mesh=mesh,
        in_specs=(split, split, split, split, P()),
        out_specs=(split, split, split, split),
        check_vma=False,
    )
```

```python
import functools
import math

import jax
import jax.numpy as jnp
from jax import lax
from jax.experimental import pallas as pl
from jax.experimental.pallas import tpu as pltpu
from jax.sharding import PartitionSpec as P

HD = 128
CORES = 2
BF = jnp.bfloat16
F32 = jnp.float32
LOWEST = -1e30
FLOOR = -1e29
SCALING = 1.0 / math.sqrt(HD)
EXPO = SCALING * math.log2(math.e)

VMEM = pl.BlockSpec(memory_space=pltpu.VMEM)
SMEM = pl.BlockSpec(memory_space=pltpu.SMEM)


def swap(block, axis, mask):
    size = lax.axis_size(axis)
    return lax.ppermute(block, axis, [(i, i ^ mask) for i in range(size)])


def nbytes(arrays):
    return sum(math.prod(a.shape) * a.dtype.itemsize for a in arrays)


def after(blocks, earlier):
    if not earlier:
        return tuple(blocks)
    return lax.optimization_barrier((tuple(blocks), tuple(earlier)))[0]


def call(kernel, name, ins, outs, specs=None, scratch=(), extra=0, flops=0):
    limit = nbytes(ins) + nbytes(outs) + extra + (12 << 20)
    return pl.pallas_call(
        kernel,
        out_shape=list(outs),
        in_specs=specs or [VMEM] * len(ins),
        out_specs=[VMEM] * len(outs),
        scratch_shapes=list(scratch),
        compiler_params=pltpu.CompilerParams(vmem_limit_bytes=min(limit, 60 << 20)),
        cost_estimate=pl.CostEstimate(
            flops=flops, bytes_accessed=nbytes(ins) + nbytes(outs), transcendentals=0
        ),
        name=name,
    )(*ins)


def dot(left, right):
    return jnp.dot(left, right, preferred_element_type=F32)


def dot_rows(left, right):
    return lax.dot_general(left, right, (((1,), (1,)), ((), ())), preferred_element_type=F32)


def stack_kernel(count, *refs):
    ins, refs = refs[:count], refs[count:]
    passed = len(refs) // 2
    refs, out_ref = refs[:-1], refs[-1]
    for i, ref in enumerate(ins):
        out_ref[i] = ref[...]
    if passed:
        refs[-1][...] = refs[0][...]


class Plan:
    def __init__(self, kv, block_len, block_rows, rows, group, cores, z_devices, parts):
        self.kv, self.block_len, self.block_rows, self.rows = kv, block_len, block_rows, rows
        self.group, self.cores, self.parts, self.z_part = group, cores, parts, z_devices // parts
        self.blocks = rows // block_rows
        self.tile_rows = block_rows if block_rows % 16 == 0 else rows
        self.lanes = group * self.tile_rows
        self.query_rows = kv * group * rows
        self.chunk_keys = self.z_part * kv * rows
        self.slices = self.chunk_keys // block_rows
        self.tiles = [(s, start) for s in range(kv) for start in range(0, rows, self.tile_rows)]

    def zone(self, part):
        first = (self.parts - 1 - part) * self.z_part
        return range(first, first + self.z_part)

    def at(self, tile):
        return pl.ds(tile * self.lanes, self.lanes)

    def keys_at(self, i):
        return pl.ds(i * self.chunk_keys, self.chunk_keys)

    def gap(self, tile, info_ref):
        s, start = self.tiles[tile]
        head, ctx = info_ref[0], info_ref[1]
        row = lax.broadcasted_iota(jnp.int32, (1, self.lanes), 1) % self.tile_rows + start
        pos = jnp.zeros((1, self.lanes), jnp.int32)
        for b in range(start // self.block_rows, -(-(start + self.tile_rows) // self.block_rows)):
            first = info_ref[2 + ctx * self.blocks + b] * self.block_len + (head ^ s) * self.block_rows
            pos = jnp.where(row // self.block_rows == b, first + row % self.block_rows, pos)
        return pos - lax.broadcasted_iota(jnp.int32, (self.block_rows, self.lanes), 0)

    def firsts(self, chunk, info_ref):
        head, ctx = info_ref[0], info_ref[1]
        a, core, part = chunk
        for j in range(self.slices):
            m, rest = divmod(j, self.kv * self.blocks)
            s, b = divmod(rest, self.blocks)
            stored = (ctx ^ (self.zone(part)[m] * self.cores + core)) * self.blocks + b
            yield info_ref[2 + stored] * self.block_len + (head ^ (a * self.kv + s)) * self.block_rows

    def first_at(self, chunk):
        a, core, part = chunk
        return ((a * self.cores + core) * self.parts + part) * self.slices

    def masked(self, scores, gap, chunk, first_ref):
        for j in range(self.slices):
            row = j * self.block_rows
            first = first_ref[pl.ds(self.first_at(chunk) + j, 1), :]
            yield row, jnp.where(gap >= first, scores[row : row + self.block_rows], LOWEST)

    def turn(self, kv_refs, turned_ref):
        for i, ref in enumerate(kv_refs):
            turned_ref[:, self.keys_at(i)] = ref[...].reshape(self.chunk_keys, 2 * HD).T

    def keys(self, ref):
        return ref[:, :, :, :HD].reshape(self.chunk_keys, HD)

    def values(self, ref):
        return ref[:, :, :, HD:].reshape(self.chunk_keys, HD)

    def fold(self, block):
        return block.reshape(block.shape[0] // 8, 8, self.lanes)

    def scores(self, tile, chunks, kv_refs, q_t, e_ref, cols, gap_ref, first_ref):
        gap = gap_ref[pl.ds(tile * self.block_rows, self.block_rows), :]
        top = jnp.full((8, self.lanes), FLOOR, F32)
        for i, ref in enumerate(kv_refs):
            scores = dot(self.keys(ref), q_t)
            for row, part in self.masked(scores, gap, chunks[i], first_ref):
                e_ref[pl.ds(i * self.chunk_keys + row, part.shape[0]), cols] = part
                top = jnp.maximum(top, jnp.max(self.fold(part), axis=0))
        return jnp.max(top, axis=0, keepdims=True)

    def exponents(self, count, e_ref, cols, top):
        total = jnp.zeros((8, self.lanes), F32)
        for i in range(count):
            part = jnp.exp2(e_ref[self.keys_at(i), cols] * EXPO - top * EXPO)
            e_ref[self.keys_at(i), cols] = part
            total = total + jnp.sum(self.fold(part), axis=0)
        return jnp.sum(total, axis=0, keepdims=True)

    def store_heads(self, out_ref, kind, tile, turned):
        s, start = self.tiles[tile]
        block = turned.T.astype(BF)
        for n in range(self.group):
            piece = block[n * self.tile_rows : (n + 1) * self.tile_rows]
            out_ref[kind, pl.ds(start, self.tile_rows), pl.ds(n * HD, HD)] = piece

    def back(self, dkv_refs, p_ref, ds_ref, q_ref, do_ref):
        shape = (self.z_part, self.kv, self.rows, HD)
        for i, out_ref in enumerate(dkv_refs):
            at = self.keys_at(i)
            out_ref[:, :, :, :HD] = dot(ds_ref[at, :], q_ref[...]).astype(BF).reshape(shape)
            out_ref[:, :, :, HD:] = dot(p_ref[at, :], do_ref[...]).astype(BF).reshape(shape)


def forward_part(plan, chunks, gap_ref, first_ref, q_t, kv_refs, e_ref, top_ref, sum_ref, mix_ref, turned_ref):
    spans = [plan.at(tile) for tile in range(len(plan.tiles))]
    tops = [
        plan.scores(tile, chunks, kv_refs, q_t[:, at], e_ref, at, gap_ref, first_ref)
        for tile, at in enumerate(spans)
    ]
    plan.turn(kv_refs, turned_ref)
    for at, top in zip(spans, tops):
        top_ref[:, at] = top
        sum_ref[:, at] = plan.exponents(len(chunks), e_ref, at, top)
    for at in spans:
        mixed = jnp.zeros((HD, plan.lanes), F32)
        for i in range(len(chunks)):
            weights = e_ref[plan.keys_at(i), at].astype(BF)
            mixed = mixed + dot(turned_ref[pl.ds(HD, HD), plan.keys_at(i)], weights)
        mix_ref[:, at] = mixed


def turn_kernel(plan, chunks, info_ref, *refs):
    q_parts, (q_all, do_all, q_t, do_t, gap_ref, first_ref) = refs[:-6], refs[-6:]
    for tile, (s, start) in enumerate(plan.tiles):
        span = pl.ds(start, plan.tile_rows)
        for n in range(plan.group):
            at = pl.ds(tile * plan.lanes + n * plan.tile_rows, plan.tile_rows)
            q_all[at, :] = q_parts[s][0, span, pl.ds(n * HD, HD)]
            do_all[at, :] = q_parts[s][1, span, pl.ds(n * HD, HD)]
        at = plan.at(tile)
        q_t[:, at] = q_all[at, :].T
        do_t[:, at] = do_all[at, :].T
        gap_ref[pl.ds(tile * plan.block_rows, plan.block_rows), :] = plan.gap(tile, info_ref)
    for chunk in chunks:
        for j, first in enumerate(plan.firsts(chunk, info_ref)):
            first_ref[pl.ds(plan.first_at(chunk) + j, 1), :] = jnp.full((1, plan.lanes), first, jnp.int32)


def part_kernel(plan, chunks, gap_ref, first_ref, q_t, *refs):
    forward_part(plan, chunks, gap_ref, first_ref, q_t, refs[: len(chunks)], *refs[-5:])


def far_kernel(plan, chunks, others, gap_ref, first_ref, q_all, do_all, q_t, do_t, *refs):
    count = len(chunks)
    partial, refs = [refs[3 * i : 3 * i + 3] for i in range(others)], refs[3 * others :]
    kv_refs, refs = refs[:count], refs[count:]
    scale_refs, refs = refs[:others], refs[others:]
    (delta_ref, mixed_ref, q_grad_ref), refs = refs[:3], refs[3:]
    dkv_refs, (turned_ref, e_ref, w_ref, p_ref, ds_ref) = refs[:-5], refs[-5:]
    spans = [plan.at(tile) for tile in range(len(plan.tiles))]
    tops = [
        plan.scores(tile, chunks, kv_refs, q_t[:, at], e_ref, at, gap_ref, first_ref)
        for tile, at in enumerate(spans)
    ]
    plan.turn(kv_refs, turned_ref)
    for at in spans:
        for i, ref in enumerate(kv_refs):
            w_ref[plan.keys_at(i), at] = dot(plan.values(ref), do_t[:, at])
    inverses = []
    for at, top in zip(spans, tops):
        for top_ref, _, _ in partial:
            top = jnp.maximum(top, top_ref[:, at])
        total = plan.exponents(count, e_ref, at, top)
        factors = [jnp.exp2((top_ref[:, at] - top) * EXPO) for top_ref, _, _ in partial]
        for factor, (_, sum_ref, _) in zip(factors, partial):
            total = total + factor * sum_ref[:, at]
        inverse = 1.0 / total
        for factor, scale_ref in zip(factors, scale_refs):
            scale_ref[:, at] = factor * inverse
        inverses.append(inverse)
    for at, inverse in zip(spans, inverses):
        mixed = jnp.zeros((HD, plan.lanes), F32)
        for scale_ref, (_, _, mix_ref) in zip(scale_refs, partial):
            mixed = mixed + mix_ref[:, at] * scale_ref[:, at]
        for i in range(count):
            probs = (e_ref[plan.keys_at(i), at] * inverse).astype(BF)
            p_ref[plan.keys_at(i), at] = probs
            mixed = mixed + dot(turned_ref[pl.ds(HD, HD), plan.keys_at(i)], probs)
        mixed = mixed.astype(BF)
        mixed_ref[:, at] = mixed
        delta_ref[:, at] = jnp.sum(do_t[:, at].astype(F32) * mixed.astype(F32), axis=0, keepdims=True)
    for at, inverse in zip(spans, inverses):
        q_grad = jnp.zeros((HD, plan.lanes), F32)
        for i in range(count):
            probs = e_ref[plan.keys_at(i), at] * inverse
            grad_s = (probs * (w_ref[plan.keys_at(i), at] - delta_ref[:, at])).astype(BF)
            ds_ref[plan.keys_at(i), at] = grad_s
            q_grad = q_grad + dot(turned_ref[pl.ds(0, HD), plan.keys_at(i)], grad_s)
        q_grad_ref[:, at] = q_grad
    plan.back(dkv_refs, p_ref, ds_ref, q_all, do_all)


def back_kernel(plan, rows_at, last, order, q_all, do_all, do_t, e_ref, scale_ref, delta_ref, q_grad_in, *refs):
    count = len(rows_at)
    mixed_ref, refs = refs[:last], refs[last:]
    kv_refs, refs = refs[:count], refs[count + order :]
    refs, (turned_ref, p_ref, ds_ref) = refs[:-3], refs[-3:]
    outs, dkv_refs = refs[:-count], refs[-count:]
    spans = [plan.at(tile) for tile in range(len(plan.tiles))]
    for at in spans:
        for i, ref in enumerate(kv_refs):
            probs = e_ref[plan.keys_at(rows_at[i]), at] * scale_ref[:, at]
            p_ref[plan.keys_at(i), at] = probs.astype(BF)
            grad_s = (probs * (dot(plan.values(ref), do_t[:, at]) - delta_ref[:, at])).astype(BF)
            ds_ref[plan.keys_at(i), at] = grad_s
    plan.turn(kv_refs, turned_ref)
    plan.back(dkv_refs, p_ref, ds_ref, q_all, do_all)
    for tile, at in enumerate(spans):
        q_grad = q_grad_in[:, at]
        for i in range(count):
            q_grad = q_grad + dot(turned_ref[pl.ds(0, HD), plan.keys_at(i)], ds_ref[plan.keys_at(i), at])
        if last:
            out_ref = outs[plan.tiles[tile][0]]
            plan.store_heads(out_ref, 0, tile, mixed_ref[0][:, at].astype(F32))
            plan.store_heads(out_ref, 1, tile, q_grad * SCALING)
        else:
            outs[0][:, at] = q_grad


def add_kernel(*refs):
    total = refs[0][...].astype(F32)
    for ref in refs[1:-1]:
        total = total + ref[...].astype(F32)
    refs[-1][...] = total.astype(BF)


def sum_heads_kernel(parts, *refs):
    for m_z, out_ref in enumerate(refs[parts:]):
        total = refs[0][m_z].astype(F32)
        for ref in refs[1:parts]:
            total = total + ref[m_z].astype(F32)
        out_ref[...] = total.astype(BF)


def sum_z_kernel(kv, *refs):
    ins, outs = refs[:-kv], refs[-kv:]
    for s, out_ref in enumerate(outs):
        total = ins[0][s].astype(F32)
        for ref in ins[1:]:
            total = total + ref[s].astype(F32)
        out_ref[...] = total.astype(BF)


def sum_far_kernel(*refs):
    total = refs[0][...].astype(F32)
    for ref in refs[1:-1]:
        total = total + ref[...].astype(F32)
    refs[-1][...] = total


def finish_kv_kernel(kv, group_ref, *refs):
    key_ref, value_ref = refs[kv + 1 :]
    for g in range(kv):

        @pl.when(group_ref[0] == g)
        def _():
            for s in range(kv):
                cols = pl.ds((g ^ s) * HD, HD)
                key_ref[:, cols] = (refs[s][:, :HD].astype(F32) * SCALING).astype(BF)
                value_ref[:, cols] = refs[s][:, HD:]


def finish_q_kernel(kv, group_ref, *refs):
    att_ref, grad_ref, done_ref = refs[kv:]
    done_ref[...] = jnp.zeros_like(done_ref)
    width = refs[0].shape[2]
    for g in range(kv):

        @pl.when(group_ref[0] == g)
        def _():
            for s in range(kv):
                cols = pl.ds((g ^ s) * width, width)
                att_ref[:, cols] = refs[s][0]
                grad_ref[:, cols] = refs[s][1]


def shards(queries, key_vectors, value_vectors, out_grad, block_order):
    heads_devices = lax.axis_size("head")
    ctx_devices = lax.axis_size("ctx")
    halves, block_rows, query_width = queries.shape
    kv = key_vectors.shape[2] // HD
    rows = halves * block_rows
    width = query_width // kv
    cores = CORES if ctx_devices % CORES == 0 else 1
    z_devices = ctx_devices // cores
    spans = heads_devices // kv
    parts = 2 if z_devices % 2 == 0 else 1
    plan = Plan(kv, block_rows * heads_devices, block_rows, rows, width // HD, cores, z_devices, parts)
    z_part = plan.z_part
    head = lax.axis_index("head").astype(jnp.int32)
    place = jnp.stack([head, lax.axis_index("ctx").astype(jnp.int32)])
    info = jnp.concatenate([place, block_order])
    own_group = (head % kv).reshape(1)
    queries = queries.reshape(rows, query_width)
    out_grad = out_grad.reshape(rows, query_width)
    key_vectors = key_vectors.reshape(rows, kv * HD)
    value_vectors = value_vectors.reshape(rows, kv * HD)

    def bf(*dims):
        return jax.ShapeDtypeStruct(dims, BF)

    def f32(*dims):
        return jax.ShapeDtypeStruct(dims, F32)

    def i32(*dims):
        return jax.ShapeDtypeStruct(dims, jnp.int32)

    def with_swaps(blocks):
        return [blocks[0]] + [swap(blocks[s], "head", s) for s in range(1, kv)]

    dkv = bf(z_part, kv, rows, 2 * HD)

    def pick(block, g, size):
        out = block[:, :size]
        for i in range(1, kv):
            out = jnp.where(g == i, block[:, i * size : (i + 1) * size], out)
        return out

    def of_head(g):
        return jnp.concatenate([pick(key_vectors, g, HD), pick(value_vectors, g, HD)], axis=1)

    def queries_of(g):
        return jnp.stack([pick(queries, g, width), pick(out_grad, g, width)])

    piece = jnp.stack(with_swaps([of_head((head % kv) ^ s) for s in range(kv)]))
    q_parts = with_swaps([queries_of((head % kv) ^ s) for s in range(kv)])
    pieces = [swap(piece, "ctx", m * cores) for m in reversed(range(1, z_devices))]
    pieces = [piece] + pieces[::-1]
    query_rows = plan.query_rows
    chunks = [(a, core, p) for a in range(spans) for core in range(cores) for p in range(parts)]
    q_all, do_all, q_t, do_t, gap, firsts = call(
        functools.partial(turn_kernel, plan, chunks),
        "turn",
        (info, *q_parts),
        [
            *[bf(query_rows, HD)] * 2,
            *[bf(HD, query_rows)] * 2,
            i32(len(plan.tiles) * block_rows, plan.lanes),
            i32(len(chunks) * plan.slices, plan.lanes),
        ],
        [SMEM] + [VMEM] * kv,
    )
    column, handed, order = [None] * parts, [None] * parts, []
    for p in reversed(range(parts)):
        parcels = [pieces[m] for m in plan.zone(p)]
        extra = [column[p + 1], *order] if order else []
        *handed_on, column[p] = call(
            functools.partial(stack_kernel, len(parcels)),
            "stack",
            (*parcels, *extra),
            [dkv] * (1 + bool(extra)),
        )
        handed[p] = column[p]
        if extra:
            handed[p + 1] = handed_on[0]
        order = q_parts[1:] if p else []
    columns = [[swap(half, "head", a * kv) for half in column] for a in range(1, spans)]
    near_kv = [column] + [[swap(half, "ctx", core) for half in handed] for core in range(1, cores)]
    near_flat = [half for pair in near_kv for half in pair]
    each = range(parts)
    near_chunks = [(0, core, p) for core in range(cores) for p in each]
    mid_chunks = [(a, 0, p) for a in range(1, spans) for p in each]
    far_chunks = [(a, core, p) for a in range(1, spans) for core in range(1, cores) for p in each]

    keys = plan.chunk_keys
    query_rows = plan.query_rows
    row, column_out = f32(1, query_rows), f32(HD, query_rows)

    def forward(name, chunks, kv_refs, order):
        size = len(chunks) * keys
        return call(
            functools.partial(part_kernel, plan, chunks),
            name,
            (gap, firsts, q_t, *kv_refs, *order),
            [f32(size, query_rows), row, row, column_out],
            None,
            [pltpu.VMEM((2 * HD, size), BF)],
            size * 4 * HD,
            8 * size * query_rows * HD,
        )

    mids, order = [None] * parts, []
    for p in reversed(each):
        if p + 1 < parts or parts == 1:
            near_e, *near = forward("attend_near", near_chunks, near_flat, order)
            order = [near[0]]
            for pair in columns:
                pair[p] = after([pair[p]], order)[0]
        mids[p] = forward("attend_mid", [c for c in mid_chunks if c[2] == p], [pair[p] for pair in columns], order)
        order = [mids[p][1]]
    far_kv = [swap(pair[p], "ctx", core) for pair in columns for core in range(1, cores) for p in each]
    far_keys = len(far_kv) * keys
    outs = call(
        functools.partial(far_kernel, plan, far_chunks, 1 + parts),
        "attend_far",
        (gap, firsts, q_all, do_all, q_t, do_t, *near, *[r for mid in mids for r in mid[1:]], *far_kv),
        [row] * (2 + parts) + [bf(HD, query_rows), column_out] + [dkv] * len(far_kv),
        None,
        [
            pltpu.VMEM((2 * HD, far_keys), BF),
            pltpu.VMEM((far_keys, query_rows), F32),
            pltpu.VMEM((far_keys, query_rows), F32),
            pltpu.VMEM((far_keys, query_rows), BF),
            pltpu.VMEM((far_keys, query_rows), BF),
        ],
        far_keys * (4 * HD + 12 * query_rows),
        16 * far_keys * query_rows * HD,
    )
    (near_scale, *mid_scales), outs = outs[: 1 + parts], outs[1 + parts :]
    (delta, mixed, q_grad), far_dkv = outs[:3], outs[3:]

    def back(rows_at, last, e, scale, q_grad, kv_refs, order):
        count = len(rows_at)
        q_outs = [bf(2, rows, width)] * kv if last else [column_out]
        outs = call(
            functools.partial(back_kernel, plan, rows_at, last, len(order)),
            "attend_back",
            (q_all, do_all, do_t, e, scale, delta, q_grad, *[mixed] * last, *kv_refs, *order),
            q_outs + [dkv] * count,
            None,
            [
                pltpu.VMEM((2 * HD, count * keys), BF),
                pltpu.VMEM((count * keys, query_rows), BF),
                pltpu.VMEM((count * keys, query_rows), BF),
            ],
            count * keys * (4 * HD + 4 * query_rows),
            12 * count * keys * query_rows * HD,
        )
        return outs[: len(q_outs)], outs[len(q_outs) :]

    sums = [[] for _ in range(parts)]
    totals = []
    for p in reversed(each):
        mid_kv = [pair[p] for pair in columns]
        (q_grad,), mid_dkv = back(
            list(range(len(mid_kv))), False, mids[p][0], mid_scales[p], q_grad, mid_kv, []
        )
        for a in range(spans - 1):
            both = [mid_dkv[a]]
            for core in range(1, cores):
                ours = far_dkv[(a * (cores - 1) + core - 1) * parts + p]
                both.append(swap(ours, "ctx", core))
            totals += call(add_kernel, "sum_cores", after(both, totals[-1:]), [dkv])
            sums[p].append(swap(totals[-1], "head", (a + 1) * kv))
    order = [swap(totals[-1][0, 0, :, :HD], "ctx", 1)] if cores > 1 else []
    for core in reversed(range(cores)):
        outs, parts_dkv = back(
            [core * parts + p for p in each], core == 0, near_e, near_scale, q_grad, near_kv[core], order
        )
        q_grad = outs[0]
        for p in range(parts):
            sums[p].append(swap(parts_dkv[p], "ctx", core) if core else parts_dkv[p])
    q_parts = outs[:kv]
    z_parts = [None] * z_devices
    for p in range(parts):
        totals = call(
            functools.partial(sum_heads_kernel, len(sums[p])),
            "sum_heads",
            sums[p],
            [bf(kv, rows, 2 * HD)] * z_part,
        )

        if p == parts - 1:
            q_parts = with_swaps(after(q_parts, totals[:1]))
        for m, total in zip(plan.zone(p), totals):
            z_parts[m] = swap(total, "ctx", m * cores) if m else total
    ordered = [z_parts[m] for p in each for m in plan.zone(p)]
    if parts > 1:
        far_z = call(sum_far_kernel, "sum_far_z", ordered[:z_part], [f32(kv, rows, 2 * HD)], flops=1 << 32)
        ordered = [*far_z, *ordered[z_part:]]
    pair_parts = call(
        functools.partial(sum_z_kernel, kv), "sum_z", ordered, [bf(rows, 2 * HD)] * kv
    )
    pair_parts = with_swaps(pair_parts)
    attended, query_grad, done = call(
        functools.partial(finish_q_kernel, kv),
        "finish_q",
        (own_group, *q_parts),
        [bf(rows, query_width)] * 2 + [f32(8, HD)],
        [SMEM] + [VMEM] * kv,
    )
    key_grad, value_grad = call(
        functools.partial(finish_kv_kernel, kv),
        "finish_kv",
        (own_group, *pair_parts, done),
        [bf(rows, kv * HD)] * 2,
        [SMEM] + [VMEM] * (kv + 1),
    )
    return (
        attended.reshape(halves, block_rows, query_width),
        query_grad.reshape(halves, block_rows, query_width),
        key_grad.reshape(halves, block_rows, kv * HD),
        value_grad.reshape(halves, block_rows, kv * HD),
    )


def solution(mesh):
    split = P("ctx", "head", None)
    return jax.shard_map(
        shards,
        mesh=mesh,
        in_specs=(split, split, split, split, P()),
        out_specs=(split, split, split, split),
        check_vma=False,
    )
```

```python
import functools
import math

import jax
import jax.numpy as jnp
from jax import lax
from jax.experimental import pallas as pl
from jax.experimental.pallas import tpu as pltpu
from jax.sharding import PartitionSpec as P

HD = 128
CORES = 2
BF = jnp.bfloat16
F32 = jnp.float32
LOWEST = -1e30
FLOOR = -1e29
SCALING = 1.0 / math.sqrt(HD)
EXPO = SCALING * math.log2(math.e)

VMEM = pl.BlockSpec(memory_space=pltpu.VMEM)
SMEM = pl.BlockSpec(memory_space=pltpu.SMEM)


def swap(block, axis, mask):
    size = lax.axis_size(axis)
    return lax.ppermute(block, axis, [(i, i ^ mask) for i in range(size)])


def nbytes(arrays):
    return sum(math.prod(a.shape) * a.dtype.itemsize for a in arrays)


def after(blocks, earlier):
    if not earlier:
        return tuple(blocks)
    return lax.optimization_barrier((tuple(blocks), tuple(earlier)))[0]


def call(kernel, name, ins, outs, specs=None, scratch=(), extra=0, flops=0):
    limit = nbytes(ins) + nbytes(outs) + extra + (12 << 20)
    return pl.pallas_call(
        kernel,
        out_shape=list(outs),
        in_specs=specs or [VMEM] * len(ins),
        out_specs=[VMEM] * len(outs),
        scratch_shapes=list(scratch),
        compiler_params=pltpu.CompilerParams(vmem_limit_bytes=min(limit, 60 << 20)),
        cost_estimate=pl.CostEstimate(
            flops=flops, bytes_accessed=nbytes(ins) + nbytes(outs), transcendentals=0
        ),
        name=name,
    )(*ins)


def dot(left, right):
    return jnp.dot(left, right, preferred_element_type=F32)


def dot_rows(left, right):
    return lax.dot_general(left, right, (((1,), (1,)), ((), ())), preferred_element_type=F32)


def stack_kernel(count, *refs):
    ins, refs = refs[:count], refs[count:]
    passed = len(refs) // 2
    refs, out_ref = refs[:-1], refs[-1]
    for i, ref in enumerate(ins):
        out_ref[i] = ref[...]
    if passed:
        refs[-1][...] = refs[0][...]


class Plan:
    def __init__(self, kv, block_len, block_rows, rows, group, cores, z_devices, parts):
        self.kv, self.block_len, self.block_rows, self.rows = kv, block_len, block_rows, rows
        self.group, self.cores, self.parts, self.z_part = group, cores, parts, z_devices // parts
        self.blocks = rows // block_rows
        self.tile_rows = block_rows if block_rows % 16 == 0 else rows
        self.lanes = group * self.tile_rows
        self.query_rows = kv * group * rows
        self.chunk_keys = self.z_part * kv * rows
        self.slices = self.chunk_keys // block_rows
        self.tiles = [(s, start) for s in range(kv) for start in range(0, rows, self.tile_rows)]

    def zone(self, part):
        first = (self.parts - 1 - part) * self.z_part
        return range(first, first + self.z_part)

    def at(self, tile):
        return pl.ds(tile * self.lanes, self.lanes)

    def keys_at(self, i):
        return pl.ds(i * self.chunk_keys, self.chunk_keys)

    def gap(self, tile, info_ref):
        s, start = self.tiles[tile]
        head, ctx = info_ref[0], info_ref[1]
        row = lax.broadcasted_iota(jnp.int32, (1, self.lanes), 1) % self.tile_rows + start
        pos = jnp.zeros((1, self.lanes), jnp.int32)
        for b in range(start // self.block_rows, -(-(start + self.tile_rows) // self.block_rows)):
            first = info_ref[2 + ctx * self.blocks + b] * self.block_len + (head ^ s) * self.block_rows
            pos = jnp.where(row // self.block_rows == b, first + row % self.block_rows, pos)
        return pos - lax.broadcasted_iota(jnp.int32, (self.block_rows, self.lanes), 0)

    def firsts(self, chunk, info_ref):
        head, ctx = info_ref[0], info_ref[1]
        a, core, part = chunk
        for j in range(self.slices):
            m, rest = divmod(j, self.kv * self.blocks)
            s, b = divmod(rest, self.blocks)
            stored = (ctx ^ (self.zone(part)[m] * self.cores + core)) * self.blocks + b
            yield info_ref[2 + stored] * self.block_len + (head ^ (a * self.kv + s)) * self.block_rows

    def first_at(self, chunk):
        a, core, part = chunk
        return ((a * self.cores + core) * self.parts + part) * self.slices

    def masked(self, scores, gap, chunk, first_ref):
        for j in range(self.slices):
            row = j * self.block_rows
            first = first_ref[pl.ds(self.first_at(chunk) + j, 1), :]
            yield row, jnp.where(gap >= first, scores[row : row + self.block_rows], LOWEST)

    def turn(self, kv_refs, turned_ref):
        for i, ref in enumerate(kv_refs):
            turned_ref[:, self.keys_at(i)] = ref[...].reshape(self.chunk_keys, 2 * HD).T

    def keys(self, ref):
        return ref[:, :, :, :HD].reshape(self.chunk_keys, HD)

    def values(self, ref):
        return ref[:, :, :, HD:].reshape(self.chunk_keys, HD)

    def fold(self, block):
        return block.reshape(block.shape[0] // 8, 8, self.lanes)

    def scores(self, tile, chunks, kv_refs, q_t, e_ref, cols, gap_ref, first_ref):
        gap = gap_ref[pl.ds(tile * self.block_rows, self.block_rows), :]
        top = jnp.full((8, self.lanes), FLOOR, F32)
        for i, ref in enumerate(kv_refs):
            scores = dot(self.keys(ref), q_t)
            for row, part in self.masked(scores, gap, chunks[i], first_ref):
                e_ref[pl.ds(i * self.chunk_keys + row, part.shape[0]), cols] = part
                top = jnp.maximum(top, jnp.max(self.fold(part), axis=0))
        return jnp.max(top, axis=0, keepdims=True)

    def exponents(self, count, e_ref, cols, top):
        total = jnp.zeros((8, self.lanes), F32)
        for i in range(count):
            part = jnp.exp2(e_ref[self.keys_at(i), cols] * EXPO - top * EXPO)
            e_ref[self.keys_at(i), cols] = part
            total = total + jnp.sum(self.fold(part), axis=0)
        return jnp.sum(total, axis=0, keepdims=True)

    def store_heads(self, out_ref, kind, tile, turned):
        s, start = self.tiles[tile]
        block = turned.T.astype(BF)
        for n in range(self.group):
            piece = block[n * self.tile_rows : (n + 1) * self.tile_rows]
            out_ref[kind, pl.ds(start, self.tile_rows), pl.ds(n * HD, HD)] = piece

    def back(self, dkv_refs, p_ref, ds_ref, q_ref, do_ref):
        shape = (self.z_part, self.kv, self.rows, HD)
        for i, out_ref in enumerate(dkv_refs):
            at = self.keys_at(i)
            out_ref[:, :, :, :HD] = dot(ds_ref[at, :], q_ref[...]).astype(BF).reshape(shape)
            out_ref[:, :, :, HD:] = dot(p_ref[at, :], do_ref[...]).astype(BF).reshape(shape)


def forward_part(plan, chunks, gap_ref, first_ref, q_t, kv_refs, e_ref, top_ref, sum_ref, mix_ref, turned_ref):
    spans = [plan.at(tile) for tile in range(len(plan.tiles))]
    tops = [
        plan.scores(tile, chunks, kv_refs, q_t[:, at], e_ref, at, gap_ref, first_ref)
        for tile, at in enumerate(spans)
    ]
    plan.turn(kv_refs, turned_ref)
    for at, top in zip(spans, tops):
        top_ref[:, at] = top
        sum_ref[:, at] = plan.exponents(len(chunks), e_ref, at, top)
    for at in spans:
        mixed = jnp.zeros((HD, plan.lanes), F32)
        for i in range(len(chunks)):
            weights = e_ref[plan.keys_at(i), at].astype(BF)
            mixed = mixed + dot(turned_ref[pl.ds(HD, HD), plan.keys_at(i)], weights)
        mix_ref[:, at] = mixed


def turn_kernel(plan, chunks, info_ref, *refs):
    q_parts, (q_all, do_all, q_t, do_t, gap_ref, first_ref) = refs[:-6], refs[-6:]
    for tile, (s, start) in enumerate(plan.tiles):
        span = pl.ds(start, plan.tile_rows)
        for n in range(plan.group):
            at = pl.ds(tile * plan.lanes + n * plan.tile_rows, plan.tile_rows)
            q_all[at, :] = q_parts[s][0, span, pl.ds(n * HD, HD)]
            do_all[at, :] = q_parts[s][1, span, pl.ds(n * HD, HD)]
        at = plan.at(tile)
        q_t[:, at] = q_all[at, :].T
        do_t[:, at] = do_all[at, :].T
        gap_ref[pl.ds(tile * plan.block_rows, plan.block_rows), :] = plan.gap(tile, info_ref)
    for chunk in chunks:
        for j, first in enumerate(plan.firsts(chunk, info_ref)):
            first_ref[pl.ds(plan.first_at(chunk) + j, 1), :] = jnp.full((1, plan.lanes), first, jnp.int32)


def part_kernel(plan, chunks, gap_ref, first_ref, q_t, *refs):
    forward_part(plan, chunks, gap_ref, first_ref, q_t, refs[: len(chunks)], *refs[-5:])


def far_kernel(plan, chunks, others, gap_ref, first_ref, q_all, do_all, q_t, do_t, *refs):
    count = len(chunks)
    partial, refs = [refs[3 * i : 3 * i + 3] for i in range(others)], refs[3 * others :]
    kv_refs, refs = refs[:count], refs[count:]
    scale_refs, refs = refs[:others], refs[others:]
    (delta_ref, mixed_ref, q_grad_ref), refs = refs[:3], refs[3:]
    dkv_refs, (turned_ref, e_ref, w_ref, p_ref, ds_ref) = refs[:-5], refs[-5:]
    spans = [plan.at(tile) for tile in range(len(plan.tiles))]
    tops = [
        plan.scores(tile, chunks, kv_refs, q_t[:, at], e_ref, at, gap_ref, first_ref)
        for tile, at in enumerate(spans)
    ]
    plan.turn(kv_refs, turned_ref)
    for at in spans:
        for i, ref in enumerate(kv_refs):
            w_ref[plan.keys_at(i), at] = dot(plan.values(ref), do_t[:, at])
    inverses = []
    for at, top in zip(spans, tops):
        for top_ref, _, _ in partial:
            top = jnp.maximum(top, top_ref[:, at])
        total = plan.exponents(count, e_ref, at, top)
        factors = [jnp.exp2((top_ref[:, at] - top) * EXPO) for top_ref, _, _ in partial]
        for factor, (_, sum_ref, _) in zip(factors, partial):
            total = total + factor * sum_ref[:, at]
        inverse = 1.0 / total
        for factor, scale_ref in zip(factors, scale_refs):
            scale_ref[:, at] = factor * inverse
        inverses.append(inverse)
    for at, inverse in zip(spans, inverses):
        mixed = jnp.zeros((HD, plan.lanes), F32)
        for scale_ref, (_, _, mix_ref) in zip(scale_refs, partial):
            mixed = mixed + mix_ref[:, at] * scale_ref[:, at]
        for i in range(count):
            probs = (e_ref[plan.keys_at(i), at] * inverse).astype(BF)
            p_ref[plan.keys_at(i), at] = probs
            mixed = mixed + dot(turned_ref[pl.ds(HD, HD), plan.keys_at(i)], probs)
        mixed = mixed.astype(BF)
        mixed_ref[:, at] = mixed
        delta_ref[:, at] = jnp.sum(do_t[:, at].astype(F32) * mixed.astype(F32), axis=0, keepdims=True)
    for at, inverse in zip(spans, inverses):
        q_grad = jnp.zeros((HD, plan.lanes), F32)
        for i in range(count):
            probs = e_ref[plan.keys_at(i), at] * inverse
            grad_s = (probs * (w_ref[plan.keys_at(i), at] - delta_ref[:, at])).astype(BF)
            ds_ref[plan.keys_at(i), at] = grad_s
            q_grad = q_grad + dot(turned_ref[pl.ds(0, HD), plan.keys_at(i)], grad_s)
        q_grad_ref[:, at] = q_grad
    plan.back(dkv_refs, p_ref, ds_ref, q_all, do_all)


def back_kernel(plan, rows_at, last, order, q_all, do_all, do_t, e_ref, scale_ref, delta_ref, q_grad_in, *refs):
    count = len(rows_at)
    mixed_ref, refs = refs[:last], refs[last:]
    kv_refs, refs = refs[:count], refs[count + order :]
    refs, (turned_ref, p_ref, ds_ref) = refs[:-3], refs[-3:]
    outs, dkv_refs = refs[:-count], refs[-count:]
    spans = [plan.at(tile) for tile in range(len(plan.tiles))]
    for at in spans:
        for i, ref in enumerate(kv_refs):
            probs = e_ref[plan.keys_at(rows_at[i]), at] * scale_ref[:, at]
            p_ref[plan.keys_at(i), at] = probs.astype(BF)
            grad_s = (probs * (dot(plan.values(ref), do_t[:, at]) - delta_ref[:, at])).astype(BF)
            ds_ref[plan.keys_at(i), at] = grad_s
    plan.turn(kv_refs, turned_ref)
    plan.back(dkv_refs, p_ref, ds_ref, q_all, do_all)
    for tile, at in enumerate(spans):
        q_grad = q_grad_in[:, at]
        for i in range(count):
            q_grad = q_grad + dot(turned_ref[pl.ds(0, HD), plan.keys_at(i)], ds_ref[plan.keys_at(i), at])
        if last:
            out_ref = outs[plan.tiles[tile][0]]
            plan.store_heads(out_ref, 0, tile, mixed_ref[0][:, at].astype(F32))
            plan.store_heads(out_ref, 1, tile, q_grad * SCALING)
        else:
            outs[0][:, at] = q_grad


def add_kernel(*refs):
    total = refs[0][...].astype(F32)
    for ref in refs[1:-1]:
        total = total + ref[...].astype(F32)
    refs[-1][...] = total.astype(BF)


def sum_heads_kernel(parts, *refs):
    for m_z, out_ref in enumerate(refs[parts:]):
        total = refs[0][m_z].astype(F32)
        for ref in refs[1:parts]:
            total = total + ref[m_z].astype(F32)
        out_ref[...] = total.astype(BF)


def sum_z_kernel(kv, *refs):
    ins, outs = refs[:-kv], refs[-kv:]
    for s, out_ref in enumerate(outs):
        total = ins[0][s].astype(F32)
        for ref in ins[1:]:
            total = total + ref[s].astype(F32)
        out_ref[...] = total.astype(BF)


def sum_far_kernel(*refs):
    total = refs[0][...].astype(F32)
    for ref in refs[1:-1]:
        total = total + ref[...].astype(F32)
    refs[-1][...] = total


def finish_kv_kernel(kv, group_ref, *refs):
    key_ref, value_ref = refs[kv + 1 :]
    for g in range(kv):

        @pl.when(group_ref[0] == g)
        def _():
            for s in range(kv):
                cols = pl.ds((g ^ s) * HD, HD)
                key_ref[:, cols] = (refs[s][:, :HD].astype(F32) * SCALING).astype(BF)
                value_ref[:, cols] = refs[s][:, HD:]


def finish_q_kernel(kv, group_ref, *refs):
    att_ref, grad_ref, done_ref = refs[kv:]
    done_ref[...] = jnp.zeros_like(done_ref)
    width = refs[0].shape[2]
    for g in range(kv):

        @pl.when(group_ref[0] == g)
        def _():
            for s in range(kv):
                cols = pl.ds((g ^ s) * width, width)
                att_ref[:, cols] = refs[s][0]
                grad_ref[:, cols] = refs[s][1]


def shards(queries, key_vectors, value_vectors, out_grad, block_order):
    heads_devices = lax.axis_size("head")
    ctx_devices = lax.axis_size("ctx")
    halves, block_rows, query_width = queries.shape
    kv = key_vectors.shape[2] // HD
    rows = halves * block_rows
    width = query_width // kv
    cores = CORES if ctx_devices % CORES == 0 else 1
    z_devices = ctx_devices // cores
    spans = heads_devices // kv
    parts = 2 if z_devices % 2 == 0 else 1
    plan = Plan(kv, block_rows * heads_devices, block_rows, rows, width // HD, cores, z_devices, parts)
    z_part = plan.z_part
    head = lax.axis_index("head").astype(jnp.int32)
    place = jnp.stack([head, lax.axis_index("ctx").astype(jnp.int32)])
    info = jnp.concatenate([place, block_order])
    own_group = (head % kv).reshape(1)
    queries = queries.reshape(rows, query_width)
    out_grad = out_grad.reshape(rows, query_width)
    key_vectors = key_vectors.reshape(rows, kv * HD)
    value_vectors = value_vectors.reshape(rows, kv * HD)

    def bf(*dims):
        return jax.ShapeDtypeStruct(dims, BF)

    def f32(*dims):
        return jax.ShapeDtypeStruct(dims, F32)

    def i32(*dims):
        return jax.ShapeDtypeStruct(dims, jnp.int32)

    def with_swaps(blocks):
        return [blocks[0]] + [swap(blocks[s], "head", s) for s in range(1, kv)]

    dkv = bf(z_part, kv, rows, 2 * HD)

    def pick(block, g, size):
        out = block[:, :size]
        for i in range(1, kv):
            out = jnp.where(g == i, block[:, i * size : (i + 1) * size], out)
        return out

    def of_head(g):
        return jnp.concatenate([pick(key_vectors, g, HD), pick(value_vectors, g, HD)], axis=1)

    def queries_of(g):
        return jnp.stack([pick(queries, g, width), pick(out_grad, g, width)])

    piece = jnp.stack(with_swaps([of_head((head % kv) ^ s) for s in range(kv)]))
    q_parts = with_swaps([queries_of((head % kv) ^ s) for s in range(kv)])
    pieces = [swap(piece, "ctx", m * cores) for m in reversed(range(1, z_devices))]
    pieces = [piece] + pieces[::-1]
    query_rows = plan.query_rows
    chunks = [(a, core, p) for a in range(spans) for core in range(cores) for p in range(parts)]
    q_all, do_all, q_t, do_t, gap, firsts = call(
        functools.partial(turn_kernel, plan, chunks),
        "turn",
        (info, *q_parts),
        [
            *[bf(query_rows, HD)] * 2,
            *[bf(HD, query_rows)] * 2,
            i32(len(plan.tiles) * block_rows, plan.lanes),
            i32(len(chunks) * plan.slices, plan.lanes),
        ],
        [SMEM] + [VMEM] * kv,
    )
    column, handed, order = [None] * parts, [None] * parts, []
    for p in reversed(range(parts)):
        parcels = [pieces[m] for m in plan.zone(p)]
        extra = [column[p + 1], *order] if order else []
        *handed_on, column[p] = call(
            functools.partial(stack_kernel, len(parcels)),
            "stack",
            (*parcels, *extra),
            [dkv] * (1 + bool(extra)),
        )
        handed[p] = column[p]
        if extra:
            handed[p + 1] = handed_on[0]
        order = list(after(q_parts[1:], [info])) if p else []
    columns = [[swap(half, "head", a * kv) for half in column] for a in range(1, spans)]
    near_kv = [column] + [[swap(half, "ctx", core) for half in handed] for core in range(1, cores)]
    near_flat = [half for pair in near_kv for half in pair]
    each = range(parts)
    near_chunks = [(0, core, p) for core in range(cores) for p in each]
    mid_chunks = [(a, 0, p) for a in range(1, spans) for p in each]
    far_chunks = [(a, core, p) for a in range(1, spans) for core in range(1, cores) for p in each]

    keys = plan.chunk_keys
    query_rows = plan.query_rows
    row, column_out = f32(1, query_rows), f32(HD, query_rows)

    def forward(name, chunks, kv_refs, order):
        size = len(chunks) * keys
        return call(
            functools.partial(part_kernel, plan, chunks),
            name,
            (gap, firsts, q_t, *kv_refs, *order),
            [f32(size, query_rows), row, row, column_out],
            None,
            [pltpu.VMEM((2 * HD, size), BF)],
            size * 4 * HD,
            8 * size * query_rows * HD,
        )

    mids, order = [None] * parts, []
    for p in reversed(each):
        if p + 1 < parts or parts == 1:
            near_e, *near = forward("attend_near", near_chunks, near_flat, order)
            order = [near[0]]
            for pair in columns:
                pair[p] = after([pair[p]], order)[0]
        mids[p] = forward("attend_mid", [c for c in mid_chunks if c[2] == p], [pair[p] for pair in columns], order)
        order = [mids[p][1]]
    far_kv = [swap(pair[p], "ctx", core) for pair in columns for core in range(1, cores) for p in each]
    far_keys = len(far_kv) * keys
    outs = call(
        functools.partial(far_kernel, plan, far_chunks, 1 + parts),
        "attend_far",
        (gap, firsts, q_all, do_all, q_t, do_t, *near, *[r for mid in mids for r in mid[1:]], *far_kv),
        [row] * (2 + parts) + [bf(HD, query_rows), column_out] + [dkv] * len(far_kv),
        None,
        [
            pltpu.VMEM((2 * HD, far_keys), BF),
            pltpu.VMEM((far_keys, query_rows), F32),
            pltpu.VMEM((far_keys, query_rows), F32),
            pltpu.VMEM((far_keys, query_rows), BF),
            pltpu.VMEM((far_keys, query_rows), BF),
        ],
        far_keys * (4 * HD + 12 * query_rows),
        16 * far_keys * query_rows * HD,
    )
    (near_scale, *mid_scales), outs = outs[: 1 + parts], outs[1 + parts :]
    (delta, mixed, q_grad), far_dkv = outs[:3], outs[3:]

    def back(rows_at, last, e, scale, q_grad, kv_refs, order):
        count = len(rows_at)
        q_outs = [bf(2, rows, width)] * kv if last else [column_out]
        outs = call(
            functools.partial(back_kernel, plan, rows_at, last, len(order)),
            "attend_back",
            (q_all, do_all, do_t, e, scale, delta, q_grad, *[mixed] * last, *kv_refs, *order),
            q_outs + [dkv] * count,
            None,
            [
                pltpu.VMEM((2 * HD, count * keys), BF),
                pltpu.VMEM((count * keys, query_rows), BF),
                pltpu.VMEM((count * keys, query_rows), BF),
            ],
            count * keys * (4 * HD + 4 * query_rows),
            12 * count * keys * query_rows * HD,
        )
        return outs[: len(q_outs)], outs[len(q_outs) :]

    sums = [[] for _ in range(parts)]
    totals = []
    for p in reversed(each):
        mid_kv = [pair[p] for pair in columns]
        (q_grad,), mid_dkv = back(
            list(range(len(mid_kv))), False, mids[p][0], mid_scales[p], q_grad, mid_kv, []
        )
        for a in range(spans - 1):
            both = [mid_dkv[a]]
            for core in range(1, cores):
                ours = far_dkv[(a * (cores - 1) + core - 1) * parts + p]
                both.append(swap(ours, "ctx", core))
            totals += call(add_kernel, "sum_cores", after(both, totals[-1:]), [dkv])
            sums[p].append(swap(totals[-1], "head", (a + 1) * kv))
    order = [swap(totals[-1][0, 0, :, :HD], "ctx", 1)] if cores > 1 else []
    for core in reversed(range(cores)):
        outs, parts_dkv = back(
            [core * parts + p for p in each], core == 0, near_e, near_scale, q_grad, near_kv[core], order
        )
        q_grad = outs[0]
        for p in range(parts):
            sums[p].append(swap(parts_dkv[p], "ctx", core) if core else parts_dkv[p])
    q_parts = outs[:kv]
    z_parts = [None] * z_devices
    for p in range(parts):
        totals = call(
            functools.partial(sum_heads_kernel, len(sums[p])),
            "sum_heads",
            sums[p],
            [bf(kv, rows, 2 * HD)] * z_part,
        )

        if p == parts - 1:
            q_parts = with_swaps(after(q_parts, totals[:1]))
        for m, total in zip(plan.zone(p), totals):
            z_parts[m] = swap(total, "ctx", m * cores) if m else total
    ordered = [z_parts[m] for p in each for m in plan.zone(p)]
    if parts > 1:
        far_z = call(sum_far_kernel, "sum_far_z", ordered[:z_part], [f32(kv, rows, 2 * HD)], flops=1 << 32)
        ordered = [*far_z, *ordered[z_part:]]
    pair_parts = call(
        functools.partial(sum_z_kernel, kv), "sum_z", ordered, [bf(rows, 2 * HD)] * kv
    )
    pair_parts = with_swaps(pair_parts)
    attended, query_grad, done = call(
        functools.partial(finish_q_kernel, kv),
        "finish_q",
        (own_group, *q_parts),
        [bf(rows, query_width)] * 2 + [f32(8, HD)],
        [SMEM] + [VMEM] * kv,
    )
    key_grad, value_grad = call(
        functools.partial(finish_kv_kernel, kv),
        "finish_kv",
        (own_group, *pair_parts, done),
        [bf(rows, kv * HD)] * 2,
        [SMEM] + [VMEM] * (kv + 1),
    )
    return (
        attended.reshape(halves, block_rows, query_width),
        query_grad.reshape(halves, block_rows, query_width),
        key_grad.reshape(halves, block_rows, kv * HD),
        value_grad.reshape(halves, block_rows, kv * HD),
    )


def solution(mesh):
    split = P("ctx", "head", None)
    return jax.shard_map(
        shards,
        mesh=mesh,
        in_specs=(split, split, split, split, P()),
        out_specs=(split, split, split, split),
        check_vma=False,
    )
```

```python
import functools
import math

import jax
import jax.numpy as jnp
from jax import lax
from jax.experimental import pallas as pl
from jax.experimental.pallas import tpu as pltpu
from jax.sharding import PartitionSpec as P

HD = 128
CORES = 2
BF = jnp.bfloat16
F32 = jnp.float32
LOWEST = -1e30
FLOOR = -1e29
SCALING = 1.0 / math.sqrt(HD)
EXPO = SCALING * math.log2(math.e)

VMEM = pl.BlockSpec(memory_space=pltpu.VMEM)
SMEM = pl.BlockSpec(memory_space=pltpu.SMEM)


def swap(block, axis, mask):
    size = lax.axis_size(axis)
    return lax.ppermute(block, axis, [(i, i ^ mask) for i in range(size)])


def nbytes(arrays):
    return sum(math.prod(a.shape) * a.dtype.itemsize for a in arrays)


def after(blocks, earlier):
    if not earlier:
        return tuple(blocks)
    return lax.optimization_barrier((tuple(blocks), tuple(earlier)))[0]


def call(kernel, name, ins, outs, specs=None, scratch=(), extra=0, flops=0):
    limit = nbytes(ins) + nbytes(outs) + extra + (12 << 20)
    return pl.pallas_call(
        kernel,
        out_shape=list(outs),
        in_specs=specs or [VMEM] * len(ins),
        out_specs=[VMEM] * len(outs),
        scratch_shapes=list(scratch),
        compiler_params=pltpu.CompilerParams(vmem_limit_bytes=min(limit, 60 << 20)),
        cost_estimate=pl.CostEstimate(
            flops=flops, bytes_accessed=nbytes(ins) + nbytes(outs), transcendentals=0
        ),
        name=name,
    )(*ins)


def dot(left, right):
    return jnp.dot(left, right, preferred_element_type=F32)


def dot_rows(left, right):
    return lax.dot_general(left, right, (((1,), (1,)), ((), ())), preferred_element_type=F32)


def stack_kernel(count, *refs):
    ins, refs = refs[:count], refs[count:]
    passed = len(refs) // 2
    refs, out_ref = refs[:-1], refs[-1]
    for i, ref in enumerate(ins):
        out_ref[i] = ref[...]
    if passed:
        refs[-1][...] = refs[0][...]


class Plan:
    def __init__(self, kv, block_len, block_rows, rows, group, cores, z_devices, parts):
        self.kv, self.block_len, self.block_rows, self.rows = kv, block_len, block_rows, rows
        self.group, self.cores, self.parts, self.z_part = group, cores, parts, z_devices // parts
        self.blocks = rows // block_rows
        self.tile_rows = block_rows if block_rows % 16 == 0 else rows
        self.lanes = group * self.tile_rows
        self.query_rows = kv * group * rows
        self.chunk_keys = self.z_part * kv * rows
        self.slices = self.chunk_keys // block_rows
        self.tiles = [(s, start) for s in range(kv) for start in range(0, rows, self.tile_rows)]

    def zone(self, part):
        first = (self.parts - 1 - part) * self.z_part
        return range(first, first + self.z_part)

    def at(self, tile):
        return pl.ds(tile * self.lanes, self.lanes)

    def keys_at(self, i):
        return pl.ds(i * self.chunk_keys, self.chunk_keys)

    def gap(self, tile, info_ref):
        s, start = self.tiles[tile]
        head, ctx = info_ref[0], info_ref[1]
        row = lax.broadcasted_iota(jnp.int32, (1, self.lanes), 1) % self.tile_rows + start
        pos = jnp.zeros((1, self.lanes), jnp.int32)
        for b in range(start // self.block_rows, -(-(start + self.tile_rows) // self.block_rows)):
            first = info_ref[2 + ctx * self.blocks + b] * self.block_len + (head ^ s) * self.block_rows
            pos = jnp.where(row // self.block_rows == b, first + row % self.block_rows, pos)
        return pos - lax.broadcasted_iota(jnp.int32, (self.block_rows, self.lanes), 0)

    def firsts(self, chunk, info_ref):
        head, ctx = info_ref[0], info_ref[1]
        a, core, part = chunk
        for j in range(self.slices):
            m, rest = divmod(j, self.kv * self.blocks)
            s, b = divmod(rest, self.blocks)
            stored = (ctx ^ (self.zone(part)[m] * self.cores + core)) * self.blocks + b
            yield info_ref[2 + stored] * self.block_len + (head ^ (a * self.kv + s)) * self.block_rows

    def first_at(self, chunk):
        a, core, part = chunk
        return ((a * self.cores + core) * self.parts + part) * self.slices

    def masked(self, scores, gap, chunk, first_ref):
        for j in range(self.slices):
            row = j * self.block_rows
            first = first_ref[pl.ds(self.first_at(chunk) + j, 1), :]
            yield row, jnp.where(gap >= first, scores[row : row + self.block_rows], LOWEST)

    def turn(self, kv_refs, turned_ref):
        for i, ref in enumerate(kv_refs):
            turned_ref[:, self.keys_at(i)] = ref[...].reshape(self.chunk_keys, 2 * HD).T

    def keys(self, ref):
        return ref[:, :, :, :HD].reshape(self.chunk_keys, HD)

    def values(self, ref):
        return ref[:, :, :, HD:].reshape(self.chunk_keys, HD)

    def fold(self, block):
        return block.reshape(block.shape[0] // 8, 8, self.lanes)

    def scores(self, tile, chunks, kv_refs, q_t, e_ref, cols, gap_ref, first_ref):
        gap = gap_ref[pl.ds(tile * self.block_rows, self.block_rows), :]
        top = jnp.full((8, self.lanes), FLOOR, F32)
        for i, ref in enumerate(kv_refs):
            scores = dot(self.keys(ref), q_t)
            for row, part in self.masked(scores, gap, chunks[i], first_ref):
                e_ref[pl.ds(i * self.chunk_keys + row, part.shape[0]), cols] = part
                top = jnp.maximum(top, jnp.max(self.fold(part), axis=0))
        return jnp.max(top, axis=0, keepdims=True)

    def exponents(self, count, e_ref, cols, top):
        total = jnp.zeros((8, self.lanes), F32)
        for i in range(count):
            part = jnp.exp2(e_ref[self.keys_at(i), cols] * EXPO - top * EXPO)
            e_ref[self.keys_at(i), cols] = part
            total = total + jnp.sum(self.fold(part), axis=0)
        return jnp.sum(total, axis=0, keepdims=True)

    def store_heads(self, out_ref, kind, tile, turned):
        s, start = self.tiles[tile]
        block = turned.T.astype(BF)
        for n in range(self.group):
            piece = block[n * self.tile_rows : (n + 1) * self.tile_rows]
            out_ref[kind, pl.ds(start, self.tile_rows), pl.ds(n * HD, HD)] = piece

    def back(self, dkv_refs, p_ref, ds_ref, q_ref, do_ref):
        shape = (self.z_part, self.kv, self.rows, HD)
        for i, out_ref in enumerate(dkv_refs):
            at = self.keys_at(i)
            out_ref[:, :, :, :HD] = dot(ds_ref[at, :], q_ref[...]).astype(BF).reshape(shape)
            out_ref[:, :, :, HD:] = dot(p_ref[at, :], do_ref[...]).astype(BF).reshape(shape)


def forward_part(plan, chunks, gap_ref, first_ref, q_t, kv_refs, e_ref, top_ref, sum_ref, mix_ref, turned_ref):
    spans = [plan.at(tile) for tile in range(len(plan.tiles))]
    tops = [
        plan.scores(tile, chunks, kv_refs, q_t[:, at], e_ref, at, gap_ref, first_ref)
        for tile, at in enumerate(spans)
    ]
    plan.turn(kv_refs, turned_ref)
    for at, top in zip(spans, tops):
        top_ref[:, at] = top
        sum_ref[:, at] = plan.exponents(len(chunks), e_ref, at, top)
    for at in spans:
        mixed = jnp.zeros((HD, plan.lanes), F32)
        for i in range(len(chunks)):
            weights = e_ref[plan.keys_at(i), at].astype(BF)
            mixed = mixed + dot(turned_ref[pl.ds(HD, HD), plan.keys_at(i)], weights)
        mix_ref[:, at] = mixed


def place_kernel(plan, chunks, info_ref, gap_ref, first_ref):
    for tile in range(len(plan.tiles)):
        gap_ref[pl.ds(tile * plan.block_rows, plan.block_rows), :] = plan.gap(tile, info_ref)
    for chunk in chunks:
        for j, first in enumerate(plan.firsts(chunk, info_ref)):
            first_ref[pl.ds(plan.first_at(chunk) + j, 1), :] = jnp.full((1, plan.lanes), first, jnp.int32)


def turn_kernel(plan, *refs):
    q_parts, (q_all, do_all, q_t, do_t) = refs[:-4], refs[-4:]
    for tile, (s, start) in enumerate(plan.tiles):
        span = pl.ds(start, plan.tile_rows)
        for n in range(plan.group):
            at = pl.ds(tile * plan.lanes + n * plan.tile_rows, plan.tile_rows)
            q_all[at, :] = q_parts[s][0, span, pl.ds(n * HD, HD)]
            do_all[at, :] = q_parts[s][1, span, pl.ds(n * HD, HD)]
        at = plan.at(tile)
        q_t[:, at] = q_all[at, :].T
        do_t[:, at] = do_all[at, :].T


def part_kernel(plan, chunks, gap_ref, first_ref, q_t, *refs):
    forward_part(plan, chunks, gap_ref, first_ref, q_t, refs[: len(chunks)], *refs[-5:])


def far_kernel(plan, chunks, others, gap_ref, first_ref, q_all, do_all, q_t, do_t, *refs):
    count = len(chunks)
    partial, refs = [refs[3 * i : 3 * i + 3] for i in range(others)], refs[3 * others :]
    kv_refs, refs = refs[:count], refs[count:]
    scale_refs, refs = refs[:others], refs[others:]
    (delta_ref, mixed_ref, q_grad_ref), refs = refs[:3], refs[3:]
    dkv_refs, (turned_ref, e_ref, w_ref, p_ref, ds_ref) = refs[:-5], refs[-5:]
    spans = [plan.at(tile) for tile in range(len(plan.tiles))]
    tops = [
        plan.scores(tile, chunks, kv_refs, q_t[:, at], e_ref, at, gap_ref, first_ref)
        for tile, at in enumerate(spans)
    ]
    plan.turn(kv_refs, turned_ref)
    for at in spans:
        for i, ref in enumerate(kv_refs):
            w_ref[plan.keys_at(i), at] = dot(plan.values(ref), do_t[:, at])
    inverses = []
    for at, top in zip(spans, tops):
        for top_ref, _, _ in partial:
            top = jnp.maximum(top, top_ref[:, at])
        total = plan.exponents(count, e_ref, at, top)
        factors = [jnp.exp2((top_ref[:, at] - top) * EXPO) for top_ref, _, _ in partial]
        for factor, (_, sum_ref, _) in zip(factors, partial):
            total = total + factor * sum_ref[:, at]
        inverse = 1.0 / total
        for factor, scale_ref in zip(factors, scale_refs):
            scale_ref[:, at] = factor * inverse
        inverses.append(inverse)
    for at, inverse in zip(spans, inverses):
        mixed = jnp.zeros((HD, plan.lanes), F32)
        for scale_ref, (_, _, mix_ref) in zip(scale_refs, partial):
            mixed = mixed + mix_ref[:, at] * scale_ref[:, at]
        for i in range(count):
            probs = (e_ref[plan.keys_at(i), at] * inverse).astype(BF)
            p_ref[plan.keys_at(i), at] = probs
            mixed = mixed + dot(turned_ref[pl.ds(HD, HD), plan.keys_at(i)], probs)
        mixed = mixed.astype(BF)
        mixed_ref[:, at] = mixed
        delta_ref[:, at] = jnp.sum(do_t[:, at].astype(F32) * mixed.astype(F32), axis=0, keepdims=True)
    for at, inverse in zip(spans, inverses):
        q_grad = jnp.zeros((HD, plan.lanes), F32)
        for i in range(count):
            probs = e_ref[plan.keys_at(i), at] * inverse
            grad_s = (probs * (w_ref[plan.keys_at(i), at] - delta_ref[:, at])).astype(BF)
            ds_ref[plan.keys_at(i), at] = grad_s
            q_grad = q_grad + dot(turned_ref[pl.ds(0, HD), plan.keys_at(i)], grad_s)
        q_grad_ref[:, at] = q_grad
    plan.back(dkv_refs, p_ref, ds_ref, q_all, do_all)


def back_kernel(plan, rows_at, last, order, q_all, do_all, do_t, e_ref, scale_ref, delta_ref, q_grad_in, *refs):
    count = len(rows_at)
    mixed_ref, refs = refs[:last], refs[last:]
    kv_refs, refs = refs[:count], refs[count + order :]
    refs, (turned_ref, p_ref, ds_ref) = refs[:-3], refs[-3:]
    outs, dkv_refs = refs[:-count], refs[-count:]
    spans = [plan.at(tile) for tile in range(len(plan.tiles))]
    for at in spans:
        for i, ref in enumerate(kv_refs):
            probs = e_ref[plan.keys_at(rows_at[i]), at] * scale_ref[:, at]
            p_ref[plan.keys_at(i), at] = probs.astype(BF)
            grad_s = (probs * (dot(plan.values(ref), do_t[:, at]) - delta_ref[:, at])).astype(BF)
            ds_ref[plan.keys_at(i), at] = grad_s
    plan.turn(kv_refs, turned_ref)
    plan.back(dkv_refs, p_ref, ds_ref, q_all, do_all)
    for tile, at in enumerate(spans):
        q_grad = q_grad_in[:, at]
        for i in range(count):
            q_grad = q_grad + dot(turned_ref[pl.ds(0, HD), plan.keys_at(i)], ds_ref[plan.keys_at(i), at])
        if last:
            out_ref = outs[plan.tiles[tile][0]]
            plan.store_heads(out_ref, 0, tile, mixed_ref[0][:, at].astype(F32))
            plan.store_heads(out_ref, 1, tile, q_grad * SCALING)
        else:
            outs[0][:, at] = q_grad


def add_kernel(*refs):
    total = refs[0][...].astype(F32)
    for ref in refs[1:-1]:
        total = total + ref[...].astype(F32)
    refs[-1][...] = total.astype(BF)


def sum_heads_kernel(parts, *refs):
    for m_z, out_ref in enumerate(refs[parts:]):
        total = refs[0][m_z].astype(F32)
        for ref in refs[1:parts]:
            total = total + ref[m_z].astype(F32)
        out_ref[...] = total.astype(BF)


def sum_z_kernel(kv, *refs):
    ins, outs = refs[:-kv], refs[-kv:]
    for s, out_ref in enumerate(outs):
        total = ins[0][s].astype(F32)
        for ref in ins[1:]:
            total = total + ref[s].astype(F32)
        out_ref[...] = total.astype(BF)


def sum_far_kernel(*refs):
    total = refs[0][...].astype(F32)
    for ref in refs[1:-1]:
        total = total + ref[...].astype(F32)
    refs[-1][...] = total


def finish_kv_kernel(kv, group_ref, *refs):
    key_ref, value_ref = refs[kv + 1 :]
    for g in range(kv):

        @pl.when(group_ref[0] == g)
        def _():
            for s in range(kv):
                cols = pl.ds((g ^ s) * HD, HD)
                key_ref[:, cols] = (refs[s][:, :HD].astype(F32) * SCALING).astype(BF)
                value_ref[:, cols] = refs[s][:, HD:]


def finish_q_kernel(kv, group_ref, *refs):
    att_ref, grad_ref, done_ref = refs[kv:]
    done_ref[...] = jnp.zeros_like(done_ref)
    width = refs[0].shape[2]
    for g in range(kv):

        @pl.when(group_ref[0] == g)
        def _():
            for s in range(kv):
                cols = pl.ds((g ^ s) * width, width)
                att_ref[:, cols] = refs[s][0]
                grad_ref[:, cols] = refs[s][1]


def shards(queries, key_vectors, value_vectors, out_grad, block_order):
    heads_devices = lax.axis_size("head")
    ctx_devices = lax.axis_size("ctx")
    halves, block_rows, query_width = queries.shape
    kv = key_vectors.shape[2] // HD
    rows = halves * block_rows
    width = query_width // kv
    cores = CORES if ctx_devices % CORES == 0 else 1
    z_devices = ctx_devices // cores
    spans = heads_devices // kv
    parts = 2 if z_devices % 2 == 0 else 1
    plan = Plan(kv, block_rows * heads_devices, block_rows, rows, width // HD, cores, z_devices, parts)
    z_part = plan.z_part
    head = lax.axis_index("head").astype(jnp.int32)
    place = jnp.stack([head, lax.axis_index("ctx").astype(jnp.int32)])
    info = jnp.concatenate([place, block_order])
    own_group = (head % kv).reshape(1)
    queries = queries.reshape(rows, query_width)
    out_grad = out_grad.reshape(rows, query_width)
    key_vectors = key_vectors.reshape(rows, kv * HD)
    value_vectors = value_vectors.reshape(rows, kv * HD)

    def bf(*dims):
        return jax.ShapeDtypeStruct(dims, BF)

    def f32(*dims):
        return jax.ShapeDtypeStruct(dims, F32)

    def i32(*dims):
        return jax.ShapeDtypeStruct(dims, jnp.int32)

    def with_swaps(blocks):
        return [blocks[0]] + [swap(blocks[s], "head", s) for s in range(1, kv)]

    dkv = bf(z_part, kv, rows, 2 * HD)

    def pick(block, g, size):
        out = block[:, :size]
        for i in range(1, kv):
            out = jnp.where(g == i, block[:, i * size : (i + 1) * size], out)
        return out

    def of_head(g):
        return jnp.concatenate([pick(key_vectors, g, HD), pick(value_vectors, g, HD)], axis=1)

    def queries_of(g):
        return jnp.stack([pick(queries, g, width), pick(out_grad, g, width)])

    piece = jnp.stack(with_swaps([of_head((head % kv) ^ s) for s in range(kv)]))
    q_parts = with_swaps([queries_of((head % kv) ^ s) for s in range(kv)])
    pieces = [swap(piece, "ctx", m * cores) for m in reversed(range(1, z_devices))]
    pieces = [piece] + pieces[::-1]
    query_rows = plan.query_rows
    chunks = [(a, core, p) for a in range(spans) for core in range(cores) for p in range(parts)]
    gap, firsts = call(
        functools.partial(place_kernel, plan, chunks),
        "place",
        (info,),
        [i32(len(plan.tiles) * block_rows, plan.lanes), i32(len(chunks) * plan.slices, plan.lanes)],
        [SMEM],
    )
    q_all, do_all, q_t, do_t = call(
        functools.partial(turn_kernel, plan),
        "turn",
        q_parts,
        [bf(query_rows, HD)] * 2 + [bf(HD, query_rows)] * 2,
    )
    column, handed, order = [None] * parts, [None] * parts, []
    for p in reversed(range(parts)):
        parcels = [pieces[m] for m in plan.zone(p)]
        extra = [column[p + 1], *order] if order else []
        *handed_on, column[p] = call(
            functools.partial(stack_kernel, len(parcels)),
            "stack",
            (*parcels, *extra),
            [dkv] * (1 + bool(extra)),
        )
        handed[p] = column[p]
        if extra:
            handed[p + 1] = handed_on[0]
        order = [*q_parts[1:], firsts] if p else []
    columns = [[swap(half, "head", a * kv) for half in column] for a in range(1, spans)]
    near_kv = [column] + [[swap(half, "ctx", core) for half in handed] for core in range(1, cores)]
    near_flat = [half for pair in near_kv for half in pair]
    each = range(parts)
    near_chunks = [(0, core, p) for core in range(cores) for p in each]
    mid_chunks = [(a, 0, p) for a in range(1, spans) for p in each]
    far_chunks = [(a, core, p) for a in range(1, spans) for core in range(1, cores) for p in each]

    keys = plan.chunk_keys
    query_rows = plan.query_rows
    row, column_out = f32(1, query_rows), f32(HD, query_rows)

    def forward(name, chunks, kv_refs, order):
        size = len(chunks) * keys
        return call(
            functools.partial(part_kernel, plan, chunks),
            name,
            (gap, firsts, q_t, *kv_refs, *order),
            [f32(size, query_rows), row, row, column_out],
            None,
            [pltpu.VMEM((2 * HD, size), BF)],
            size * 4 * HD,
            8 * size * query_rows * HD,
        )

    mids, order = [None] * parts, []
    for p in reversed(each):
        if p + 1 < parts or parts == 1:
            near_e, *near = forward("attend_near", near_chunks, near_flat, order)
            order = [near[0]]
            for pair in columns:
                pair[p] = after([pair[p]], order)[0]
        mids[p] = forward("attend_mid", [c for c in mid_chunks if c[2] == p], [pair[p] for pair in columns], order)
        order = [mids[p][1]]
    far_kv = [swap(pair[p], "ctx", core) for pair in columns for core in range(1, cores) for p in each]
    far_keys = len(far_kv) * keys
    outs = call(
        functools.partial(far_kernel, plan, far_chunks, 1 + parts),
        "attend_far",
        (gap, firsts, q_all, do_all, q_t, do_t, *near, *[r for mid in mids for r in mid[1:]], *far_kv),
        [row] * (2 + parts) + [bf(HD, query_rows), column_out] + [dkv] * len(far_kv),
        None,
        [
            pltpu.VMEM((2 * HD, far_keys), BF),
            pltpu.VMEM((far_keys, query_rows), F32),
            pltpu.VMEM((far_keys, query_rows), F32),
            pltpu.VMEM((far_keys, query_rows), BF),
            pltpu.VMEM((far_keys, query_rows), BF),
        ],
        far_keys * (4 * HD + 12 * query_rows),
        16 * far_keys * query_rows * HD,
    )
    (near_scale, *mid_scales), outs = outs[: 1 + parts], outs[1 + parts :]
    (delta, mixed, q_grad), far_dkv = outs[:3], outs[3:]

    def back(rows_at, last, e, scale, q_grad, kv_refs, order):
        count = len(rows_at)
        q_outs = [bf(2, rows, width)] * kv if last else [column_out]
        outs = call(
            functools.partial(back_kernel, plan, rows_at, last, len(order)),
            "attend_back",
            (q_all, do_all, do_t, e, scale, delta, q_grad, *[mixed] * last, *kv_refs, *order),
            q_outs + [dkv] * count,
            None,
            [
                pltpu.VMEM((2 * HD, count * keys), BF),
                pltpu.VMEM((count * keys, query_rows), BF),
                pltpu.VMEM((count * keys, query_rows), BF),
            ],
            count * keys * (4 * HD + 4 * query_rows),
            12 * count * keys * query_rows * HD,
        )
        return outs[: len(q_outs)], outs[len(q_outs) :]

    sums = [[] for _ in range(parts)]
    totals = []
    for p in reversed(each):
        mid_kv = [pair[p] for pair in columns]
        (q_grad,), mid_dkv = back(
            list(range(len(mid_kv))), False, mids[p][0], mid_scales[p], q_grad, mid_kv, []
        )
        for a in range(spans - 1):
            both = [mid_dkv[a]]
            for core in range(1, cores):
                ours = far_dkv[(a * (cores - 1) + core - 1) * parts + p]
                both.append(swap(ours, "ctx", core))
            totals += call(add_kernel, "sum_cores", after(both, totals[-1:]), [dkv])
            sums[p].append(swap(totals[-1], "head", (a + 1) * kv))
    order = [swap(totals[-1][0, 0, :, :HD], "ctx", 1)] if cores > 1 else []
    for core in reversed(range(cores)):
        outs, parts_dkv = back(
            [core * parts + p for p in each], core == 0, near_e, near_scale, q_grad, near_kv[core], order
        )
        q_grad = outs[0]
        for p in range(parts):
            sums[p].append(swap(parts_dkv[p], "ctx", core) if core else parts_dkv[p])
    q_parts = outs[:kv]
    z_parts = [None] * z_devices
    for p in range(parts):
        totals = call(
            functools.partial(sum_heads_kernel, len(sums[p])),
            "sum_heads",
            sums[p],
            [bf(kv, rows, 2 * HD)] * z_part,
        )

        if p == parts - 1:
            q_parts = with_swaps(after(q_parts, totals[:1]))
        for m, total in zip(plan.zone(p), totals):
            z_parts[m] = swap(total, "ctx", m * cores) if m else total
    ordered = [z_parts[m] for p in each for m in plan.zone(p)]
    if parts > 1:
        far_z = call(sum_far_kernel, "sum_far_z", ordered[:z_part], [f32(kv, rows, 2 * HD)], flops=1 << 32)
        ordered = [*far_z, *ordered[z_part:]]
    pair_parts = call(
        functools.partial(sum_z_kernel, kv), "sum_z", ordered, [bf(rows, 2 * HD)] * kv
    )
    pair_parts = with_swaps(pair_parts)
    attended, query_grad, done = call(
        functools.partial(finish_q_kernel, kv),
        "finish_q",
        (own_group, *q_parts),
        [bf(rows, query_width)] * 2 + [f32(8, HD)],
        [SMEM] + [VMEM] * kv,
    )
    key_grad, value_grad = call(
        functools.partial(finish_kv_kernel, kv),
        "finish_kv",
        (own_group, *pair_parts, done),
        [bf(rows, kv * HD)] * 2,
        [SMEM] + [VMEM] * (kv + 1),
    )
    return (
        attended.reshape(halves, block_rows, query_width),
        query_grad.reshape(halves, block_rows, query_width),
        key_grad.reshape(halves, block_rows, kv * HD),
        value_grad.reshape(halves, block_rows, kv * HD),
    )


def solution(mesh):
    split = P("ctx", "head", None)
    return jax.shard_map(
        shards,
        mesh=mesh,
        in_specs=(split, split, split, split, P()),
        out_specs=(split, split, split, split),
        check_vma=False,
    )
```

```python
import functools
import math

import jax
import jax.numpy as jnp
from jax import lax
from jax.experimental import pallas as pl
from jax.experimental.pallas import tpu as pltpu
from jax.sharding import PartitionSpec as P

HD = 128
CORES = 2
BF = jnp.bfloat16
F32 = jnp.float32
LOWEST = -1e30
FLOOR = -1e29
SCALING = 1.0 / math.sqrt(HD)
EXPO = SCALING * math.log2(math.e)

VMEM = pl.BlockSpec(memory_space=pltpu.VMEM)
SMEM = pl.BlockSpec(memory_space=pltpu.SMEM)


def swap(block, axis, mask):
    size = lax.axis_size(axis)
    return lax.ppermute(block, axis, [(i, i ^ mask) for i in range(size)])


def nbytes(arrays):
    return sum(math.prod(a.shape) * a.dtype.itemsize for a in arrays)


def after(blocks, earlier):
    if not earlier:
        return tuple(blocks)
    return lax.optimization_barrier((tuple(blocks), tuple(earlier)))[0]


def call(kernel, name, ins, outs, specs=None, scratch=(), extra=0, flops=0):
    limit = nbytes(ins) + nbytes(outs) + extra + (12 << 20)
    return pl.pallas_call(
        kernel,
        out_shape=list(outs),
        in_specs=specs or [VMEM] * len(ins),
        out_specs=[VMEM] * len(outs),
        scratch_shapes=list(scratch),
        compiler_params=pltpu.CompilerParams(vmem_limit_bytes=min(limit, 60 << 20)),
        cost_estimate=pl.CostEstimate(
            flops=flops, bytes_accessed=nbytes(ins) + nbytes(outs), transcendentals=0
        ),
        name=name,
    )(*ins)


def dot(left, right):
    return jnp.dot(left, right, preferred_element_type=F32)


def dot_rows(left, right):
    return lax.dot_general(left, right, (((1,), (1,)), ((), ())), preferred_element_type=F32)


def stack_kernel(count, *refs):
    ins, refs = refs[:count], refs[count:]
    passed = len(refs) // 2
    refs, out_ref = refs[:-1], refs[-1]
    for i, ref in enumerate(ins):
        out_ref[i] = ref[...]
    if passed:
        refs[-1][...] = refs[0][...]


class Plan:
    def __init__(self, kv, block_len, block_rows, rows, group, cores, z_devices, parts):
        self.kv, self.block_len, self.block_rows, self.rows = kv, block_len, block_rows, rows
        self.group, self.cores, self.parts, self.z_part = group, cores, parts, z_devices // parts
        self.blocks = rows // block_rows
        self.tile_rows = block_rows if block_rows % 16 == 0 else rows
        self.lanes = group * self.tile_rows
        self.query_rows = kv * group * rows
        self.chunk_keys = self.z_part * kv * rows
        self.slices = self.chunk_keys // block_rows
        self.tiles = [(s, start) for s in range(kv) for start in range(0, rows, self.tile_rows)]

    def zone(self, part):
        first = (self.parts - 1 - part) * self.z_part
        return range(first, first + self.z_part)

    def at(self, tile):
        return pl.ds(tile * self.lanes, self.lanes)

    def keys_at(self, i):
        return pl.ds(i * self.chunk_keys, self.chunk_keys)

    def gap(self, tile, info_ref):
        s, start = self.tiles[tile]
        (place_ref, order_ref) = info_ref
        head, ctx = place_ref[0], place_ref[1]
        row = lax.broadcasted_iota(jnp.int32, (1, self.lanes), 1) % self.tile_rows + start
        pos = jnp.zeros((1, self.lanes), jnp.int32)
        for b in range(start // self.block_rows, -(-(start + self.tile_rows) // self.block_rows)):
            first = order_ref[ctx * self.blocks + b] * self.block_len + (head ^ s) * self.block_rows
            pos = jnp.where(row // self.block_rows == b, first + row % self.block_rows, pos)
        return pos - lax.broadcasted_iota(jnp.int32, (self.block_rows, self.lanes), 0)

    def firsts(self, chunk, info_ref):
        (place_ref, order_ref) = info_ref
        head, ctx = place_ref[0], place_ref[1]
        a, core, part = chunk
        for j in range(self.slices):
            m, rest = divmod(j, self.kv * self.blocks)
            s, b = divmod(rest, self.blocks)
            stored = (ctx ^ (self.zone(part)[m] * self.cores + core)) * self.blocks + b
            yield order_ref[stored] * self.block_len + (head ^ (a * self.kv + s)) * self.block_rows

    def first_at(self, chunk):
        a, core, part = chunk
        return ((a * self.cores + core) * self.parts + part) * self.slices

    def masked(self, scores, gap, chunk, first_ref):
        for j in range(self.slices):
            row = j * self.block_rows
            first = first_ref[pl.ds(self.first_at(chunk) + j, 1), :]
            yield row, jnp.where(gap >= first, scores[row : row + self.block_rows], LOWEST)

    def turn(self, kv_refs, turned_ref):
        for i, ref in enumerate(kv_refs):
            turned_ref[:, self.keys_at(i)] = ref[...].reshape(self.chunk_keys, 2 * HD).T

    def keys(self, ref):
        return ref[:, :, :, :HD].reshape(self.chunk_keys, HD)

    def values(self, ref):
        return ref[:, :, :, HD:].reshape(self.chunk_keys, HD)

    def fold(self, block):
        return block.reshape(block.shape[0] // 8, 8, self.lanes)

    def scores(self, tile, chunks, kv_refs, q_t, e_ref, cols, gap_ref, first_ref):
        gap = gap_ref[pl.ds(tile * self.block_rows, self.block_rows), :]
        top = jnp.full((8, self.lanes), FLOOR, F32)
        for i, ref in enumerate(kv_refs):
            scores = dot(self.keys(ref), q_t)
            for row, part in self.masked(scores, gap, chunks[i], first_ref):
                e_ref[pl.ds(i * self.chunk_keys + row, part.shape[0]), cols] = part
                top = jnp.maximum(top, jnp.max(self.fold(part), axis=0))
        return jnp.max(top, axis=0, keepdims=True)

    def exponents(self, count, e_ref, cols, top):
        total = jnp.zeros((8, self.lanes), F32)
        for i in range(count):
            part = jnp.exp2(e_ref[self.keys_at(i), cols] * EXPO - top * EXPO)
            e_ref[self.keys_at(i), cols] = part
            total = total + jnp.sum(self.fold(part), axis=0)
        return jnp.sum(total, axis=0, keepdims=True)

    def store_heads(self, out_ref, kind, tile, turned):
        s, start = self.tiles[tile]
        block = turned.T.astype(BF)
        for n in range(self.group):
            piece = block[n * self.tile_rows : (n + 1) * self.tile_rows]
            out_ref[kind, pl.ds(start, self.tile_rows), pl.ds(n * HD, HD)] = piece

    def back(self, dkv_refs, p_ref, ds_ref, q_ref, do_ref):
        shape = (self.z_part, self.kv, self.rows, HD)
        for i, out_ref in enumerate(dkv_refs):
            at = self.keys_at(i)
            out_ref[:, :, :, :HD] = dot(ds_ref[at, :], q_ref[...]).astype(BF).reshape(shape)
            out_ref[:, :, :, HD:] = dot(p_ref[at, :], do_ref[...]).astype(BF).reshape(shape)


def forward_part(plan, chunks, gap_ref, first_ref, q_t, kv_refs, e_ref, top_ref, sum_ref, mix_ref, turned_ref):
    spans = [plan.at(tile) for tile in range(len(plan.tiles))]
    tops = [
        plan.scores(tile, chunks, kv_refs, q_t[:, at], e_ref, at, gap_ref, first_ref)
        for tile, at in enumerate(spans)
    ]
    plan.turn(kv_refs, turned_ref)
    for at, top in zip(spans, tops):
        top_ref[:, at] = top
        sum_ref[:, at] = plan.exponents(len(chunks), e_ref, at, top)
    for at in spans:
        mixed = jnp.zeros((HD, plan.lanes), F32)
        for i in range(len(chunks)):
            weights = e_ref[plan.keys_at(i), at].astype(BF)
            mixed = mixed + dot(turned_ref[pl.ds(HD, HD), plan.keys_at(i)], weights)
        mix_ref[:, at] = mixed


def place_kernel(plan, chunks, place_ref, order_ref, gap_ref, first_ref):
    info_ref = (place_ref, order_ref)
    for tile in range(len(plan.tiles)):
        gap_ref[pl.ds(tile * plan.block_rows, plan.block_rows), :] = plan.gap(tile, info_ref)
    for chunk in chunks:
        for j, first in enumerate(plan.firsts(chunk, info_ref)):
            first_ref[pl.ds(plan.first_at(chunk) + j, 1), :] = jnp.full((1, plan.lanes), first, jnp.int32)


def turn_kernel(plan, *refs):
    q_parts, (q_all, do_all, q_t, do_t) = refs[:-4], refs[-4:]
    for tile, (s, start) in enumerate(plan.tiles):
        span = pl.ds(start, plan.tile_rows)
        for n in range(plan.group):
            at = pl.ds(tile * plan.lanes + n * plan.tile_rows, plan.tile_rows)
            q_all[at, :] = q_parts[s][0, span, pl.ds(n * HD, HD)]
            do_all[at, :] = q_parts[s][1, span, pl.ds(n * HD, HD)]
        at = plan.at(tile)
        q_t[:, at] = q_all[at, :].T
        do_t[:, at] = do_all[at, :].T


def part_kernel(plan, chunks, gap_ref, first_ref, q_t, *refs):
    forward_part(plan, chunks, gap_ref, first_ref, q_t, refs[: len(chunks)], *refs[-5:])


def far_kernel(plan, chunks, others, gap_ref, first_ref, q_all, do_all, q_t, do_t, *refs):
    count = len(chunks)
    partial, refs = [refs[3 * i : 3 * i + 3] for i in range(others)], refs[3 * others :]
    kv_refs, refs = refs[:count], refs[count:]
    scale_refs, refs = refs[:others], refs[others:]
    (delta_ref, mixed_ref, q_grad_ref), refs = refs[:3], refs[3:]
    dkv_refs, (turned_ref, e_ref, w_ref, p_ref, ds_ref) = refs[:-5], refs[-5:]
    spans = [plan.at(tile) for tile in range(len(plan.tiles))]
    tops = [
        plan.scores(tile, chunks, kv_refs, q_t[:, at], e_ref, at, gap_ref, first_ref)
        for tile, at in enumerate(spans)
    ]
    plan.turn(kv_refs, turned_ref)
    for at in spans:
        for i, ref in enumerate(kv_refs):
            w_ref[plan.keys_at(i), at] = dot(plan.values(ref), do_t[:, at])
    inverses = []
    for at, top in zip(spans, tops):
        for top_ref, _, _ in partial:
            top = jnp.maximum(top, top_ref[:, at])
        total = plan.exponents(count, e_ref, at, top)
        factors = [jnp.exp2((top_ref[:, at] - top) * EXPO) for top_ref, _, _ in partial]
        for factor, (_, sum_ref, _) in zip(factors, partial):
            total = total + factor * sum_ref[:, at]
        inverse = 1.0 / total
        for factor, scale_ref in zip(factors, scale_refs):
            scale_ref[:, at] = factor * inverse
        inverses.append(inverse)
    for at, inverse in zip(spans, inverses):
        mixed = jnp.zeros((HD, plan.lanes), F32)
        for scale_ref, (_, _, mix_ref) in zip(scale_refs, partial):
            mixed = mixed + mix_ref[:, at] * scale_ref[:, at]
        for i in range(count):
            probs = (e_ref[plan.keys_at(i), at] * inverse).astype(BF)
            p_ref[plan.keys_at(i), at] = probs
            mixed = mixed + dot(turned_ref[pl.ds(HD, HD), plan.keys_at(i)], probs)
        mixed = mixed.astype(BF)
        mixed_ref[:, at] = mixed
        delta_ref[:, at] = jnp.sum(do_t[:, at].astype(F32) * mixed.astype(F32), axis=0, keepdims=True)
    for at, inverse in zip(spans, inverses):
        q_grad = jnp.zeros((HD, plan.lanes), F32)
        for i in range(count):
            probs = e_ref[plan.keys_at(i), at] * inverse
            grad_s = (probs * (w_ref[plan.keys_at(i), at] - delta_ref[:, at])).astype(BF)
            ds_ref[plan.keys_at(i), at] = grad_s
            q_grad = q_grad + dot(turned_ref[pl.ds(0, HD), plan.keys_at(i)], grad_s)
        q_grad_ref[:, at] = q_grad
    plan.back(dkv_refs, p_ref, ds_ref, q_all, do_all)


def back_kernel(plan, rows_at, last, order, q_all, do_all, do_t, e_ref, scale_ref, delta_ref, q_grad_in, *refs):
    count = len(rows_at)
    mixed_ref, refs = refs[:last], refs[last:]
    kv_refs, refs = refs[:count], refs[count + order :]
    refs, (turned_ref, p_ref, ds_ref) = refs[:-3], refs[-3:]
    outs, dkv_refs = refs[:-count], refs[-count:]
    spans = [plan.at(tile) for tile in range(len(plan.tiles))]
    for at in spans:
        for i, ref in enumerate(kv_refs):
            probs = e_ref[plan.keys_at(rows_at[i]), at] * scale_ref[:, at]
            p_ref[plan.keys_at(i), at] = probs.astype(BF)
            grad_s = (probs * (dot(plan.values(ref), do_t[:, at]) - delta_ref[:, at])).astype(BF)
            ds_ref[plan.keys_at(i), at] = grad_s
    plan.turn(kv_refs, turned_ref)
    plan.back(dkv_refs, p_ref, ds_ref, q_all, do_all)
    for tile, at in enumerate(spans):
        q_grad = q_grad_in[:, at]
        for i in range(count):
            q_grad = q_grad + dot(turned_ref[pl.ds(0, HD), plan.keys_at(i)], ds_ref[plan.keys_at(i), at])
        if last:
            out_ref = outs[plan.tiles[tile][0]]
            plan.store_heads(out_ref, 0, tile, mixed_ref[0][:, at].astype(F32))
            plan.store_heads(out_ref, 1, tile, q_grad * SCALING)
        else:
            outs[0][:, at] = q_grad


def add_kernel(*refs):
    total = refs[0][...].astype(F32)
    for ref in refs[1:-1]:
        total = total + ref[...].astype(F32)
    refs[-1][...] = total.astype(BF)


def sum_heads_kernel(parts, *refs):
    for m_z, out_ref in enumerate(refs[parts:]):
        total = refs[0][m_z].astype(F32)
        for ref in refs[1:parts]:
            total = total + ref[m_z].astype(F32)
        out_ref[...] = total.astype(BF)


def sum_z_kernel(kv, *refs):
    ins, outs = refs[:-kv], refs[-kv:]
    for s, out_ref in enumerate(outs):
        total = ins[0][s].astype(F32)
        for ref in ins[1:]:
            total = total + ref[s].astype(F32)
        out_ref[...] = total.astype(BF)


def sum_far_kernel(*refs):
    total = refs[0][...].astype(F32)
    for ref in refs[1:-1]:
        total = total + ref[...].astype(F32)
    refs[-1][...] = total


def finish_kv_kernel(kv, group_ref, *refs):
    key_ref, value_ref = refs[kv + 1 :]
    for g in range(kv):

        @pl.when(group_ref[0] == g)
        def _():
            for s in range(kv):
                cols = pl.ds((g ^ s) * HD, HD)
                key_ref[:, cols] = (refs[s][:, :HD].astype(F32) * SCALING).astype(BF)
                value_ref[:, cols] = refs[s][:, HD:]


def finish_q_kernel(kv, group_ref, *refs):
    att_ref, grad_ref, done_ref = refs[kv:]
    done_ref[...] = jnp.zeros_like(done_ref)
    width = refs[0].shape[2]
    for g in range(kv):

        @pl.when(group_ref[0] == g)
        def _():
            for s in range(kv):
                cols = pl.ds((g ^ s) * width, width)
                att_ref[:, cols] = refs[s][0]
                grad_ref[:, cols] = refs[s][1]


def shards(queries, key_vectors, value_vectors, out_grad, block_order):
    heads_devices = lax.axis_size("head")
    ctx_devices = lax.axis_size("ctx")
    halves, block_rows, query_width = queries.shape
    kv = key_vectors.shape[2] // HD
    rows = halves * block_rows
    width = query_width // kv
    cores = CORES if ctx_devices % CORES == 0 else 1
    z_devices = ctx_devices // cores
    spans = heads_devices // kv
    parts = 2 if z_devices % 2 == 0 else 1
    plan = Plan(kv, block_rows * heads_devices, block_rows, rows, width // HD, cores, z_devices, parts)
    z_part = plan.z_part
    head = lax.axis_index("head").astype(jnp.int32)
    place = jnp.stack([head, lax.axis_index("ctx").astype(jnp.int32)])
    own_group = (head % kv).reshape(1)
    queries = queries.reshape(rows, query_width)
    out_grad = out_grad.reshape(rows, query_width)
    key_vectors = key_vectors.reshape(rows, kv * HD)
    value_vectors = value_vectors.reshape(rows, kv * HD)

    def bf(*dims):
        return jax.ShapeDtypeStruct(dims, BF)

    def f32(*dims):
        return jax.ShapeDtypeStruct(dims, F32)

    def i32(*dims):
        return jax.ShapeDtypeStruct(dims, jnp.int32)

    def with_swaps(blocks):
        return [blocks[0]] + [swap(blocks[s], "head", s) for s in range(1, kv)]

    dkv = bf(z_part, kv, rows, 2 * HD)

    def pick(block, g, size):
        out = block[:, :size]
        for i in range(1, kv):
            out = jnp.where(g == i, block[:, i * size : (i + 1) * size], out)
        return out

    def of_head(g):
        return jnp.concatenate([pick(key_vectors, g, HD), pick(value_vectors, g, HD)], axis=1)

    def queries_of(g):
        return jnp.stack([pick(queries, g, width), pick(out_grad, g, width)])

    piece = jnp.stack(with_swaps([of_head((head % kv) ^ s) for s in range(kv)]))
    q_parts = with_swaps([queries_of((head % kv) ^ s) for s in range(kv)])
    pieces = [swap(piece, "ctx", m * cores) for m in reversed(range(1, z_devices))]
    pieces = [piece] + pieces[::-1]
    query_rows = plan.query_rows
    chunks = [(a, core, p) for a in range(spans) for core in range(cores) for p in range(parts)]
    gap, firsts = call(
        functools.partial(place_kernel, plan, chunks),
        "place",
        (place, block_order),
        [i32(len(plan.tiles) * block_rows, plan.lanes), i32(len(chunks) * plan.slices, plan.lanes)],
        [SMEM, SMEM],
    )
    q_all, do_all, q_t, do_t = call(
        functools.partial(turn_kernel, plan),
        "turn",
        q_parts,
        [bf(query_rows, HD)] * 2 + [bf(HD, query_rows)] * 2,
    )
    column, handed, order = [None] * parts, [None] * parts, []
    for p in reversed(range(parts)):
        parcels = [pieces[m] for m in plan.zone(p)]
        extra = [column[p + 1], *order] if order else []
        *handed_on, column[p] = call(
            functools.partial(stack_kernel, len(parcels)),
            "stack",
            (*parcels, *extra),
            [dkv] * (1 + bool(extra)),
        )
        handed[p] = column[p]
        if extra:
            handed[p + 1] = handed_on[0]
        order = [*q_parts[1:], firsts] if p else []
    columns = [[swap(half, "head", a * kv) for half in column] for a in range(1, spans)]
    near_kv = [column] + [[swap(half, "ctx", core) for half in handed] for core in range(1, cores)]
    near_flat = [half for pair in near_kv for half in pair]
    each = range(parts)
    near_chunks = [(0, core, p) for core in range(cores) for p in each]
    mid_chunks = [(a, 0, p) for a in range(1, spans) for p in each]
    far_chunks = [(a, core, p) for a in range(1, spans) for core in range(1, cores) for p in each]

    keys = plan.chunk_keys
    query_rows = plan.query_rows
    row, column_out = f32(1, query_rows), f32(HD, query_rows)

    def forward(name, chunks, kv_refs, order):
        size = len(chunks) * keys
        return call(
            functools.partial(part_kernel, plan, chunks),
            name,
            (gap, firsts, q_t, *kv_refs, *order),
            [f32(size, query_rows), row, row, column_out],
            None,
            [pltpu.VMEM((2 * HD, size), BF)],
            size * 4 * HD,
            8 * size * query_rows * HD,
        )

    mids, order = [None] * parts, []
    for p in reversed(each):
        if p + 1 < parts or parts == 1:
            near_e, *near = forward("attend_near", near_chunks, near_flat, order)
            order = [near[0]]
            for pair in columns:
                pair[p] = after([pair[p]], order)[0]
        mids[p] = forward("attend_mid", [c for c in mid_chunks if c[2] == p], [pair[p] for pair in columns], order)
        order = [mids[p][1]]
    far_kv = [swap(pair[p], "ctx", core) for pair in columns for core in range(1, cores) for p in each]
    far_keys = len(far_kv) * keys
    outs = call(
        functools.partial(far_kernel, plan, far_chunks, 1 + parts),
        "attend_far",
        (gap, firsts, q_all, do_all, q_t, do_t, *near, *[r for mid in mids for r in mid[1:]], *far_kv),
        [row] * (2 + parts) + [bf(HD, query_rows), column_out] + [dkv] * len(far_kv),
        None,
        [
            pltpu.VMEM((2 * HD, far_keys), BF),
            pltpu.VMEM((far_keys, query_rows), F32),
            pltpu.VMEM((far_keys, query_rows), F32),
            pltpu.VMEM((far_keys, query_rows), BF),
            pltpu.VMEM((far_keys, query_rows), BF),
        ],
        far_keys * (4 * HD + 12 * query_rows),
        16 * far_keys * query_rows * HD,
    )
    (near_scale, *mid_scales), outs = outs[: 1 + parts], outs[1 + parts :]
    (delta, mixed, q_grad), far_dkv = outs[:3], outs[3:]

    def back(rows_at, last, e, scale, q_grad, kv_refs, order):
        count = len(rows_at)
        q_outs = [bf(2, rows, width)] * kv if last else [column_out]
        outs = call(
            functools.partial(back_kernel, plan, rows_at, last, len(order)),
            "attend_back",
            (q_all, do_all, do_t, e, scale, delta, q_grad, *[mixed] * last, *kv_refs, *order),
            q_outs + [dkv] * count,
            None,
            [
                pltpu.VMEM((2 * HD, count * keys), BF),
                pltpu.VMEM((count * keys, query_rows), BF),
                pltpu.VMEM((count * keys, query_rows), BF),
            ],
            count * keys * (4 * HD + 4 * query_rows),
            12 * count * keys * query_rows * HD,
        )
        return outs[: len(q_outs)], outs[len(q_outs) :]

    sums = [[] for _ in range(parts)]
    totals = []
    for p in reversed(each):
        mid_kv = [pair[p] for pair in columns]
        (q_grad,), mid_dkv = back(
            list(range(len(mid_kv))), False, mids[p][0], mid_scales[p], q_grad, mid_kv, []
        )
        for a in range(spans - 1):
            both = [mid_dkv[a]]
            for core in range(1, cores):
                ours = far_dkv[(a * (cores - 1) + core - 1) * parts + p]
                both.append(swap(ours, "ctx", core))
            totals += call(add_kernel, "sum_cores", after(both, totals[-1:]), [dkv])
            sums[p].append(swap(totals[-1], "head", (a + 1) * kv))
    order = [swap(totals[-1][0, 0, :, :HD], "ctx", 1)] if cores > 1 else []
    for core in reversed(range(cores)):
        outs, parts_dkv = back(
            [core * parts + p for p in each], core == 0, near_e, near_scale, q_grad, near_kv[core], order
        )
        q_grad = outs[0]
        for p in range(parts):
            sums[p].append(swap(parts_dkv[p], "ctx", core) if core else parts_dkv[p])
    q_parts = outs[:kv]
    z_parts = [None] * z_devices
    for p in range(parts):
        totals = call(
            functools.partial(sum_heads_kernel, len(sums[p])),
            "sum_heads",
            sums[p],
            [bf(kv, rows, 2 * HD)] * z_part,
        )

        if p == parts - 1:
            q_parts = with_swaps(after(q_parts, totals[:1]))
        for m, total in zip(plan.zone(p), totals):
            z_parts[m] = swap(total, "ctx", m * cores) if m else total
    ordered = [z_parts[m] for p in each for m in plan.zone(p)]
    if parts > 1:
        far_z = call(sum_far_kernel, "sum_far_z", ordered[:z_part], [f32(kv, rows, 2 * HD)], flops=1 << 32)
        ordered = [*far_z, *ordered[z_part:]]
    pair_parts = call(
        functools.partial(sum_z_kernel, kv), "sum_z", ordered, [bf(rows, 2 * HD)] * kv
    )
    pair_parts = with_swaps(pair_parts)
    attended, query_grad, done = call(
        functools.partial(finish_q_kernel, kv),
        "finish_q",
        (own_group, *q_parts),
        [bf(rows, query_width)] * 2 + [f32(8, HD)],
        [SMEM] + [VMEM] * kv,
    )
    key_grad, value_grad = call(
        functools.partial(finish_kv_kernel, kv),
        "finish_kv",
        (own_group, *pair_parts, done),
        [bf(rows, kv * HD)] * 2,
        [SMEM] + [VMEM] * (kv + 1),
    )
    return (
        attended.reshape(halves, block_rows, query_width),
        query_grad.reshape(halves, block_rows, query_width),
        key_grad.reshape(halves, block_rows, kv * HD),
        value_grad.reshape(halves, block_rows, kv * HD),
    )


def solution(mesh):
    split = P("ctx", "head", None)
    return jax.shard_map(
        shards,
        mesh=mesh,
        in_specs=(split, split, split, split, P()),
        out_specs=(split, split, split, split),
        check_vma=False,
    )
```
